32 devices in a mesh: seq: 8 (over z, x), batch: 4 (over y, core).
Axes of the slice: x: 2, y: 2, z: 4, core: 2. Of those that a mesh axis runs over, the one named last changes fastest.
Arguments:
- inputs: bfloat16 [8, 1024, 1024], P('batch', 'seq'), may hold values from -6 to 6
- memory: bfloat16 [8, 512, 1024], P('batch', 'seq'), may hold values from -6 to 6
- cotangent: bfloat16 [8, 1024, 1024], P('batch', 'seq'), may hold values from -6 to 6
- valid_len: int32 [8], P('batch'), may hold values from 32 to 1024, as said below
- value_routes: int32 [8, 1024, 4, 2], P('batch', 'seq'), may hold values from 0 to 4, all different within a row
- memory_routes: int32 [8, 512, 4, 2], P('batch', 'seq'), may hold values from 0 to 4, all different within a row
- output_routes: int32 [8, 1024, 4, 2], P('batch', 'seq'), may hold values from 0 to 4, all different within a row
- norm1_gain: float32 [1024], replicated, may hold values from 0.5 to 1.5
- norm2_gain: float32 [1024], replicated, may hold values from 0.5 to 1.5
- query_weight: bfloat16 [1024, 448], replicated, may hold values from -0.1875 to 0.1875
- key_weight: bfloat16 [1024, 448], replicated, may hold values from -0.1875 to 0.1875
- value_weight: bfloat16 [1024, 2240], replicated, may hold values from -0.1875 to 0.1875
- router_weight: bfloat16 [1024, 40], replicated, may hold values from -0.12988281 to 0.12988281
- output_weight: bfloat16 [2240, 1024], replicated, may hold values from -15 to 15
- up_weight: bfloat16 [1024, 4096], replicated, may hold values from -0.1875 to 0.1875
- down_weight: bfloat16 [4096, 1024], replicated, may hold values from -0.09375 to 0.09375
Outputs:
- output: bfloat16 [8, 1024, 1024], P('batch', 'seq')
- input_grad: float32 [8, 1024, 1024], P('batch', 'seq')
- norm1_grad: float32 [1024], P(('seq', 'batch'))
- norm2_grad: float32 [1024], P(('seq', 'batch'))
- query_grad: float32 [1024, 448], P(('seq', 'batch'))
- key_grad: float32 [1024, 448], P(('seq', 'batch'))
- value_grad: float32 [1024, 2240], P(('seq', 'batch'))
- router_grad: float32 [1024, 40], P(('seq', 'batch'))
- outproj_grad: float32 [2240, 1024], P(None, ('seq', 'batch'))
- up_grad: float32 [1024, 4096], P(('seq', 'batch'))
- down_grad: float32 [4096, 1024], P(('seq', 'batch'))
The draws below stay inside these ranges and needn't reach their ends.
Inputs may be any that keep to these rules, and one draw needn't show every extreme that they name: `valid_len`: each aligned run of 2 sequences holds one of full length 1024.
All inputs are finite; a program needn't handle non-finite values.
Results may differ from the reference program's by a relative error of at most 0.015.
Values may be sent and summed in bfloat16 or wider, within the bound.
No kernel may reach another device: no remote copies, remote signals or barrier semaphores. Data moves between devices by JAX's collectives and lax.ppermute only.
A program may use at most 256 MiB of HBM per device.

```python
import jax
import jax.numpy as jnp
from jax import lax

D = 1024
H = 4
DH = 112
E = 5
FF = 4096
PICKS = 2
SEQS = 2
SEQUENCES = 8
SEG_LEN = 1024
MEM_LEN = 512


def draw_valid_len(key, part):
    key = jax.random.fold_in(key, 7)
    key_base, key_halving, key_chosen = jax.random.split(key, 3)
    group_count = SEQUENCES // SEQS
    base_len = jax.random.randint(key_base, (SEQUENCES,), SEG_LEN // 2, SEG_LEN + 1)
    halving = jax.random.randint(key_halving, (SEQUENCES,), 0, 5)
    shortened = jnp.maximum(jnp.right_shift(base_len, halving), 1)
    chosen = jax.random.randint(key_chosen, (group_count,), 0, SEQS)
    slot_index = jnp.arange(SEQUENCES, dtype=jnp.int32) % SEQS
    full_rows = slot_index == jnp.repeat(chosen, SEQS)
    return jnp.where(full_rows, SEG_LEN, shortened).astype(jnp.int32)


def raised(values, key, source, target, blocks, factor):
    owner, partner = [(jnp.arange(values.shape[dim]) // (values.shape[dim] // blocks)).reshape([-1 if axis == dim else 1 for axis in range(values.ndim)]) for dim in (source, target)]
    chosen = jax.random.permutation(key, blocks)[partner]
    strong = (owner == chosen) | (owner == (partner + blocks // 2) % blocks)
    return jnp.where(strong, factor * values, values)


def levels(own_key, shape, cuts, least, top_value):
    factor_of = 1.0
    for axis_at, blocks in cuts:
        steps = jax.random.uniform(jax.random.fold_in(jax.random.fold_in(own_key, 6), axis_at), (blocks,), jnp.float32, least / len(cuts), top_value / len(cuts))
        factor_of = factor_of * jnp.repeat(jnp.exp(steps), shape[axis_at] // blocks).reshape((-1,) + (1,) * (len(shape) - 1 - axis_at))
    return factor_of


def picks_of(key, rows, amount, top, lift):
    order = jax.random.permutation(jax.random.fold_in(key, 1), amount)
    pull = order
    for power in range(3):
        pull = pull * pull // amount
    pull = pull * lift // amount
    lots = jax.random.randint(jax.random.fold_in(key, 2), (rows, amount), 0, 4096) + pull
    sure = jax.random.permutation(jax.random.fold_in(key, 3), rows)[jnp.arange(amount) % rows]
    lots = jnp.where(jnp.arange(rows)[:, None] == sure[None, :], 1 << 14, lots)
    priority = lots * amount + jnp.arange(amount)
    return lax.top_k(priority.astype(jnp.int32), top)[1].astype(jnp.int32)


def bell_draw(own_key, shape, deviation, reach, shards=(), held_as=jnp.bfloat16):
    values = deviation * jax.random.normal(own_key, shape, jnp.float32)
    if shards:
        values = values * levels(own_key, shape, shards, -0.22, 0.18)
    return jnp.clip(values, -reach, reach).astype(held_as)


def bell_draw_with(own_key, shape, scale, most, shards, heavy, kind=jnp.bfloat16):
    drawn = scale * jax.random.normal(own_key, shape, jnp.float32)
    if shards:
        drawn = drawn * levels(own_key, shape, shards, -0.22, 0.18)
    return jnp.clip(raised(drawn, jax.random.fold_in(own_key, 3), *heavy), -most, most).astype(kind)


def setup_inputs(seed: int = 0) -> dict:
    keys = jax.random.split(jax.random.key(seed), 17)
    inputs = bell_draw(keys[0], (SEQUENCES, SEG_LEN, D), 1.0, 6.0, ((0, 4), (1, 8)))
    memory = bell_draw(keys[1], (SEQUENCES, MEM_LEN, D), 1.0, 6.0, ((0, 4), (1, 8)))
    cotangent = bell_draw_with(keys[2], (SEQUENCES, SEG_LEN, D), 1.0, 6.0, ((0, 4), (1, 8)), (1, 2, 8, 2.0))
    valid_len = draw_valid_len(jax.random.fold_in(keys[16], 71), 0)
    value_routes = picks_of(keys[4], SEQUENCES * SEG_LEN * H, E, PICKS, 3276).reshape((SEQUENCES, SEG_LEN, H, PICKS))
    memory_routes = picks_of(keys[5], SEQUENCES * MEM_LEN * H, E, PICKS, 3276).reshape((SEQUENCES, MEM_LEN, H, PICKS))
    output_routes = picks_of(keys[6], SEQUENCES * SEG_LEN * H, E, PICKS, 3276).reshape((SEQUENCES, SEG_LEN, H, PICKS))
    norm1_gain = jnp.clip(1.0 + 0.1 * jax.random.normal(keys[7], (D,), jnp.float32), 0.5, 1.5)
    norm2_gain = jnp.clip(1.0 + 0.1 * jax.random.normal(keys[8], (D,), jnp.float32), 0.5, 1.5)
    query_weight = bell_draw(keys[9], (D, H * DH), D ** -0.5, 0.1875)
    key_weight = bell_draw(keys[10], (D, H * DH), D ** -0.5, 0.1875)
    value_weight = bell_draw(keys[11], (D, H * E * DH), D ** -0.5, 0.1875)
    router_weight = bell_draw(keys[12], (D, 2 * H * E), 0.022, 0.12988281)
    output_weight = bell_draw(keys[13], (H * E * DH, D), 2.5, 15.0)
    up_weight = bell_draw(keys[14], (D, FF), D ** -0.5, 0.1875)
    down_weight = bell_draw(keys[15], (FF, D), FF ** -0.5, 0.09375)
    return dict(inputs=inputs, memory=memory, cotangent=cotangent, valid_len=valid_len, value_routes=value_routes, memory_routes=memory_routes, output_routes=output_routes, norm1_gain=norm1_gain, norm2_gain=norm2_gain, query_weight=query_weight, key_weight=key_weight, value_weight=value_weight, router_weight=router_weight, output_weight=output_weight, up_weight=up_weight, down_weight=down_weight)


@jax.custom_vjp
def low(v):
    return lax.optimization_barrier(v.astype(jnp.bfloat16)).astype(jnp.float32)

@jax.custom_vjp
def low_back(v):
    return v

def low_keep(v):
    return (low(v), None)

def low_pass(kept, grad):
    return (grad,)

def back_keep(v):
    return (v, None)

def back_low(kept, grad):
    return (low(grad),)
low.defvjp(low_keep, low_pass)
low_back.defvjp(back_keep, back_low)
epsilon = 1e-05
neg_large = -1e+30
slope_base = 0.5

def matmul(left_arr, right_arr):
    return jnp.dot(left_arr, right_arr, precision=lax.Precision.HIGHEST, preferred_element_type=jnp.float32)

def layer_norm(values, gain_row):
    centred = values - lax.optimization_barrier(jnp.mean(values, axis=-1, keepdims=True))
    spread = lax.optimization_barrier(jnp.mean(centred * centred, axis=-1, keepdims=True))
    return centred * lax.rsqrt(spread + epsilon) * gain_row

def selection(routes):
    choices_hit = routes[..., None] == jnp.arange(E, dtype=jnp.int32)
    return lax.optimization_barrier(jnp.sum(choices_hit.astype(jnp.float32), axis=-2))

def layer(params, tokens, memory_rows, value_pick, memory_pick, output_pick, length):
    gain_one, gain_two, w_query, w_key, w_value, w_router, w_output, w_up, w_down = params
    gate_count = H * E
    normed = low(layer_norm(tokens, gain_one))
    mem_normed = low(layer_norm(memory_rows, gain_one))
    context = jnp.concatenate([mem_normed, normed], axis=0)
    logits = low_back(matmul(context, w_router))
    value_gate = jax.nn.sigmoid(logits[:, :gate_count]).reshape(-1, H, E) * jnp.concatenate([memory_pick, value_pick], axis=0)
    out_gate = jax.nn.sigmoid(logits[MEM_LEN:, gate_count:]).reshape(-1, H, E) * output_pick
    queries = low_back(low(matmul(normed, w_query))).reshape(SEG_LEN, H, DH)
    key_rows = low_back(low(matmul(context, w_key))).reshape(-1, H, DH)
    expanded = low_back(matmul(context, w_value)).reshape(-1, H, E, DH)
    values = low_back(low(lax.optimization_barrier(jnp.sum(value_gate[..., None] * expanded, axis=2))))
    key_place = jnp.concatenate([jnp.arange(MEM_LEN, dtype=jnp.int32) - MEM_LEN, jnp.arange(SEG_LEN, dtype=jnp.int32)])
    slopes = slope_base * (jnp.arange(H, dtype=jnp.float32) + 1.0) / (MEM_LEN + SEG_LEN)
    block_size = min(512, SEG_LEN)

    def attend_block(block_item):
        query_block, query_place = block_item
        raw_scores = jnp.einsum('qhd,khd->hqk', query_block, key_rows, precision=lax.Precision.HIGHEST)
        distance = (query_place[:, None] - key_place[None, :]).astype(jnp.float32)
        scores = low_back(raw_scores * DH ** (-0.5) - slopes[:, None, None] * distance[None])
        allowed = (key_place[None, :] < 0) | (key_place[None, :] <= query_place[:, None]) & (key_place[None, :] < length)
        scores = jnp.where(allowed[None], scores, neg_large)
        shifted = scores - lax.optimization_barrier(jnp.max(scores, axis=-1, keepdims=True))
        weights = jnp.where(allowed[None], jnp.exp(shifted), 0.0)
        probability = weights / lax.optimization_barrier(jnp.sum(weights, axis=-1, keepdims=True))
        return low_back(jnp.einsum('hqk,khd->qhd', low(probability), values, precision=lax.Precision.HIGHEST))
    places = jnp.arange(SEG_LEN, dtype=jnp.int32)
    attended = lax.map(jax.checkpoint(attend_block), (queries.reshape(-1, block_size, H, DH), places.reshape(-1, block_size)))
    attended = attended.reshape(SEG_LEN, H, DH)
    mixed_rows = low(out_gate[..., None] * attended[:, :, None, :]).reshape(SEG_LEN, H * E * DH)
    residual = tokens + low_back(matmul(mixed_rows, w_output))
    normed_two = low(layer_norm(residual, gain_two))
    up_value = low_back(matmul(normed_two, w_up))
    active = low(jax.nn.gelu(up_value))
    live_rows = (places < length).astype(jnp.float32)[:, None]
    return (residual + low_back(matmul(active, w_down))) * live_rows

def reference(inputs, memory, cotangent, valid_len, value_routes, memory_routes, output_routes, norm1_gain, norm2_gain, query_weight, key_weight, value_weight, router_weight, output_weight, up_weight, down_weight):
    params = (norm1_gain.astype(jnp.float32), norm2_gain.astype(jnp.float32), query_weight.astype(jnp.float32), key_weight.astype(jnp.float32), value_weight.astype(jnp.float32), router_weight.astype(jnp.float32), output_weight.astype(jnp.float32), up_weight.astype(jnp.float32), down_weight.astype(jnp.float32))

    def one_sequence(grad_sums, seq_item):
        tokens, memory_rows, grad_rows, length, routes_value, routes_memory, routes_output = seq_item
        value_pick = selection(routes_value)
        memory_pick = selection(routes_memory)
        output_pick = selection(routes_output)

        def forward(weight_set, token_rows):
            return layer(weight_set, token_rows, memory_rows, value_pick, memory_pick, output_pick, length)
        result, backward = jax.vjp(forward, params, tokens)
        weight_grads, token_grads = backward(grad_rows)
        grad_sums = jax.tree.map(jnp.add, grad_sums, weight_grads)
        return (grad_sums, (result.astype(jnp.bfloat16), token_grads))
    start_sums = jax.tree.map(jnp.zeros_like, params)
    grad_sums, (outputs, input_grads) = lax.scan(one_sequence, start_sums, (inputs.astype(jnp.float32), memory.astype(jnp.float32), cotangent.astype(jnp.float32), valid_len, value_routes, memory_routes, output_routes))
    return (outputs, input_grads, grad_sums[0], grad_sums[1], grad_sums[2], grad_sums[3], grad_sums[4], grad_sums[5], grad_sums[6], grad_sums[7], grad_sums[8])
```

```python
import functools

import jax
import jax.numpy as jnp
import numpy as np
from jax import lax
from jax.experimental import pallas as pl
from jax.experimental.pallas import tpu as pltpu
from jax.sharding import PartitionSpec as P

epsilon = 1e-05
neg_large = -1e30
slope_base = 0.5
log2_e = 1.4426950408889634
lanes = 128
low = jnp.bfloat16
full = jnp.float32
vmem_bytes = 56 << 20


def dot_nn(left, right):
    return lax.dot_general(left, right, (((1,), (0,)), ((), ())), preferred_element_type=full)


def dot_nt(left, right):
    return lax.dot_general(left, right, (((1,), (1,)), ((), ())), preferred_element_type=full)


def dot_tn(left, right):
    return lax.dot_general(left, right, (((0,), (0,)), ((), ())), preferred_element_type=full)


def norm_parts(values):
    centred = values - jnp.mean(values, axis=-1, keepdims=True)
    spread = jnp.mean(centred * centred, axis=-1, keepdims=True)
    inverse = lax.rsqrt(spread + epsilon)
    return centred * inverse, inverse


def norm_back(grad, hat, inverse, gain_row):
    scaled = grad * gain_row
    along = jnp.mean(scaled * hat, axis=-1, keepdims=True)
    return inverse * (scaled - jnp.mean(scaled, axis=-1, keepdims=True) - hat * along)


def call(kernel, outs, operands, scratch=(), scalars=(), cost=(0, 0)):
    count = len(operands)
    specs = [
        pl.BlockSpec(memory_space=pltpu.SMEM if i in scalars else pltpu.VMEM) for i in range(count)
    ]
    return pl.pallas_call(
        kernel,
        out_shape=[jax.ShapeDtypeStruct(shape, kind) for shape, kind in outs],
        in_specs=specs,
        out_specs=[pl.BlockSpec(memory_space=pltpu.VMEM)] * len(outs),
        scratch_shapes=list(scratch),
        compiler_params=pltpu.CompilerParams(vmem_limit_bytes=vmem_bytes),
        cost_estimate=pl.CostEstimate(flops=cost[0], bytes_accessed=cost[1], transcendentals=0),
    )(*operands)


def picks(routes, head_count, expert_count):
    gate_count = head_count * expert_count
    slot_count = routes.shape[1] // head_count
    gate_row = lax.broadcasted_iota(jnp.int32, (routes.shape[1], gate_count), 1)
    slot_row = lax.broadcasted_iota(jnp.int32, (routes.shape[1], gate_count), 0)
    expert_of = (lax.broadcasted_iota(jnp.int32, (1, gate_count), 1) % expert_count).astype(full)
    wanted = routes.astype(full).astype(low)
    total = jnp.zeros((routes.shape[0], gate_count), full)
    for slot in range(slot_count):
        spread = (slot_row == (gate_row // expert_count) * slot_count + slot).astype(full)
        chosen = dot_nn(wanted, spread.astype(low))
        total = total + (chosen == expert_of).astype(full)
    return total


def project(
    x_ref, m_ref, vr_ref, or_ref, gain_ref, wq_ref, wk_ref, wv_ref, wr_ref,
    pay_ref, ctx_ref, vgate_ref, ogate_ref, dims=None
):
    seqs, seg, mem, heads, size, experts, parts = dims
    rows = seg + mem
    gates = heads * experts
    context = []
    for s in range(seqs):
        block = jnp.concatenate([m_ref[s], x_ref[s]], axis=0).astype(full)
        hat, _ = norm_parts(block)
        block_low = (hat * gain_ref[...]).astype(low)
        ctx_ref[s] = block_low
        context.append(block_low)
    ctx = jnp.concatenate(context, axis=0)
    segment = jnp.concatenate([c[mem:] for c in context], axis=0)
    logits = dot_nn(ctx, wr_ref[...])
    sig = jax.nn.sigmoid(logits)
    vgate = sig[:, :gates] * picks(vr_ref[...], heads, experts)
    out_sig = jnp.concatenate([sig[s * rows + mem : (s + 1) * rows, gates : 2 * gates] for s in range(seqs)], axis=0)
    ogate = out_sig * picks(or_ref[...], heads, experts)
    vgate_ref[...] = vgate
    ogate_ref[...] = ogate
    high = vgate.astype(low)
    rest = (vgate - high.astype(full)).astype(low)
    queries = dot_nn(segment, wq_ref[...]).astype(low)
    keys = dot_nn(ctx, wk_ref[...]).astype(low)
    expanded = dot_nn(ctx, wv_ref[...])
    share = seg // parts
    half = share // 2
    spare = lanes - size
    for h in range(heads):
        value = jnp.zeros((seqs * rows, size), full)
        for e in range(experts):
            j = h * experts + e
            value = value + vgate[:, j : j + 1] * expanded[:, j * size : (j + 1) * size]
        joined = jnp.concatenate(
            [
                keys[:, h * size : (h + 1) * size],
                jnp.zeros((seqs * rows, spare), low),
                value.astype(low),
                high[:, h * experts : (h + 1) * experts],
                rest[:, h * experts : (h + 1) * experts],
                jnp.zeros((seqs * rows, spare - 2 * experts), low),
            ],
            axis=1,
        )
        query = jnp.concatenate(
            [queries[:, h * size : (h + 1) * size], jnp.zeros((seqs * seg, spare), low)], axis=1
        )
        for s in range(seqs):
            for p in range(parts):
                dest = (p * heads + h) * seqs + s
                first = s * seg + p * share
                pay_ref[dest, 0:rows, :] = joined[s * rows : (s + 1) * rows]
                pay_ref[dest, rows : rows + half, 0:lanes] = query[first : first + half]
                pay_ref[dest, rows : rows + half, lanes:] = query[first + half : first + share]


def key_value(pay_ref, k_ref, v_ref, seg, mem):
    cycle = pay_ref.shape[0]
    for j in range(cycle):
        k_ref[j * mem : (j + 1) * mem] = pay_ref[j, 0:mem, 0:lanes]
        v_ref[j * mem : (j + 1) * mem] = pay_ref[j, 0:mem, lanes:]
        base = cycle * mem + j * seg
        k_ref[base : base + seg] = pay_ref[j, mem : mem + seg, 0:lanes]
        v_ref[base : base + seg] = pay_ref[j, mem : mem + seg, lanes:]


def query_block(pay_ref, first, group, seg, mem, share):
    rows = seg + mem
    half = share // 2
    found = []
    for j in range(first, first + group):
        found.append(pay_ref[j, rows : rows + half, 0:lanes])
        found.append(pay_ref[j, rows : rows + half, lanes:])
    return jnp.concatenate(found, axis=0)


def attend(scal_ref, pay_ref, att_ref, keep_ref, lse_ref, k_ref, v_ref, dims=None):
    seqs, seg, mem, heads, size, parts, group = dims
    cycle = pay_ref.shape[0]
    share = seg // parts
    mem_len = cycle * mem
    ctx_len = cycle * (mem + seg)
    length = scal_ref[0]
    head = scal_ref[1]
    part = scal_ref[2]
    key_value(pay_ref, k_ref, v_ref, seg, mem)
    slope = slope_base * (head + 1).astype(full) / ctx_len * log2_e
    place = lax.broadcasted_iota(jnp.int32, (1, ctx_len), 1) - mem_len
    bias = jnp.where(place < length, place.astype(full) * slope, neg_large)
    q_rows = group * share
    for first in range(0, cycle, group):
        width = mem_len + (first + group) * seg
        query = query_block(pay_ref, first, group, seg, mem, share)
        scores = dot_nt(query, k_ref[0:width]) * (size**-0.5 * log2_e) + bias[:, :width]
        row = lax.broadcasted_iota(jnp.int32, (q_rows, group * seg), 0)
        col = lax.broadcasted_iota(jnp.int32, (q_rows, group * seg), 1)
        row_place = (row // share) * seg + part * share + row % share
        tail = jnp.where(col <= row_place, scores[:, width - group * seg :], neg_large)
        scores = jnp.concatenate([scores[:, : width - group * seg], tail], axis=1)
        top = jnp.max(scores, axis=1, keepdims=True)
        weights = jnp.exp2(scores - top)
        total = jnp.sum(weights, axis=1, keepdims=True)
        attended = dot_nn(weights.astype(low), v_ref[0:width]) / total
        keep_ref[first * share : first * share + q_rows] = attended
        lse_ref[first * share : first * share + q_rows] = top + jnp.log2(total)
        for j in range(group):
            att_ref[first + j] = attended[j * share : (j + 1) * share].astype(low)


def attend_back(
    scal_ref, pay_ref, keep_ref, lse_ref, grad_ref, wv_ref, ctx_ref, out_ref, d_ref,
    k_ref, v_ref, dk_ref, dv_ref, dims=None
):
    seqs, seg, mem, heads, size, experts, parts, group = dims
    cycle = pay_ref.shape[0]
    rows = seg + mem
    share = seg // parts
    half = share // 2
    mem_len = cycle * mem
    ctx_len = cycle * rows
    length = scal_ref[0]
    head = scal_ref[1]
    part = scal_ref[2]
    key_value(pay_ref, k_ref, v_ref, seg, mem)
    scale = size**-0.5
    slope = slope_base * (head + 1).astype(full) / ctx_len * log2_e
    place = lax.broadcasted_iota(jnp.int32, (ctx_len, lanes), 0) - mem_len
    bias = jnp.where(place < length, place.astype(full) * slope, neg_large)[:, 0:1]
    dk_ref[...] = jnp.zeros_like(dk_ref)
    dv_ref[...] = jnp.zeros_like(dv_ref)
    q_rows = group * share
    lane_at = lax.broadcasted_iota(jnp.int32, (q_rows, lanes), 1)
    query_grads = []
    for first in range(0, cycle, group):
        width = mem_len + (first + group) * seg
        begin = first * share
        query = query_block(pay_ref, first, group, seg, mem, share)
        raw = jnp.concatenate([grad_ref[j] for j in range(first, first + group)], axis=0)
        grad = jnp.where(lane_at < size, raw, jnp.zeros_like(raw))
        kept = keep_ref[begin : begin + q_rows]
        delta = jnp.sum(jnp.where(lane_at < size, grad.astype(full) * kept, 0.0), axis=1, keepdims=True)
        both = jnp.concatenate([jnp.broadcast_to(delta, (q_rows, lanes)), jnp.broadcast_to(lse_ref[begin : begin + q_rows], (q_rows, lanes))], axis=1)
        both = both.T
        delta_row = both[0:1]
        lse_row = both[lanes : lanes + 1]
        scores = dot_nt(k_ref[0:width], query) * (scale * log2_e) + bias[:width]
        weights = jnp.exp2(scores - lse_row)
        row = lax.broadcasted_iota(jnp.int32, (group * seg, q_rows), 0)
        col = lax.broadcasted_iota(jnp.int32, (group * seg, q_rows), 1)
        col_place = (col // share) * seg + part * share + col % share
        cut = width - group * seg
        weights = jnp.concatenate([weights[:cut], jnp.where(row <= col_place, weights[cut:], 0.0)], axis=0)
        grad_weights = dot_nt(v_ref[0:width], grad)
        grad_scores = (weights * (grad_weights - delta_row)).astype(low)
        dk_ref[0:width] += dot_nn(grad_scores, query)
        dv_ref[0:width] += dot_nn(weights.astype(low), grad)
        query_grads.append((dot_tn(grad_scores, k_ref[0:width]) * scale).astype(low))
    spare = lanes - size
    zero_spare = jnp.zeros((rows, spare), low)
    wv = wv_ref[...]
    for j in range(cycle):
        base = cycle * mem + j * seg
        dk = jnp.concatenate([dk_ref[j * mem : (j + 1) * mem], dk_ref[base : base + seg]], axis=0)
        dk = (dk * scale).astype(low)
        dv = jnp.concatenate([dv_ref[j * mem : (j + 1) * mem], dv_ref[base : base + seg]], axis=0)
        dv = dv.astype(low)
        dq = query_grads[j // group][(j % group) * share : (j % group + 1) * share]
        gate_low = pay_ref[j, 0:rows, lanes:].astype(full)
        gate = gate_low[:, size : size + experts] + gate_low[:, size + experts : size + 2 * experts]
        expanded = dot_nn(ctx_ref[j], wv)
        dv_full = dv.astype(full)[:, :size]
        pieces = []
        logit = []
        for e in range(experts):
            one = gate[:, e : e + 1]
            pieces.append((one * dv_full).astype(low))
            along = jnp.sum(dv_full * expanded[:, e * size : (e + 1) * size], axis=1, keepdims=True)
            logit.append(along * one * (1.0 - one))
        logit = jnp.concatenate(logit, axis=1).astype(low)
        out_ref[j, 0:rows, 0:lanes] = dk
        out_ref[j, 0:rows, lanes:] = jnp.concatenate([dv[:, :size], logit, jnp.zeros((rows, spare - experts), low)], axis=1)
        out_ref[j, rows : rows + half, 0:lanes] = dq[:half]
        out_ref[j, rows : rows + half, lanes:] = dq[half:]
        out_logit = grad_ref[j][:, size : size + experts]
        before = mem + 0 * share
        dq_all = []
        out_all = []
        for p in range(parts):
            mine = (part == p).astype(full)
            dq_all.append((dq.astype(full) * mine).astype(low))
            out_all.append((out_logit.astype(full) * mine).astype(low))
        dq_rows = jnp.concatenate([jnp.zeros((before, lanes), low)] + dq_all, axis=0)
        out_rows = jnp.concatenate([jnp.zeros((before, experts), low)] + out_all, axis=0)
        joined = jnp.concatenate([dq_rows[:, :size], dk[:, :size]] + pieces + [logit, out_rows], axis=1)
        width_all = joined.shape[1]
        d_ref[j, :, 0:width_all] = joined
        if d_ref.shape[2] > width_all:
            d_ref[j, :, width_all:] = jnp.zeros((rows, d_ref.shape[2] - width_all), low)
    del zero_spare


def mix(att_ref, ogate_ref, x_ref, gain_ref, wo_ref, mixed_ref, resid_ref, normed_ref, dims=None):
    seqs, seg, heads, size, experts, parts = dims
    share = seg // parts
    ogate = ogate_ref[...]
    tokens = []
    for h in range(heads):
        found = []
        for s in range(seqs):
            for p in range(parts):
                found.append(att_ref[(p * heads + h) * seqs + s])
        att = jnp.concatenate(found, axis=0).astype(full)[:, :size]
        for e in range(experts):
            j = h * experts + e
            mixed_ref[:, j * size : (j + 1) * size] = (ogate[:, j : j + 1] * att).astype(low)
    for s in range(seqs):
        tokens.append(x_ref[s].astype(full))
    residual = jnp.concatenate(tokens, axis=0) + dot_nn(mixed_ref[...], wo_ref[...])
    resid_ref[...] = residual
    hat, _ = norm_parts(residual)
    normed_ref[...] = (hat * gain_ref[...]).astype(low)


def unmix(branch_ref, att_ref, ogate_ref, wo_ref, out_ref, dims=None):
    seqs, seg, heads, size, experts, parts = dims
    share = seg // parts
    ogate = ogate_ref[...]
    grad_mixed = dot_nt(branch_ref[...], wo_ref[...])
    spare = lanes - size
    for h in range(heads):
        found = []
        for s in range(seqs):
            for p in range(parts):
                found.append(att_ref[(p * heads + h) * seqs + s])
        att = jnp.concatenate(found, axis=0).astype(full)[:, :size]
        grad = jnp.zeros((seqs * seg, size), full)
        logit = []
        for e in range(experts):
            j = h * experts + e
            piece = grad_mixed[:, j * size : (j + 1) * size]
            one = ogate[:, j : j + 1]
            grad = grad + one * piece
            logit.append(jnp.sum(piece * att, axis=1, keepdims=True) * one * (1.0 - one))
        joined = jnp.concatenate(
            [grad.astype(low), jnp.concatenate(logit, axis=1).astype(low), jnp.zeros((seqs * seg, spare - experts), low)],
            axis=1,
        )
        for s in range(seqs):
            for p in range(parts):
                first = s * seg + p * share
                out_ref[(p * heads + h) * seqs + s] = joined[first : first + share]


def finish(
    back_ref, grad_out_ref, vgate_ref, x_ref, gain_ref, resid_ref, wq_ref, wk_ref, wv_ref, wr_ref,
    out_ref, dexp_ref, dims=None
):
    seqs, seg, mem, heads, size, experts, parts = dims
    rows = seg + mem
    share = seg // parts
    half = share // 2
    vgate = vgate_ref[...]
    queries, keys, logits, out_logits = [], [], [], []
    for h in range(heads):
        q_found, kv_found, lo_found = [], [], []
        for s in range(seqs):
            kv = back_ref[h * seqs + s, mem:rows, :]
            if parts > 1:
                kv = kv.astype(full)
                for p in range(1, parts):
                    kv = kv + back_ref[(p * heads + h) * seqs + s, mem:rows, :].astype(full)
                kv = kv.astype(low)
            kv_found.append(kv)
            for p in range(parts):
                at = (p * heads + h) * seqs + s
                q_found.append(back_ref[at, rows : rows + half, 0:lanes])
                q_found.append(back_ref[at, rows : rows + half, lanes:])
                lo_found.append(grad_out_ref[at][:, size : size + experts])
        queries.append(jnp.concatenate(q_found, axis=0)[:, :size])
        kv = jnp.concatenate(kv_found, axis=0)
        keys.append(kv[:, :size])
        value = kv[:, lanes : lanes + size].astype(full)
        logits.append(kv[:, lanes + size : lanes + size + experts])
        out_logits.append(jnp.concatenate(lo_found, axis=0))
        for e in range(experts):
            j = h * experts + e
            gate = jnp.concatenate([vgate[s * rows + mem : (s + 1) * rows, j : j + 1] for s in range(seqs)], axis=0)
            dexp_ref[:, j * size : (j + 1) * size] = (gate * value).astype(low)
    grad = dot_nt(dexp_ref[...], wv_ref[...])
    grad = grad + dot_nt(jnp.concatenate(queries, axis=1), wq_ref[...])
    grad = grad + dot_nt(jnp.concatenate(keys, axis=1), wk_ref[...])
    grad = grad + dot_nt(jnp.concatenate(logits + out_logits, axis=1), wr_ref[...])
    for s in range(seqs):
        hat, inverse = norm_parts(x_ref[s].astype(full))
        out_ref[s] = resid_ref[s * seg : (s + 1) * seg] + norm_back(
            grad[s * seg : (s + 1) * seg], hat, inverse, gain_ref[...]
        )


class Halver:
    def __init__(self):
        self.cycle = lax.axis_size("seq")
        self.width = lax.axis_size("batch")
        self.low_bits = self.width.bit_length() - 1
        self.high_bits = self.cycle.bit_length() - 1
        self.me = lax.axis_index("seq") * self.width + lax.axis_index("batch")

    def swap(self, value, bit):
        if bit < self.low_bits:
            axis, size, mask = "batch", self.width, 1 << bit
        else:
            axis, size, mask = "seq", self.cycle, 1 << (bit - self.low_bits)
        return lax.ppermute(value, axis, [(i, i ^ mask) for i in range(size)])

    def order(self, bits):
        count = len(bits)
        found = np.zeros(1 << count, np.int32)
        for place in range(1 << count):
            for at, bit in enumerate(bits):
                if place >> (count - 1 - at) & 1:
                    found[place] |= 1 << bit
        return found

    def scatter(self, first_half, second_half, bits, axis=0):
        return None


def halve(value, axis):
    size = value.shape[axis] // 2
    return (
        lax.slice_in_dim(value, 0, size, axis=axis),
        lax.slice_in_dim(value, size, 2 * size, axis=axis),
    )


def reduce_by(halver, product, bits, axis):
    got = halver.swap(product(2, 4).astype(low), bits[0])
    got_keep, got_send = halve(got, axis)
    keep_send = (product(1, 2) + got_send.astype(full)).astype(low)
    got = halver.swap(keep_send, bits[1])
    keep = product(0, 1) + got_keep.astype(full) + got.astype(full)
    for bit in bits[2:]:
        keep, send = halve(keep, axis)
        got = halver.swap(send.astype(low), bit)
        keep = keep + got.astype(full)
    return keep


def local(
    inputs, memory, cotangent, valid_len, value_routes, memory_routes, output_routes, norm1_gain, norm2_gain,
    query_weight, key_weight, value_weight, router_weight, output_weight, up_weight, down_weight
):
    seqs, seg, width = inputs.shape
    mem = memory.shape[1]
    rows = seg + mem
    heads = value_routes.shape[2]
    qk_width = query_weight.shape[1]
    size = qk_width // heads
    experts = value_weight.shape[1] // qk_width
    halver = Halver()
    cycle = halver.cycle
    parts = cycle // (seqs * heads)
    share = seg // parts
    group = 2
    at = lax.axis_index("seq")
    my_seq = at % seqs
    my_head = at // seqs % heads
    my_part = at // (seqs * heads)
    scal = jnp.stack([lax.dynamic_index_in_dim(valid_len, my_seq, 0, keepdims=False), my_head, my_part]).astype(jnp.int32)
    gain_one = norm1_gain.reshape(1, width)
    gain_two = norm2_gain.reshape(1, width)
    place = at * seg + jnp.arange(seg, dtype=jnp.int32)
    live = (place[None, :] < valid_len[:, None]).astype(full).reshape(seqs * seg, 1)
    grad_output = cotangent.reshape(seqs * seg, width).astype(full) * live
    grad_ffn = grad_output.astype(low)

    v_routes = jnp.concatenate([memory_routes, value_routes], axis=1).reshape(seqs * rows, -1)
    o_routes = output_routes.reshape(seqs * seg, -1)
    pay, ctx, vgate, ogate = call(
        functools.partial(project, dims=(seqs, seg, mem, heads, size, experts, parts)),
        [
            ((cycle, rows + share // 2, 2 * lanes), low),
            ((seqs, rows, width), low),
            ((seqs * rows, heads * experts), full),
            ((seqs * seg, heads * experts), full),
        ],
        [inputs, memory, v_routes, o_routes, gain_one, query_weight, key_weight, value_weight, router_weight],
    )
    pay = lax.all_to_all(pay, "seq", 0, 0)
    other = lax.dynamic_index_in_dim(ctx, 1 - my_seq, 0, keepdims=False)
    mine = lax.dynamic_index_in_dim(ctx, my_seq, 0, keepdims=False)
    got = lax.ppermute(other, "seq", [(i, i ^ 1) for i in range(cycle)])
    even = jnp.where(my_seq == 0, mine, got)
    odd = jnp.where(my_seq == 0, got, mine)
    groups = [[i for i in range(cycle) if i % seqs == s] for s in range(seqs)]
    ctx_all = lax.all_gather(
        jnp.stack([even, odd]), "seq", axis=0, tiled=True, axis_index_groups=groups
    )
    grad_active = dot_nt(grad_ffn, down_weight)
    att, kept, lse = call(
        functools.partial(attend, dims=(seqs, seg, mem, heads, size, parts, group)),
        [
            ((cycle, share, lanes), low),
            ((cycle * share, lanes), full),
            ((cycle * share, 1), full),
        ],
        [scal, pay],
        scratch=[pltpu.VMEM((cycle * rows, lanes), low)] * 2,
        scalars=(0,),
    )
    att = lax.all_to_all(att, "seq", 0, 0)
    mixed, residual, normed_two = call(
        functools.partial(mix, dims=(seqs, seg, heads, size, experts, parts)),
        [
            ((seqs * seg, output_weight.shape[0]), low),
            ((seqs * seg, width), full),
            ((seqs * seg, width), low),
        ],
        [att, ogate, inputs, gain_two, output_weight],
    )
    up_value = dot_nn(normed_two, up_weight)
    gelu_value, gelu_back = jax.vjp(jax.nn.gelu, up_value)
    active = gelu_value.astype(low)
    grad_up = gelu_back(grad_active)[0].astype(low)

    blocks = halver.cycle * halver.width
    bit_count = halver.low_bits + halver.high_bits
    low_b = list(range(halver.low_bits))
    high_b = list(range(halver.low_bits, bit_count))
    core, chip_y, chip_x, chip_z = low_b[:1], low_b[1:], high_b[:1], high_b[1:]

    def rows_by(array, order):
        cols = array.T.reshape(blocks, -1, array.shape[0])
        return jnp.take(cols, order ^ halver.me, axis=0).reshape(-1, array.shape[0])

    def row_product(left, right):
        quarter = left.shape[0] // 4
        return lambda lo, hi: dot_nn(left[lo * quarter : hi * quarter], right)

    down_bits = core + chip_x + chip_y + chip_z
    order = halver.order(down_bits)
    act_blocks = active.reshape(seqs * seg, blocks, -1)
    act_blocks = jnp.take(act_blocks, order ^ halver.me, axis=1).reshape(seqs * seg, -1)
    grad_ffn_t = grad_ffn.T

    def down_product(lo, hi):
        quarter = act_blocks.shape[1] // 4
        return dot_nn(grad_ffn_t, act_blocks[:, lo * quarter : hi * quarter])

    down_grad = reduce_by(halver, down_product, down_bits, 1).T
    up_bits = core + chip_y + chip_x + chip_z
    up_left = rows_by(normed_two, halver.order(up_bits))
    up_grad = reduce_by(halver, row_product(up_left, grad_up), up_bits, 0)

    ffn_out = dot_nn(active, down_weight)
    output = ((residual + ffn_out) * live).astype(low).reshape(seqs, seg, width)
    grad_normed_two = dot_nt(grad_up, up_weight)
    hat_two, inverse_two = norm_parts(residual)
    grad_residual = grad_output + norm_back(grad_normed_two, hat_two, inverse_two, gain_two)
    grad_branch = grad_residual.astype(low)
    (grad_att,) = call(
        functools.partial(unmix, dims=(seqs, seg, heads, size, experts, parts)),
        [((cycle, share, lanes), low)],
        [grad_branch, att, ogate, output_weight],
    )
    grad_out = grad_att
    grad_att = lax.all_to_all(grad_att, "seq", 0, 0)
    out_bits = core + chip_z + chip_x + chip_y
    out_left = rows_by(grad_branch, halver.order(out_bits))
    outproj_grad = reduce_by(halver, row_product(out_left, mixed), out_bits, 0).T

    head_width = 2 * size + experts * size + 2 * experts
    padded = -(-head_width // lanes) * lanes
    my_values = lax.dynamic_slice_in_dim(value_weight, my_head * (experts * size), experts * size, axis=1)
    back, deltas = call(
        functools.partial(attend_back, dims=(seqs, seg, mem, heads, size, experts, parts, group)),
        [((cycle, rows + share // 2, 2 * lanes), low), ((cycle, rows, padded), low)],
        [scal, pay, kept, lse, grad_att, my_values, ctx_all],
        scratch=[pltpu.VMEM((cycle * rows, lanes), low)] * 2 + [pltpu.VMEM((cycle * rows, lanes), full)] * 2,
        scalars=(0,),
    )
    back = lax.all_to_all(back, "seq", 0, 0)
    seq_bits = high_b[: seqs.bit_length() - 1]
    head_bits = high_b[len(seq_bits) : len(seq_bits) + heads.bit_length() - 1]
    part_bits = high_b[len(seq_bits) + len(head_bits) :]
    sum_bits = core + seq_bits + chip_y + part_bits
    qkv_bits = sum_bits + head_bits
    qkv_left = rows_by(ctx_all.reshape(cycle * rows, width), halver.order(qkv_bits))
    qkv_grad = reduce_by(halver, row_product(qkv_left, deltas.reshape(cycle * rows, padded)), sum_bits, 0)
    pieces = qkv_grad.reshape(heads, -1, padded)
    head_order = [int(v) >> head_bits[0] for v in halver.order(head_bits)]
    by_mask = [None] * heads
    for index, mask in enumerate(head_order):
        sent = pieces[index].astype(low)
        if mask:
            sent = lax.ppermute(sent, "seq", [(i, i ^ (mask * seqs)) for i in range(cycle)])
        by_mask[mask] = sent
    by_head = jnp.take(jnp.stack(by_mask), my_head ^ np.arange(heads, dtype=np.int32), axis=0).astype(full)
    own = by_head.shape[1]
    by_head = jnp.transpose(by_head, (1, 0, 2))
    query_grad = by_head[:, :, :size].reshape(own, -1)
    key_grad = by_head[:, :, size : 2 * size].reshape(own, -1)
    value_grad = by_head[:, :, 2 * size : (2 + experts) * size].reshape(own, -1)
    gate_from = (2 + experts) * size
    router_grad = jnp.concatenate(
        [
            by_head[:, :, gate_from : gate_from + experts].reshape(own, -1),
            by_head[:, :, gate_from + experts : gate_from + 2 * experts].reshape(own, -1),
        ],
        axis=1,
    )

    (input_grad, _) = call(
        functools.partial(finish, dims=(seqs, seg, mem, heads, size, experts, parts)),
        [((seqs, seg, width), full), ((seqs * seg, value_weight.shape[1]), low)],
        [back, grad_out, vgate, inputs, gain_one, grad_residual, query_weight, key_weight, value_weight, router_weight],
    )

    def own_rows(array, axis=0):
        return lax.dynamic_slice_in_dim(array, halver.me * own, own, axis=axis)

    def gain_sum(pairs, gain):
        total = jnp.zeros((own,), full)
        for weight, grad in pairs:
            total = total + jnp.sum(own_rows(weight).astype(full) * grad, axis=1)
        return total / own_rows(gain)

    norm1_grad = gain_sum(
        ((query_weight, query_grad), (key_weight, key_grad), (value_weight, value_grad), (router_weight, router_grad)), norm1_gain
    )
    norm2_grad = gain_sum(((up_weight, up_grad),), norm2_gain)
    return (
        output, input_grad, norm1_grad, norm2_grad, query_grad, key_grad, value_grad, router_grad,
        outproj_grad, up_grad, down_grad,
    )


def solution(mesh):
    token = P("batch", "seq", None)
    routes = P("batch", "seq", None, None)
    spread = ("seq", "batch")
    return jax.shard_map(
        local,
        mesh=mesh,
        in_specs=(token, token, token, P("batch"), routes, routes, routes) + (P(),) * 9,
        out_specs=(
            token, token, P(spread), P(spread), P(spread, None), P(spread, None), P(spread, None), P(spread, None),
            P(None, spread), P(spread, None), P(spread, None),
        ),
        check_vma=False,
    )
```

```python
import collections
import functools

import jax
import jax.numpy as jnp
import numpy as np
from jax import lax
from jax.experimental import pallas as pl
from jax.experimental.pallas import tpu as pltpu
from jax.sharding import PartitionSpec as P

epsilon = 1e-05
neg_large = -1e30
slope_base = 0.5
log2_e = 1.4426950408889634
lanes = 128
low = jnp.bfloat16
full = jnp.float32
vmem_bytes = 56 << 20
vmem_less = 24 << 20
cost = {'heads_split': 2000000000, 'heads_third': 2000000000, 'heads_join': 6000000000, 'outer_split': 3000000000}
vmem_back = 56 << 20
vmem_finish = 56 << 20
vmem_big = 56 << 20
vmem_attend = 56 << 20
vmem_end = 56 << 20
vmem_delta = 56 << 20
vmem_plane = 56 << 20

names = ["seqs", "seg", "mem", "rows", "heads", "size"]
names += ["experts", "parts", "share", "cycle", "width", "group"]
Dims = collections.namedtuple("Dims", names)


def dot_nn(left, right):
    return lax.dot_general(left, right, (((1,), (0,)), ((), ())), preferred_element_type=full)


def dot_nt(left, right):
    return lax.dot_general(left, right, (((1,), (1,)), ((), ())), preferred_element_type=full)


def dot_tn(left, right):
    return lax.dot_general(left, right, (((0,), (0,)), ((), ())), preferred_element_type=full)


def norm_parts(values):
    centred = values - jnp.mean(values, axis=-1, keepdims=True)
    spread = jnp.mean(centred * centred, axis=-1, keepdims=True)
    inverse = lax.rsqrt(spread + epsilon)
    return centred * inverse, inverse


def norm_back(grad, hat, inverse, gain_row):
    scaled = grad * gain_row
    along = jnp.mean(scaled * hat, axis=-1, keepdims=True)
    return inverse * (scaled - jnp.mean(scaled, axis=-1, keepdims=True) - hat * along)


smem = pl.BlockSpec(memory_space=pltpu.SMEM)
whole = pl.BlockSpec(memory_space=pltpu.VMEM)
unread = pl.BlockSpec(memory_space=pl.ANY)


def by_step(shape, axis):
    return pl.BlockSpec(shape, lambda i: tuple(i if a == axis else 0 for a in range(len(shape))))


def at_all(shape):
    return pl.BlockSpec(shape, lambda *i: (0,) * len(shape))


def call(kernel, steps, operands, outs, scratch=(), vmem=vmem_bytes, flops=1):
    return pl.pallas_call(
        kernel,
        grid=(steps,),
        out_shape=[jax.ShapeDtypeStruct(shape, kind) for shape, kind, _ in outs],
        in_specs=[spec for _, spec in operands],
        out_specs=[spec for _, _, spec in outs],
        scratch_shapes=list(scratch),
        compiler_params=pltpu.CompilerParams(
            vmem_limit_bytes=vmem, dimension_semantics=("arbitrary",)
        ),
        cost_estimate=pl.CostEstimate(flops=flops, bytes_accessed=1, transcendentals=0),
    )(*[a for a, _ in operands])


def picks(routes, experts):
    slots, tokens = routes.shape
    wide = jnp.concatenate([routes.astype(full), jnp.zeros((8 - slots, tokens), full)], axis=0)
    columns = wide.T
    expert = lax.broadcasted_iota(jnp.int32, (tokens, experts), 1).astype(full)
    total = jnp.zeros((tokens, experts), full)
    for slot in range(slots):
        total = total + (columns[:, slot : slot + 1] == expert).astype(full)
    return total


def fill_wall(wall_ref, wq_ref, wk_ref, wv_ref, wr_ref, d):
    size, experts = d.size, d.experts
    blank = jnp.zeros((lanes - size, d.width), low)
    wall_ref[0:size] = wq_ref[...]
    wall_ref[size:lanes] = jnp.concatenate([wr_ref[0], blank[2 * experts :]], axis=0)
    wall_ref[lanes : lanes + size] = wk_ref[...]
    wall_ref[lanes + size : 2 * lanes] = blank
    for e in range(experts):
        first = (2 + e) * lanes
        wall_ref[first : first + size] = wv_ref[e * size : (e + 1) * size]
        wall_ref[first + size : first + lanes] = blank


def prepare(scal_ref, ctx_ref, wq_ref, wk_ref, wv_ref, wr_ref, wo_ref, wall_ref, exp_ref, out_ref, own_ref, d=None):
    fill_wall(wall_ref.at[0], wq_ref, wk_ref, wv_ref, wr_ref, d)
    ctx = ctx_ref[...].reshape(-1, d.width)
    exp_ref[0] = dot_nt(ctx, wall_ref[0, 2 * lanes :]).astype(low)
    for e in range(d.experts):
        out_ref[0, e * lanes : e * lanes + d.size] = wo_ref[e * d.size : (e + 1) * d.size]
        out_ref[0, e * lanes + d.size : (e + 1) * lanes] = jnp.zeros((lanes - d.size, d.width), low)
    rows = own_ref.shape[1]
    if lanes % rows == 0:
        first = scal_ref[3] * rows
        column = pl.ds(pl.multiple_of(lax.div(first, lanes) * lanes, lanes), lanes)
        turned = wall_ref[0, :, column].T
        for at in range(0, lanes, rows):

            @pl.when(lax.rem(first, lanes) == at)
            def _():
                own_ref[0] = turned[at : at + rows]


def project(
    x_ref, m_ref, vr_ref, mr_ref, or_ref, gain_ref, wq_ref, wk_ref, wv_ref, wr_ref,
    pay_ref, ctx_ref, vgate_ref, ogate_ref, wall_ref, held_ref, d=None
):
    size, experts = d.size, d.experts
    spare = lanes - size

    @pl.when(pl.program_id(0) == 0)
    def _():
        for s in range(d.seqs):
            block = jnp.concatenate([m_ref[s], x_ref[s]], axis=0).astype(full)
            hat, _ = norm_parts(block)
            block_low = (hat * gain_ref[...]).astype(low)
            held_ref[s * d.rows : (s + 1) * d.rows] = block_low
            ctx_ref[s] = block_low

    fill_wall(wall_ref, wq_ref, wk_ref, wv_ref, wr_ref, d)
    ctx = held_ref[...]
    every = dot_nt(ctx, wall_ref[...])
    query = every[:, 0:lanes]
    sig = jax.nn.sigmoid(query[:, size : size + 2 * experts])
    pick = []
    out_pick = []
    out_sig = []
    for s in range(d.seqs):
        pick.append(picks(mr_ref[s, 0], experts))
        pick.append(picks(vr_ref[s, 0], experts))
        out_pick.append(picks(or_ref[s, 0], experts))
        out_sig.append(sig[s * d.rows + d.mem : (s + 1) * d.rows, experts:])
    gate = sig[:, :experts] * jnp.concatenate(pick, axis=0)
    vgate_ref[0] = gate
    ogate_ref[0] = jnp.concatenate(out_sig, axis=0) * jnp.concatenate(out_pick, axis=0)
    high = gate.astype(low)
    rest = (gate - high.astype(full)).astype(low)
    count = d.seqs * d.rows
    value = jnp.zeros((count, lanes), full)
    for e in range(experts):
        value = value + gate[:, e : e + 1] * every[:, (2 + e) * lanes : (3 + e) * lanes]
    lane_at = lax.broadcasted_iota(jnp.int32, (count, lanes), 1)
    query = jnp.where(lane_at < size, query, 0.0).astype(low)
    keys = every[:, lanes : 2 * lanes].astype(low)
    value = jnp.concatenate(
        [value[:, :size].astype(low), high, rest, jnp.zeros((count, spare - 2 * experts), low)], axis=1
    )
    half = d.share // 2
    for s in range(d.seqs):
        mine = slice(s * d.rows, (s + 1) * d.rows)
        for p in range(d.parts):
            first = s * d.rows + d.mem + p * d.share
            pay_ref[p, 0, s, 0 : d.rows, 0:lanes] = keys[mine]
            pay_ref[p, 0, s, 0 : d.rows, lanes:] = value[mine]
            pay_ref[p, 0, s, d.rows :, 0:lanes] = query[first : first + half]
            pay_ref[p, 0, s, d.rows :, lanes:] = query[first + half : first + d.share]


def lane_sums(product, experts):
    slot = lax.broadcasted_iota(jnp.int32, (experts * lanes, lanes), 0) // lanes
    target = lax.broadcasted_iota(jnp.int32, (experts * lanes, lanes), 1)
    ones = (slot == target).astype(full).astype(low)
    high = product.astype(low)
    rest = (product - high.astype(full)).astype(low)
    return (dot_nn(high, ones) + dot_nn(rest, ones))[:, :experts]


def turn_context(scal_ref, ctx_ref, *refs, bits=None):
    first_ref, second_ref = refs[-2:]
    value = ctx_ref[...].reshape(-1, ctx_ref.shape[-1])
    turn(value, first_ref, scal_ref[3], bits[0])
    turn(value, second_ref, scal_ref[3], bits[1])


def key_value(pay_ref, k_ref, v_ref, d):
    for j in range(d.cycle):
        k_ref[j * d.mem : (j + 1) * d.mem] = pay_ref[j, 0 : d.mem, 0:lanes]
        v_ref[j * d.mem : (j + 1) * d.mem] = pay_ref[j, 0 : d.mem, lanes:]
        base = d.cycle * d.mem + j * d.seg
        k_ref[base : base + d.seg] = pay_ref[j, d.mem : d.rows, 0:lanes]
        v_ref[base : base + d.seg] = pay_ref[j, d.mem : d.rows, lanes:]


def query_block(pay_ref, first, d):
    found = []
    for j in range(first, first + d.group):
        found.append(pay_ref[j, d.rows :, 0:lanes])
        found.append(pay_ref[j, d.rows :, lanes:])
    return jnp.concatenate(found, axis=0)


def attend(scal_ref, pay_ref, *refs, d=None):
    att_ref, keep_ref, lse_ref, k_ref, v_ref = refs[-5:]
    share, group = d.share, d.group
    mem_len = d.cycle * d.mem
    ctx_len = d.cycle * d.rows
    length, head, part = scal_ref[0], scal_ref[1], scal_ref[2]
    key_value(pay_ref, k_ref, v_ref, d)
    slope = slope_base * (head + 1).astype(full) / ctx_len * log2_e
    place = lax.broadcasted_iota(jnp.int32, (1, ctx_len), 1) - mem_len
    bias = jnp.where(place < length, place.astype(full) * slope, neg_large)
    q_rows = group * share
    for first in range(0, d.cycle, group):
        width = mem_len + (first + group) * d.seg
        cut = width - group * d.seg
        query = query_block(pay_ref, first, d)
        scores = dot_nt(query, k_ref[0:width]) * (d.size**-0.5 * log2_e) + bias[:, :width]
        row = lax.broadcasted_iota(jnp.int32, (q_rows, group * d.seg), 0)
        col = lax.broadcasted_iota(jnp.int32, (q_rows, group * d.seg), 1)
        row_place = (row // share) * d.seg + part * share + row % share
        tail = jnp.where(col <= row_place, scores[:, cut:], neg_large)
        scores = jnp.concatenate([scores[:, :cut], tail], axis=1)
        top = jnp.max(scores, axis=1, keepdims=True)
        weights = jnp.exp2(scores - top)
        total = jnp.sum(weights, axis=1, keepdims=True)
        attended = dot_nn(weights.astype(low), v_ref[0:width]) / total
        keep_ref[first * share : first * share + q_rows] = attended
        lse_ref[first * share : first * share + q_rows] = top + jnp.log2(total)
        for j in range(group):
            att_ref[first + j] = attended[j * share : (j + 1) * share].astype(low)


def attend_back(
    scal_ref, pay_ref, keep_ref, lse_ref, grad_ref, *refs, d=None
):
    out_ref, k_ref, v_ref, dk_ref, dv_ref = refs[-5:]
    share, group, size = d.share, d.group, d.size
    half = share // 2
    mem_len = d.cycle * d.mem
    ctx_len = d.cycle * d.rows
    length, head, part = scal_ref[0], scal_ref[1], scal_ref[2]
    key_value(pay_ref, k_ref, v_ref, d)
    scale = size**-0.5
    slope = slope_base * (head + 1).astype(full) / ctx_len * log2_e
    place = lax.broadcasted_iota(jnp.int32, (ctx_len, lanes), 0) - mem_len
    bias = jnp.where(place < length, place.astype(full) * slope, neg_large)[:, 0:1]
    dk_ref[...] = jnp.zeros_like(dk_ref)
    dv_ref[...] = jnp.zeros_like(dv_ref)
    q_rows = group * share
    lane_at = lax.broadcasted_iota(jnp.int32, (q_rows, lanes), 1)
    for first in range(0, d.cycle, group):
        width = mem_len + (first + group) * d.seg
        cut = width - group * d.seg
        begin = first * share
        query = query_block(pay_ref, first, d)
        raw = jnp.concatenate([grad_ref[j] for j in range(first, first + group)], axis=0)
        grad = jnp.where(lane_at < size, raw, jnp.zeros_like(raw))
        kept = keep_ref[begin : begin + q_rows]
        delta = jnp.sum(jnp.where(lane_at < size, grad.astype(full) * kept, 0.0), axis=1, keepdims=True)
        both = jnp.concatenate(
            [
                jnp.broadcast_to(delta, (q_rows, lanes)),
                jnp.broadcast_to(lse_ref[begin : begin + q_rows], (q_rows, lanes)),
            ],
            axis=1,
        ).T
        delta_row = both[0:1]
        lse_row = both[lanes : lanes + 1]
        scores = dot_nt(k_ref[0:width], query) * (scale * log2_e) + bias[:width]
        weights = jnp.exp2(scores - lse_row)
        row = lax.broadcasted_iota(jnp.int32, (group * d.seg, q_rows), 0)
        col = lax.broadcasted_iota(jnp.int32, (group * d.seg, q_rows), 1)
        col_place = (col // share) * d.seg + part * share + col % share
        weights = jnp.concatenate([weights[:cut], jnp.where(row <= col_place, weights[cut:], 0.0)], axis=0)
        grad_weights = dot_nt(v_ref[0:width], grad)
        grad_scores = (weights * (grad_weights - delta_row)).astype(low)
        dk_ref[0:width] += dot_nn(grad_scores, query)
        dv_ref[0:width] += dot_nn(weights.astype(low), grad)
        dq = (dot_tn(grad_scores, k_ref[0:width]) * scale).astype(low)
        for j in range(group):
            out_ref[first + j, d.rows :, 0:lanes] = dq[j * share : j * share + half]
            out_ref[first + j, d.rows :, lanes:] = dq[j * share + half : (j + 1) * share]
    for j in range(d.cycle):
        base = mem_len + j * d.seg
        dk = jnp.concatenate([dk_ref[j * d.mem : (j + 1) * d.mem], dk_ref[base : base + d.seg]], axis=0)
        dv = jnp.concatenate([dv_ref[j * d.mem : (j + 1) * d.mem], dv_ref[base : base + d.seg]], axis=0)
        out_ref[j, 0 : d.rows, 0:lanes] = (dk * scale).astype(low)
        out_ref[j, 0 : d.rows, lanes:] = dv.astype(low)


def place_of(mask, bits):
    place = jnp.int32(0)
    for at, bit in enumerate(bits):
        place = place + ((mask >> bit) & 1) * (1 << (len(bits) - 1 - at))
    return place


def turn(value, out_ref, me, bits):
    turned = value.T
    count = 1 << len(bits)
    own = turned.shape[0] // count
    for block in range(count):
        place = place_of(block ^ me, bits)
        side = lax.div(place, count // 2)
        inside = lax.rem(place, count // 2)
        out_ref[side, pl.ds(pl.multiple_of(inside * own, own), own), :] = turned[block * own : (block + 1) * own]


def beside(turn_ref, pack_ref):
    half, tokens = turn_ref.shape[1] // 2, turn_ref.shape[2]
    first = pack_ref.shape[1] - 2 * tokens
    pack_ref[:, first : first + tokens] = turn_ref[1, 0:half]
    pack_ref[:, first + tokens :] = turn_ref[1, half:]


def feed(
    scal_ref, att_ref, ogate_ref, x_ref, gain_ref, live_ref, gf_ref, wo_ref, up_ref, down_ref,
    out_mix_ref, act_ref, pack_ref, out_ref, resid_ref, branch_ref, normed_ref, turned_ref, gatt_ref,
    sum_ref, ffn_ref, back_ref, held_ref, turn_ref, d=None, bits=None
):
    step = pl.program_id(0)
    last = pl.num_programs(0) - 1 - d.heads
    experts = d.experts
    me = scal_ref[3]

    @pl.when(step == 0)
    def _():
        for s in range(d.seqs):
            sum_ref[s * d.seg : (s + 1) * d.seg] = x_ref[s].astype(full)
        ffn_ref[...] = jnp.zeros_like(ffn_ref)
        back_ref[...] = jnp.zeros_like(back_ref)

    @pl.when(step < d.heads)
    def _():
        found = [att_ref[p, 0, s] for s in range(d.seqs) for p in range(d.parts)]
        att = jnp.concatenate(found, axis=0).astype(full)
        gate = ogate_ref[0]
        mixed = jnp.concatenate([(gate[:, e : e + 1] * att).astype(low) for e in range(experts)], axis=1)
        wide = mixed.shape[1]
        out_mix_ref[:, pl.ds(pl.multiple_of(step * wide, lanes), wide)] = mixed
        sum_ref[...] += dot_nn(mixed, wo_ref[0])

    @pl.when(step == d.heads - 1)
    def _():
        hat, _ = norm_parts(sum_ref[...])
        normed = (hat * gain_ref[...]).astype(low)
        held_ref[...] = normed
        if bits is None:
            normed_ref[...] = normed
        else:
            turn(normed, turn_ref, me, bits[1])
            normed_ref[...] = turn_ref[0]
            beside(turn_ref, pack_ref)

    @pl.when((step >= d.heads) & (step <= last))
    def _():
        coeff = 0.7978845608028654
        held = held_ref[...]
        outer_grad = gf_ref[...]
        acts = []
        grads = []
        part = up_ref.shape[1] // 4
        for c in range(4):
            mine = slice(c * part, (c + 1) * part)
            value = dot_nn(held, up_ref[:, mine])
            grad_act = dot_nt(outer_grad, down_ref[mine, :])
            square = value * value
            wave = jnp.tanh(value * (coeff + (0.044715 * coeff) * square))
            rise = 0.5 + 0.5 * wave
            acts.append((value * rise).astype(low))
            slope = rise + (0.5 * value) * (1.0 - wave * wave) * (coeff + (3 * 0.044715 * coeff) * square)
            grads.append((grad_act * slope).astype(low))
        act = jnp.concatenate(acts, axis=1)
        gu = jnp.concatenate(grads, axis=1)
        ffn_ref[...] += dot_nn(act, down_ref[...])
        back_ref[...] += dot_nt(gu, up_ref[...])
        block = step - d.heads
        span = act.shape[1]
        if bits is None:
            pack_ref[:, pl.ds(pl.multiple_of(block * span, span), span)] = gu
            act_ref[:, pl.ds(pl.multiple_of(block * span, span), span)] = act
        else:
            half = 1 << (len(bits[0]) - 1)
            own = act_ref.shape[1] // half
            pack_ref[:, pl.ds(pl.multiple_of(half * own + block * span, lanes), span)] = gu
            for b in range(span // own):
                piece = act[:, b * own : (b + 1) * own]
                place = place_of((block * (span // own) + b) ^ me, bits[0])
                inside = pl.ds(pl.multiple_of(lax.rem(place, half) * own, own), own)

                @pl.when(place < half)
                def _():
                    act_ref[:, inside] = piece

                @pl.when(place >= half)
                def _():
                    pack_ref[:, inside] = piece

    @pl.when(step == last)
    def _():
        residual = sum_ref[...]
        out_ref[...] = ((residual + ffn_ref[...]) * live_ref[...]).astype(low)
        hat, inverse = norm_parts(residual)
        grad = gf_ref[...].astype(full) + norm_back(back_ref[...], hat, inverse, gain_ref[...])
        resid_ref[...] = grad
        branch = grad.astype(low)
        branch_ref[...] = branch
        if bits is None:
            turned_ref[...] = branch
        else:
            turn(branch, turn_ref, me, bits[2])
            turned_ref[...] = turn_ref[0]
            beside(turn_ref, out_mix_ref)

    @pl.when(step > last)
    def _():
        unmix(branch_ref, att_ref, ogate_ref, wo_ref, gatt_ref, d=d)


def unmix(branch_ref, att_ref, ogate_ref, wo_ref, out_ref, d=None):
    size, experts = d.size, d.experts
    tokens = d.seqs * d.seg
    grad_mixed = dot_nt(branch_ref[...], wo_ref[0])
    found = [att_ref[p, 0, s] for s in range(d.seqs) for p in range(d.parts)]
    att = jnp.concatenate(found, axis=0).astype(full)
    gate = ogate_ref[0]
    grad = jnp.zeros((tokens, lanes), full)
    product = []
    for e in range(experts):
        piece = grad_mixed[:, e * lanes : (e + 1) * lanes]
        grad = grad + gate[:, e : e + 1] * piece
        product.append(piece * att)
    logit = lane_sums(jnp.concatenate(product, axis=1), experts) * gate * (1.0 - gate)
    joined = jnp.concatenate(
        [grad[:, :size].astype(low), logit.astype(low), jnp.zeros((tokens, lanes - size - experts), low)], axis=1
    )
    for s in range(d.seqs):
        for p in range(d.parts):
            first = s * d.seg + p * d.share
            out_ref[p, 0, s] = joined[first : first + d.share]


def make_deltas(back_ref, grad_ref, vgate_ref, exp_ref, *refs, d=None):
    size, experts = d.size, d.experts
    q_found, kv_found, lo_found = [], [], []
    for s in range(d.seqs):
        kv = back_ref[0, 0, s, 0 : d.rows, :]
        if d.parts > 1:
            kv = kv.astype(full)
            for p in range(1, d.parts):
                kv = kv + back_ref[p, 0, s, 0 : d.rows, :].astype(full)
            kv = kv.astype(low)
        kv_found.append(kv)
        q_found.append(jnp.zeros((d.mem, lanes), low))
        lo_found.append(jnp.zeros((d.mem, lanes), low))
        for p in range(d.parts):
            q_found.append(back_ref[p, 0, s, d.rows :, 0:lanes])
            q_found.append(back_ref[p, 0, s, d.rows :, lanes:])
            lo_found.append(grad_ref[p, 0, s])
    query = jnp.concatenate(q_found, axis=0)
    kv = jnp.concatenate(kv_found, axis=0)
    out_logit = jnp.concatenate(lo_found, axis=0)[:, size : size + experts]
    gate = vgate_ref[0]
    lane_at = lax.broadcasted_iota(jnp.int32, (d.seqs * d.rows, lanes), 1)
    value = jnp.where(lane_at < size, kv[:, lanes:].astype(full), 0.0)
    product = jnp.concatenate(
        [value * exp_ref[0, :, e * lanes : (e + 1) * lanes].astype(full) for e in range(experts)], axis=1
    )
    logit = (lane_sums(product, experts) * gate * (1.0 - gate)).astype(low)
    first = jnp.concatenate(
        [query[:, :size], logit, out_logit, jnp.zeros((d.seqs * d.rows, lanes - size - 2 * experts), low)], axis=1
    )
    step = pl.program_id(0)
    for at, delta_ref in enumerate(refs[-2:]):

        @pl.when(step // (d.heads // 2) == at)
        def _():
            delta_ref[:, 0:lanes] = first
            delta_ref[:, lanes : 2 * lanes] = kv[:, :lanes]
            for e in range(experts):
                delta_ref[:, (2 + e) * lanes : (3 + e) * lanes] = (gate[:, e : e + 1] * value).astype(low)


def finish(first_ref, second_ref, x_ref, gain_ref, resid_ref, wall_ref, *refs, d=None):
    out_ref, sum_ref = refs[-2:]
    step = pl.program_id(0)

    @pl.when(step == 0)
    def _():
        sum_ref[...] = jnp.zeros_like(sum_ref)

    for at, delta_ref in enumerate((first_ref, second_ref)):

        @pl.when(step // (d.heads // 2) == at)
        def _():
            rows = [delta_ref[s * d.rows + d.mem : (s + 1) * d.rows] for s in range(d.seqs)]
            sum_ref[...] += dot_nn(jnp.concatenate(rows, axis=0), wall_ref[0])

    @pl.when(step == pl.num_programs(0) - 1)
    def _():
        for s in range(d.seqs):
            hat, inverse = norm_parts(x_ref[s].astype(full))
            mine = slice(s * d.seg, (s + 1) * d.seg)
            out_ref[s] = resid_ref[mine] + norm_back(sum_ref[mine], hat, inverse, gain_ref[...])


def both(first, second, axis):
    return jnp.concatenate([first, second], axis=axis)


def send_down(gf_ref, act_ref, act_got_ref, *refs):
    refs[-1][...] = dot_nn(gf_ref[...], both(act_ref[...], act_got_ref[...], 0)).astype(low)


def send_up(left_ref, left_got_ref, gu_ref, gu_got_ref, *refs):
    left = both(left_ref[...], left_got_ref[...], 1)
    refs[-1][...] = dot_nn(left, both(gu_ref[...], gu_got_ref[...], 0)).astype(low)


def cross_down(gf_ref, act_ref, act_got_ref, new_ref, *refs):
    send_ref, keep_ref = refs[-2:]
    total = dot_nn(gf_ref[...], both(act_ref[...], act_got_ref[...], 0)) + new_ref[...].astype(full)
    half = total.shape[1] // 2
    keep_ref[...] = total[:, :half]
    send_ref[...] = total[:, half:].astype(low)


def cross_up(left_ref, left_got_ref, gu_ref, gu_got_ref, new_ref, *refs):
    send_ref, keep_ref = refs[-2:]
    left = both(left_ref[...], left_got_ref[...], 1)
    total = dot_nn(left, both(gu_ref[...], gu_got_ref[...], 0)) + new_ref[...].astype(full)
    half = total.shape[0] // 2
    keep_ref[...] = total[:half]
    send_ref[...] = total[half:].astype(low)


def fold_lanes(keep_ref, got_ref, *refs):
    send_ref, left_ref = refs[-2:]
    total = keep_ref[...] + got_ref[...].astype(full)
    half = total.shape[1] // 2
    left_ref[...] = total[:, :half]
    send_ref[...] = total[:, half:].astype(low)


def end_feed(keep_d_ref, got_d_ref, keep_u_ref, got_u_ref, weight_ref, gain_ref, *refs):
    down_ref, up_ref, norm_ref = refs[-3:]
    down_ref[...] = (keep_d_ref[...] + got_d_ref[...].astype(full)).T
    total = keep_u_ref[...] + got_u_ref[...].astype(full)
    up_ref[...] = total
    along = jnp.sum(total * weight_ref[...].astype(full), axis=1, keepdims=True)
    norm_ref[...] = row_of(along / gain_ref[...])


def outer_send(left_ref, left_got_ref, right_ref, right_got_ref, *refs):
    left = both(left_ref[...], left_got_ref[...], 1)
    refs[-1][...] = dot_nn(left, both(right_ref[...], right_got_ref[...], 0)).astype(low)


def outer_split(left_ref, left_got_ref, right_ref, right_got_ref, new_ref, *refs):
    send_ref, keep_ref = refs[-2:]
    left = both(left_ref[...], left_got_ref[...], 1)
    total = dot_nn(left, both(right_ref[...], right_got_ref[...], 0)) + new_ref[...].astype(full)
    half = total.shape[0] // 2
    keep_ref[...] = total[:half]
    send_ref[...] = total[half:].astype(low)


def heads_send(a_ref, a_got_ref, b_ref, b_got_ref, da_ref, da_got_ref, db_ref, db_got_ref, *refs):
    a_out, b_out = refs[-2:]
    a_out[...] = dot_nn(both(a_ref[0], a_got_ref[...], 1), both(da_ref[...], da_got_ref[...], 0)).astype(low)
    b_out[...] = dot_nn(both(b_ref[0], b_got_ref[...], 1), both(db_ref[...], db_got_ref[...], 0)).astype(low)


def heads_split(
    a_ref, a_got_ref, b_ref, b_got_ref, da_ref, da_got_ref, db_ref, db_got_ref, new_a_ref, new_b_ref, *refs
):
    outs = refs[-4:]
    left = both(a_ref[0], a_got_ref[...], 1), both(b_ref[0], b_got_ref[...], 1)
    right = both(da_ref[...], da_got_ref[...], 0), both(db_ref[...], db_got_ref[...], 0)
    for at, new_ref in enumerate((new_a_ref, new_b_ref)):
        total = dot_nn(left[at], right[at]) + new_ref[...].astype(full)
        half = total.shape[0] // 2
        outs[2 + at][...] = total[:half]
        outs[at][...] = total[half:].astype(low)


def heads_third(keep_a_ref, keep_b_ref, got_a_ref, got_b_ref, *refs):
    outs = refs[-4:]
    for at, (keep_ref, got_ref) in enumerate(((keep_a_ref, got_a_ref), (keep_b_ref, got_b_ref))):
        half = keep_ref.shape[0] // 2
        outs[2 + at][...] = keep_ref[:half] + got_ref[:half].astype(full)
        outs[at][...] = (keep_ref[half:] + got_ref[half:].astype(full)).astype(low)


def heads_join(keep_a_ref, keep_b_ref, keep_o_ref, got_a_ref, got_b_ref, got_o_ref, *refs):
    send_ref, left_ref = refs[-2:]
    half = send_ref.shape[0]
    first = 0
    for keep_ref, got_ref in ((keep_a_ref, got_a_ref), (keep_b_ref, got_b_ref), (keep_o_ref, got_o_ref)):
        here = slice(first, first + keep_ref.shape[1])
        left_ref[:, here] = keep_ref[:half] + got_ref[:half].astype(full)
        send_ref[:, here] = (keep_ref[half:] + got_ref[half:].astype(full)).astype(low)
        first += keep_ref.shape[1]


def fold(keep_ref, got_ref, *refs):
    send_ref, left_ref = refs[-2:]
    half = keep_ref.shape[0] // 2
    left_ref[...] = keep_ref[:half] + got_ref[:half].astype(full)
    send_ref[...] = (keep_ref[half:] + got_ref[half:].astype(full)).astype(low)


def row_of(column):
    n = column.shape[0]
    same = lax.broadcasted_iota(jnp.int32, (n, n), 0) == lax.broadcasted_iota(jnp.int32, (n, n), 1)
    return jnp.sum(jnp.where(same, column, 0.0), axis=0, keepdims=True)


def assemble(keep_ref, got_ref, wall_ref, gain_ref, *refs, d=None):
    q_ref, k_ref, v_ref, r_ref, out_ref, norm_ref = refs[-6:]
    size, experts = d.size, d.experts
    slots = 2 + experts

    def total(first):
        here = slice(first * lanes, (first + 1) * lanes)
        return keep_ref[:, here] + got_ref[:, here].astype(full)

    every = [[total(h * slots + at) for at in range(slots)] for h in range(d.heads)]
    along = jnp.zeros(every[0][0].shape, full)
    for h in range(d.heads):
        for at in range(slots):
            along = along + every[h][at] * wall_ref[h, :, at * lanes : (at + 1) * lanes].astype(full)
    norm_ref[...] = row_of(jnp.sum(along, axis=1, keepdims=True) / gain_ref[...])
    q_ref[...] = jnp.concatenate([one[0][:, :size] for one in every], axis=1)
    k_ref[...] = jnp.concatenate([one[1][:, :size] for one in every], axis=1)
    v_ref[...] = jnp.concatenate([one[2 + e][:, :size] for one in every for e in range(experts)], axis=1)
    values = [one[0][:, size : size + experts] for one in every]
    outs = [one[0][:, size + experts : size + 2 * experts] for one in every]
    r_ref[...] = jnp.concatenate(values + outs, axis=1)
    out_ref[...] = jnp.concatenate([total(d.heads * slots + at)[:, :size] for at in range(d.heads * experts)], axis=1)


class Halver:
    def __init__(self):
        self.cycle = lax.axis_size("seq")
        self.width = lax.axis_size("batch")
        self.low_bits = self.width.bit_length() - 1
        self.high_bits = self.cycle.bit_length() - 1
        self.me = lax.axis_index("seq") * self.width + lax.axis_index("batch")

    def swap(self, value, bit):
        if bit < self.low_bits:
            axis, size, mask = "batch", self.width, 1 << bit
        else:
            axis, size, mask = "seq", self.cycle, 1 << (bit - self.low_bits)
        return lax.ppermute(value, axis, [(i, i ^ mask) for i in range(size)])

    def order(self, bits):
        count = len(bits)
        found = np.zeros(1 << count, np.int32)
        for place in range(1 << count):
            for at, bit in enumerate(bits):
                if place >> (count - 1 - at) & 1:
                    found[place] |= 1 << bit
        return found


def halve(value, axis):
    size = value.shape[axis] // 2
    return (
        lax.slice_in_dim(value, 0, size, axis=axis),
        lax.slice_in_dim(value, size, 2 * size, axis=axis),
    )


def reduced(halver, product, bits, axis):
    got = halver.swap(product(2, 4).astype(low), bits[0])
    got_keep, got_send = halve(got, axis)
    got = halver.swap((product(1, 2) + got_send.astype(full)).astype(low), bits[1])
    keep = product(0, 1) + got_keep.astype(full) + got.astype(full)
    for bit in bits[2:]:
        keep, send = halve(keep, axis)
        keep = keep + halver.swap(send.astype(low), bit).astype(full)
    return keep


def local(
    inputs, memory, cotangent, valid_len, value_routes, memory_routes, output_routes, norm1_gain, norm2_gain,
    query_weight, key_weight, value_weight, router_weight, output_weight, up_weight, down_weight
):
    seqs, seg, width = inputs.shape
    mem = memory.shape[1]
    rows = seg + mem
    heads = value_routes.shape[2]
    slots_count = value_routes.shape[3]
    qk_width = query_weight.shape[1]
    size = qk_width // heads
    experts = value_weight.shape[1] // qk_width
    span = experts * size
    ff = up_weight.shape[1]
    tokens = seqs * seg
    halver = Halver()
    cycle = halver.cycle
    parts = cycle // (seqs * heads)
    share = seg // parts
    d = Dims(seqs, seg, mem, rows, heads, size, experts, parts, share, cycle, width, 2)
    pay_rows = rows + share // 2
    at = lax.axis_index("seq")
    my_seq = at % seqs
    my_head = at // seqs % heads
    my_part = at // (seqs * heads)
    my_length = lax.dynamic_index_in_dim(valid_len, my_seq, 0, keepdims=False)
    scal = jnp.stack([my_length, my_head, my_part, halver.me]).astype(jnp.int32)
    gain_one = norm1_gain.reshape(1, width)
    gain_two = norm2_gain.reshape(1, width)
    place = at * seg + jnp.arange(seg, dtype=jnp.int32)
    live = (place[None, :] < valid_len[:, None]).astype(full).reshape(tokens, 1)
    grad_ffn = (cotangent.reshape(tokens, width).astype(full) * live).astype(low)
    wq, wk, wv, wr = query_weight.T, key_weight.T, value_weight.T, router_weight.T
    wr = jnp.concatenate(
        [wr[: heads * experts].reshape(heads, experts, width), wr[heads * experts :].reshape(heads, experts, width)], axis=1
    )
    v_routes = jnp.transpose(value_routes, (0, 2, 3, 1))
    m_routes = jnp.transpose(memory_routes, (0, 2, 3, 1))
    o_routes = jnp.transpose(output_routes, (0, 2, 3, 1))
    blocks = cycle * halver.width
    own = width // blocks
    wide = experts * lanes
    wall_rows = 2 * lanes + wide
    wall_shape = (heads, wall_rows, width)

    def routes_spec(count):
        return by_step((seqs, 1, slots_count, count), 1)

    def head_spec(*tail):
        return by_step((parts, 1, seqs) + tail, 1)

    def given(array):
        return (array, at_all(array.shape))

    def made(shape, kind):
        return (shape, kind, at_all(shape))

    pay, ctx, vgate, ogate = call(
        functools.partial(project, d=d),
        heads,
        [
            given(inputs),
            given(memory),
            (v_routes, routes_spec(seg)),
            (m_routes, routes_spec(mem)),
            (o_routes, routes_spec(seg)),
            given(gain_one),
            (wq, by_step((size, width), 0)),
            (wk, by_step((size, width), 0)),
            (wv, by_step((span, width), 0)),
            (wr, by_step((1, 2 * experts, width), 0)),
        ],
        [
            ((parts, heads, seqs, pay_rows, 2 * lanes), low, head_spec(pay_rows, 2 * lanes)),
            made((seqs, rows, width), low),
            ((heads, seqs * rows, experts), full, by_step((1, seqs * rows, experts), 0)),
            ((heads, tokens, experts), full, by_step((1, tokens, experts), 0)),
        ],
        scratch=[pltpu.VMEM(wall_shape[1:], low), pltpu.VMEM((seqs * rows, width), low)],
    )
    wall, expanded, wo, wall_own = call(
        functools.partial(prepare, d=d),
        heads,
        [
            (scal, smem),
            given(ctx),
            (wq, by_step((size, width), 0)),
            (wk, by_step((size, width), 0)),
            (wv, by_step((span, width), 0)),
            (wr, by_step((1, 2 * experts, width), 0)),
            (output_weight, by_step((span, width), 0)),
        ],
        [
            (wall_shape, low, by_step((1,) + wall_shape[1:], 0)),
            ((heads, seqs * rows, wide), low, by_step((1, seqs * rows, wide), 0)),
            ((heads, wide, width), low, by_step((1, wide, width), 0)),
            ((heads, own, wall_rows), low, by_step((1, own, wall_rows), 0)),
        ],
    )
    up_own = lax.dynamic_slice_in_dim(up_weight, halver.me * own, own, axis=0)
    bit_count = halver.low_bits + halver.high_bits
    low_b = list(range(halver.low_bits))
    high_b = list(range(halver.low_bits, bit_count))
    core, chip_y, chip_x, chip_z = low_b[:1], low_b[1:], high_b[:1], high_b[1:]
    down_bits = core + chip_x + chip_y + chip_z
    up_bits = core + chip_y + chip_z + chip_x
    out_bits = core + chip_z[:1] + chip_x + chip_y + chip_z[1:]
    fast = own == 32 and ff == blocks * lanes and len(chip_z) == 2 and len(chip_y) == 1

    qkv_bits = down_bits, core + chip_y + chip_z[:1] + chip_x + chip_z[1:]
    grad_ffn_t = grad_ffn.T
    after = [wo]
    if fast:
        turned_ctx = (2, width // 2, seqs * rows)
        ctx_a, ctx_b = call(
            functools.partial(turn_context, bits=qkv_bits),
            1,
            [(scal, smem), given(ctx), (wo, unread)],
            [made(turned_ctx, low), made(turned_ctx, low)],
        )
        grad_ffn_both = jnp.concatenate([grad_ffn_t, halver.swap(grad_ffn_t, core[0])], axis=1)
        ctx_a_got, ctx_b_got = halver.swap(ctx_a[1], core[0]), halver.swap(ctx_b[1], core[0])
        after += [grad_ffn_both, ctx_a_got, ctx_b_got]
    pay = lax.all_to_all(pay.reshape(cycle, pay_rows, 2 * lanes), "seq", 0, 0)
    att, kept, lse = call(
        functools.partial(attend, d=d),
        1,
        [(scal, smem), given(pay)] + [(a, unread) for a in after],
        [
            made((cycle, share, lanes), low),
            made((cycle * share, lanes), full),
            made((cycle * share, 1), full),
        ],
        scratch=[pltpu.VMEM((cycle * rows, lanes), low)] * 2,
        vmem=vmem_attend,
    )
    att = lax.all_to_all(att, "seq", 0, 0)
    steps = 4
    att_heads = att.reshape(parts, heads, seqs, share, lanes)

    def ff_block(i):
        return jnp.clip(i - heads, 0, steps - 1)

    def head_of(i):
        return jnp.where(i < heads + steps, jnp.minimum(i, heads - 1), i - heads - steps)

    def back_of(i):
        return jnp.maximum(i - heads - steps, 0)

    turned_shape = (width // 2, tokens) if fast else (tokens, width)
    act_shape = (tokens, ff // 2) if fast else (tokens, ff)
    pack_shape = (tokens, ff // 2 + ff + 2 * tokens) if fast else (tokens, ff)
    mix_shape = (tokens, heads * wide + 2 * tokens) if fast else (tokens, heads * wide)
    mixed, act, pack, output, grad_residual, grad_branch, normed, turned, grad_out = call(
        functools.partial(feed, d=d, bits=(tuple(down_bits), tuple(up_bits), tuple(out_bits)) if fast else None),
        2 * heads + steps,
        [
            (scal, smem),
            (att_heads, pl.BlockSpec((parts, 1, seqs, share, lanes), lambda i: (0, head_of(i), 0, 0, 0))),
            (ogate, pl.BlockSpec((1, tokens, experts), lambda i: (head_of(i), 0, 0))),
            given(inputs),
            given(gain_two),
            given(live),
            given(grad_ffn),
            (wo, pl.BlockSpec((1, wide, width), lambda i: (head_of(i), 0, 0))),
            (up_weight, pl.BlockSpec((width, ff // steps), lambda i: (0, ff_block(i)))),
            (down_weight, pl.BlockSpec((ff // steps, width), lambda i: (ff_block(i), 0))),
        ],
        [
            made(mix_shape, low),
            made(act_shape, low),
            made(pack_shape, low),
            made((tokens, width), low),
            made((tokens, width), full),
            made((tokens, width), low),
            made(turned_shape, low),
            made(turned_shape, low),
            (
                (parts, heads, seqs, share, lanes),
                low,
                pl.BlockSpec((parts, 1, seqs, share, lanes), lambda i: (0, back_of(i), 0, 0, 0)),
            ),
        ],
        scratch=[pltpu.VMEM((tokens, width), full)] * 3
        + [pltpu.VMEM((tokens, width), low), pltpu.VMEM((2, width // 2, tokens), low)],
    )
    output = output.reshape(seqs, seg, width)

    pay_shape = (cycle, pay_rows, 2 * lanes)

    def attended_back(grad_att, *after):
        (back,) = call(
            functools.partial(attend_back, d=d),
            1,
            [(scal, smem), given(pay), given(kept), given(lse), given(grad_att)]
            + [(a, unread) for a in after],
            [made(pay_shape, low)],
            scratch=[pltpu.VMEM((cycle * rows, lanes), low)] * 2 + [pltpu.VMEM((cycle * rows, lanes), full)] * 2,
            vmem=vmem_back,
        )
        return back

    delta_shape = (seqs * rows, heads // 2 * wall_rows)
    first_half = pl.BlockSpec((seqs * rows, wall_rows), lambda i: (0, jnp.minimum(i, heads // 2 - 1)))
    second_half = pl.BlockSpec((seqs * rows, wall_rows), lambda i: (0, jnp.maximum(i - heads // 2, 0)))

    def head_deltas(returned, grad_out, *after):
        return call(
            functools.partial(make_deltas, d=d),
            heads,
            [
                (returned.reshape(parts, heads, seqs, pay_rows, 2 * lanes), head_spec(pay_rows, 2 * lanes)),
                (grad_out, head_spec(share, lanes)),
                (vgate, by_step((1, seqs * rows, experts), 0)),
                (expanded, by_step((1, seqs * rows, wide), 0)),
            ]
            + [(a, unread) for a in after],
            [(delta_shape, low, first_half), (delta_shape, low, second_half)],
            vmem=vmem_delta,
            flops=cost.get("deltas", 1),
        )

    def finished(deltas, *after):
        (input_grad,) = call(
            functools.partial(finish, d=d),
            heads,
            [
                (deltas[0], first_half),
                (deltas[1], second_half),
                given(inputs),
                given(gain_one),
                given(grad_residual),
                (wall, by_step((1, wall_rows, width), 0)),
            ]
            + [(a, unread) for a in after],
            [made((seqs, seg, width), full)],
            scratch=[pltpu.VMEM((tokens, width), full)],
            vmem=vmem_finish,
        )
        return input_grad

    def rows_by(array, order):
        cols = array.T.reshape(blocks, -1, array.shape[0])
        return jnp.take(cols, order ^ halver.me, axis=0).reshape(-1, array.shape[0])

    def row_product(left, right):
        quarter = left.shape[0] // 4
        return lambda lo, hi: dot_nn(left[lo * quarter : hi * quarter], right)

    gain_rows = lax.dynamic_slice_in_dim(jnp.stack([norm1_gain, norm2_gain], axis=1), halver.me * own, own, axis=0)
    if fast:
        split = 2
        pack_got = halver.swap(pack, core[0])
        mixed_got = halver.swap(mixed, core[0])
        assert width // 4 == tokens

        def down_products(piece):
            return [
                (grad_ffn_both, by_step((width // split, 2 * tokens), 0)),
                (act, pl.BlockSpec((tokens, ff // 4), lambda i: (0, piece))),
                (pack_got, pl.BlockSpec((tokens, ff // 4), lambda i: (0, piece))),
            ]

        def up_products(piece):
            step_u = ff // split
            first_u, first_n = ff // 2 // step_u, (ff // 2 + ff) // tokens
            right = pl.BlockSpec((tokens, step_u), lambda i: (0, first_u + i))
            return [
                (normed, pl.BlockSpec((tokens, tokens), lambda i: (piece, 0))),
                (pack_got, pl.BlockSpec((tokens, tokens), lambda i: (0, first_n + piece))),
                (pack, right),
                (pack_got, right),
            ]

        def d_made(cols, kind):
            return ((width, cols), kind, by_step((width // split, cols), 0))

        def u_made(rows_u, kind):
            return ((rows_u, ff), kind, by_step((rows_u, ff // split), 1))

        def out_products(piece):
            first_t = heads * wide // tokens
            right = by_step((tokens, heads * wide // split), 1)
            return [
                (turned, pl.BlockSpec((tokens, tokens), lambda i: (piece, 0))),
                (mixed_got, pl.BlockSpec((tokens, tokens), lambda i: (0, first_t + piece))),
                (mixed, right),
                (mixed_got, right),
            ]

        def out_made(rows_o, kind):
            return ((rows_o, heads * wide), kind, by_step((rows_o, heads * wide // split), 1))

        span_d = heads // 2 * wall_rows

        def head_products(piece):
            half = width // 4
            turned_spec = pl.BlockSpec((1, half, seqs * rows), lambda i: (0, piece, 0))
            got_spec = pl.BlockSpec((half, seqs * rows), lambda i: (piece, 0))
            right = by_step((seqs * rows, wall_rows), 1)
            return [
                (ctx_a, turned_spec), (ctx_a_got, got_spec), (ctx_b, turned_spec), (ctx_b_got, got_spec),
                (deltas[0], right), (deltas_a, right), (deltas[1], right), (deltas_b, right),
            ]

        def head_made(count, kind):
            return ((count, span_d), kind, by_step((count, wall_rows), 1))

        def then(*after):
            return [(a, unread) for a in after]

        def stage(kernel, steps, operands, after, outs, vmem=vmem_less):
            name = kernel.__name__
            return call(kernel, steps, operands + then(*after), outs, vmem=vmem, flops=cost.get(name, 1))

        def step_fold(kernel, keep, got, axis, *after):
            shape = tuple(n // 2 if a == axis else n for a, n in enumerate(keep.shape))
            return stage(kernel, 1, [given(keep), given(got)], after, [made(shape, low), made(shape, full)])

        grad_att = lax.all_to_all(grad_out.reshape(cycle, share, lanes), "seq", 0, 0)
        (send_u,) = stage(send_up, split, up_products(1), [grad_out], [u_made(width // 4, low)], vmem_plane)
        got_u = halver.swap(send_u, up_bits[1])
        back = attended_back(grad_att, send_u)
        returned = lax.all_to_all(back, "seq", 0, 0)
        (send_d,) = stage(send_down, split, down_products(1), [back], [d_made(ff // 4, low)], vmem_plane)
        got_d = halver.swap(send_d, down_bits[1])
        (send_o,) = stage(outer_send, split, out_products(1), [send_d], [out_made(width // 4, low)], vmem_plane)
        got_o = halver.swap(send_o, out_bits[1])
        deltas = head_deltas(returned, grad_out, send_o)
        deltas_a, deltas_b = halver.swap(deltas[0], core[0]), halver.swap(deltas[1], core[0])
        send_o, keep_o = stage(
            outer_split,
            split,
            out_products(0) + [(got_o, by_step((width // 4, heads * wide // split), 1))],
            [deltas[0]],
            [out_made(width // 8, low), out_made(width // 8, full)],
            vmem_big,
        )
        got_o = halver.swap(send_o, out_bits[2])
        send_a, send_b = stage(
            heads_send, heads // 2, head_products(1), [send_o], [head_made(width // 4, low)] * 2,
            vmem_big,
        )
        got_a, got_b = halver.swap(send_a, qkv_bits[0][1]), halver.swap(send_b, qkv_bits[1][1])
        send_u, keep_u = stage(
            cross_up,
            split,
            up_products(0) + [(got_u, by_step((width // 4, ff // split), 1))],
            [send_a],
            [u_made(width // 8, low), u_made(width // 8, full)],
            vmem_big,
        )
        got_u = halver.swap(send_u, up_bits[2])
        send_d, keep_d = stage(
            cross_down,
            split,
            down_products(0) + [(got_d, by_step((width // split, ff // 4), 0))],
            [send_u],
            [d_made(ff // 8, low), d_made(ff // 8, full)],
            vmem_big,
        )
        got_d = halver.swap(send_d, down_bits[2])
        input_grad = finished(deltas, send_d)
        send_a, send_b, keep_a, keep_b = stage(
            heads_split,
            heads // 2,
            head_products(0)
            + [(got_a, by_step((width // 4, wall_rows), 1)), (got_b, by_step((width // 4, wall_rows), 1))],
            [input_grad],
            [head_made(width // 8, low)] * 2 + [head_made(width // 8, full)] * 2,
            vmem_big,
        )
        got_a, got_b = halver.swap(send_a, qkv_bits[0][2]), halver.swap(send_b, qkv_bits[1][2])
        send_u, keep_u = step_fold(fold, keep_u, got_u, 0, send_a)
        got_u = halver.swap(send_u, up_bits[3])
        send_d, keep_d = step_fold(fold_lanes, keep_d, got_d, 1, send_u)
        got_d = halver.swap(send_d, down_bits[3])
        send_o, keep_o = step_fold(fold, keep_o, got_o, 0, send_d)
        got_o = halver.swap(send_o, out_bits[3])
        a_shape = (width // 16, span_d)
        send_a, send_b, keep_a, keep_b = stage(
            heads_third,
            1,
            [given(a) for a in (keep_a, keep_b, got_a, got_b)],
            [send_o],
            [made(a_shape, low)] * 2 + [made(a_shape, full)] * 2,
        )
        got_a, got_b = halver.swap(send_a, qkv_bits[0][3]), halver.swap(send_b, qkv_bits[1][3])
        send_u, keep_u = step_fold(fold, keep_u, got_u, 0, send_a)
        got_u = halver.swap(send_u, up_bits[4])
        send_d, keep_d = step_fold(fold_lanes, keep_d, got_d, 1, send_u)
        got_d = halver.swap(send_d, down_bits[4])
        h_shape = (own, 2 * span_d + heads * wide)
        send_h, keep_h = stage(
            heads_join,
            1,
            [given(a) for a in (keep_a, keep_b, keep_o, got_a, got_b, got_o)],
            [send_d],
            [made(h_shape, low), made(h_shape, full)],
        )
        got_h = halver.swap(send_h, chip_z[1])
        down_grad, up_grad, norm2_grad = stage(
            end_feed,
            1,
            [given(a) for a in (keep_d, got_d, keep_u, got_u, up_own, gain_rows[:, 1:2])],
            [send_h],
            [made((lanes, width), full), made((own, ff), full), made((1, own), full)],
        )
        norm2_grad = norm2_grad.reshape(own)
        flat = [heads * size, heads * size, heads * span, 2 * heads * experts, heads * span]
        query_grad, key_grad, value_grad, router_grad, outproj_grad, norm1_grad = call(
            functools.partial(assemble, d=d),
            1,
            [given(a) for a in (keep_h, got_h, wall_own, gain_rows[:, 0:1])] + then(up_grad),
            [made((own, cols), full) for cols in flat] + [made((1, own), full)],
            vmem=vmem_less,
        )
        norm1_grad = norm1_grad.reshape(own)
        outproj_grad = outproj_grad.T
    else:
        act = act.reshape(tokens, blocks, -1)
        act = jnp.take(act, halver.order(down_bits) ^ halver.me, axis=1).reshape(tokens, -1)

        def down_product(lo, hi):
            quarter = ff // 4
            return dot_nn(grad_ffn_t, act[:, lo * quarter : hi * quarter])

        up_product = row_product(rows_by(normed, halver.order(up_bits)), pack)
        out_product = row_product(rows_by(grad_branch, halver.order(out_bits)), mixed)
        grad_att = lax.all_to_all(grad_out.reshape(cycle, share, lanes), "seq", 0, 0)
        back = attended_back(grad_att)
        returned = lax.all_to_all(back, "seq", 0, 0)
        deltas = head_deltas(returned, grad_out)
        input_grad = finished(deltas)
        down_grad = reduced(halver, down_product, down_bits, 1).T
        up_grad = reduced(halver, up_product, up_bits, 0)
        outproj_grad = reduced(halver, out_product, out_bits, 0)
        outproj_grad = outproj_grad.reshape(own, heads * experts, lanes)[:, :, :size].reshape(own, -1).T
        qkv_left = rows_by(ctx.reshape(seqs * rows, width), halver.order(qkv_bits[0]))
        qkv_product = row_product(qkv_left, jnp.concatenate(deltas, axis=1))
        by_head = reduced(halver, qkv_product, qkv_bits[0], 0).reshape(own, heads, 2 + experts, lanes)
        query_grad = by_head[:, :, 0, :size].reshape(own, -1)
        key_grad = by_head[:, :, 1, :size].reshape(own, -1)
        value_grad = by_head[:, :, 2:, :size].reshape(own, -1)
        router_grad = jnp.concatenate(
            [by_head[:, :, 0, size + i * experts : size + (i + 1) * experts].reshape(own, -1) for i in range(2)], axis=1
        )

        def own_rows(array):
            return lax.dynamic_slice_in_dim(array, halver.me * own, own, axis=0).astype(full)

        norm1_grad = (
            jnp.sum(own_rows(query_weight) * query_grad, axis=1)
            + jnp.sum(own_rows(key_weight) * key_grad, axis=1)
            + jnp.sum(own_rows(value_weight) * value_grad, axis=1)
            + jnp.sum(own_rows(router_weight) * router_grad, axis=1)
        ) / gain_rows[:, 0]
        norm2_grad = jnp.sum(own_rows(up_weight) * up_grad, axis=1) / gain_rows[:, 1]
    return (
        output, input_grad, norm1_grad, norm2_grad, query_grad, key_grad, value_grad, router_grad,
        outproj_grad, up_grad, down_grad,
    )


def solution(mesh):
    token = P("batch", "seq", None)
    routes = P("batch", "seq", None, None)
    spread = ("seq", "batch")
    return jax.shard_map(
        local,
        mesh=mesh,
        in_specs=(token, token, token, P("batch"), routes, routes, routes) + (P(),) * 9,
        out_specs=(
            token, token, P(spread), P(spread), P(spread, None), P(spread, None), P(spread, None), P(spread, None),
            P(None, spread), P(spread, None), P(spread, None),
        ),
        check_vma=False,
    )
```

```python
import collections
import functools

import jax
import jax.numpy as jnp
import numpy as np
from jax import lax
from jax.experimental import pallas as pl
from jax.experimental.pallas import tpu as pltpu
from jax.sharding import PartitionSpec as P

epsilon = 1e-05
neg_large = -1e30
slope_base = 0.5
log2_e = 1.4426950408889634
lanes = 128
low = jnp.bfloat16
full = jnp.float32
vmem_bytes = 56 << 20
vmem_less = 24 << 20
cost = {'heads_split': 4000000000, 'heads_third': 4000000000, 'heads_last': 4000000000, 'cross_down': 2000000000, 'end_feed': 6000000000, 'assemble': 3000000000}
vmem_back = 56 << 20
vmem_finish = 56 << 20
vmem_big = 56 << 20
vmem_attend = 56 << 20
vmem_end = 56 << 20
vmem_delta = 56 << 20
vmem_plane = 56 << 20

names = ["seqs", "seg", "mem", "rows", "heads", "size"]
names += ["experts", "parts", "share", "cycle", "width", "group"]
Dims = collections.namedtuple("Dims", names)


def dot_nn(left, right):
    return lax.dot_general(left, right, (((1,), (0,)), ((), ())), preferred_element_type=full)


def dot_nt(left, right):
    return lax.dot_general(left, right, (((1,), (1,)), ((), ())), preferred_element_type=full)


def dot_tn(left, right):
    return lax.dot_general(left, right, (((0,), (0,)), ((), ())), preferred_element_type=full)


def norm_parts(values):
    centred = values - jnp.mean(values, axis=-1, keepdims=True)
    spread = jnp.mean(centred * centred, axis=-1, keepdims=True)
    inverse = lax.rsqrt(spread + epsilon)
    return centred * inverse, inverse


def norm_back(grad, hat, inverse, gain_row):
    scaled = grad * gain_row
    along = jnp.mean(scaled * hat, axis=-1, keepdims=True)
    return inverse * (scaled - jnp.mean(scaled, axis=-1, keepdims=True) - hat * along)


smem = pl.BlockSpec(memory_space=pltpu.SMEM)
whole = pl.BlockSpec(memory_space=pltpu.VMEM)
unread = pl.BlockSpec(memory_space=pl.ANY)


def by_step(shape, axis):
    return pl.BlockSpec(shape, lambda i: tuple(i if a == axis else 0 for a in range(len(shape))))


def at_all(shape):
    return pl.BlockSpec(shape, lambda *i: (0,) * len(shape))


def call(kernel, steps, operands, outs, scratch=(), vmem=vmem_bytes, flops=1):
    return pl.pallas_call(
        kernel,
        grid=(steps,),
        out_shape=[jax.ShapeDtypeStruct(shape, kind) for shape, kind, _ in outs],
        in_specs=[spec for _, spec in operands],
        out_specs=[spec for _, _, spec in outs],
        scratch_shapes=list(scratch),
        compiler_params=pltpu.CompilerParams(
            vmem_limit_bytes=vmem, dimension_semantics=("arbitrary",)
        ),
        cost_estimate=pl.CostEstimate(flops=flops, bytes_accessed=1, transcendentals=0),
    )(*[a for a, _ in operands])


def picks(routes, experts):
    slots, tokens = routes.shape
    wide = jnp.concatenate([routes.astype(full), jnp.zeros((8 - slots, tokens), full)], axis=0)
    columns = wide.T
    expert = lax.broadcasted_iota(jnp.int32, (tokens, experts), 1).astype(full)
    total = jnp.zeros((tokens, experts), full)
    for slot in range(slots):
        total = total + (columns[:, slot : slot + 1] == expert).astype(full)
    return total


def fill_wall(wall_ref, wq_ref, wk_ref, wv_ref, wr_ref, d):
    size, experts = d.size, d.experts
    blank = jnp.zeros((lanes - size, d.width), low)
    wall_ref[0:size] = wq_ref[...]
    router = wr_ref[...]
    count = router.shape[0] // 2
    for h in range(d.heads):

        @pl.when(pl.program_id(0) == h)
        def _():
            mine = [router[at + h * experts : at + (h + 1) * experts] for at in (0, count)]
            wall_ref[size:lanes] = jnp.concatenate(mine + [blank[2 * experts :]], axis=0)

    wall_ref[lanes : lanes + size] = wk_ref[...]
    wall_ref[lanes + size : 2 * lanes] = blank
    for e in range(experts):
        first = (2 + e) * lanes
        wall_ref[first : first + size] = wv_ref[e * size : (e + 1) * size]
        wall_ref[first + size : first + lanes] = blank


def prepare(scal_ref, ctx_ref, wq_ref, wk_ref, wv_ref, wr_ref, wo_ref, wall_ref, exp_ref, out_ref, own_ref, d=None):
    fill_wall(wall_ref.at[0], wq_ref, wk_ref, wv_ref, wr_ref, d)
    ctx = ctx_ref[...].reshape(-1, d.width)
    exp_ref[0] = dot_nt(ctx, wall_ref[0, 2 * lanes :]).astype(low)
    for e in range(d.experts):
        out_ref[0, e * lanes : e * lanes + d.size] = wo_ref[e * d.size : (e + 1) * d.size]
        out_ref[0, e * lanes + d.size : (e + 1) * lanes] = jnp.zeros((lanes - d.size, d.width), low)
    rows = own_ref.shape[1]
    if lanes % rows == 0:
        first = scal_ref[3] * rows
        column = pl.ds(pl.multiple_of(lax.div(first, lanes) * lanes, lanes), lanes)
        turned = wall_ref[0, :, column].T
        for at in range(0, lanes, rows):

            @pl.when(lax.rem(first, lanes) == at)
            def _():
                own_ref[0] = turned[at : at + rows]


def project(
    x_ref, m_ref, vr_ref, mr_ref, or_ref, gain_ref, wq_ref, wk_ref, wv_ref, wr_ref,
    pay_ref, ctx_ref, vgate_ref, ogate_ref, wall_ref, held_ref, d=None
):
    size, experts = d.size, d.experts
    spare = lanes - size

    @pl.when(pl.program_id(0) == 0)
    def _():
        for s in range(d.seqs):
            block = jnp.concatenate([m_ref[s], x_ref[s]], axis=0).astype(full)
            hat, _ = norm_parts(block)
            block_low = (hat * gain_ref[...]).astype(low)
            held_ref[s * d.rows : (s + 1) * d.rows] = block_low
            ctx_ref[s] = block_low

    fill_wall(wall_ref, wq_ref, wk_ref, wv_ref, wr_ref, d)
    ctx = held_ref[...]
    every = dot_nt(ctx, wall_ref[...])
    query = every[:, 0:lanes]
    sig = jax.nn.sigmoid(query[:, size : size + 2 * experts])
    pick = []
    out_pick = []
    out_sig = []
    for s in range(d.seqs):
        pick.append(picks(mr_ref[s, 0], experts))
        pick.append(picks(vr_ref[s, 0], experts))
        out_pick.append(picks(or_ref[s, 0], experts))
        out_sig.append(sig[s * d.rows + d.mem : (s + 1) * d.rows, experts:])
    gate = sig[:, :experts] * jnp.concatenate(pick, axis=0)
    vgate_ref[0] = gate
    ogate_ref[0] = jnp.concatenate(out_sig, axis=0) * jnp.concatenate(out_pick, axis=0)
    count = d.seqs * d.rows
    value = jnp.zeros((count, lanes), full)
    for e in range(experts):
        value = value + gate[:, e : e + 1] * every[:, (2 + e) * lanes : (3 + e) * lanes]
    lane_at = lax.broadcasted_iota(jnp.int32, (count, lanes), 1)
    query = jnp.where(lane_at < size, query, 0.0).astype(low)
    keys = every[:, lanes : 2 * lanes].astype(low)
    value = value.astype(low)
    for s in range(d.seqs):
        mine = slice(s * d.rows, (s + 1) * d.rows)
        for p in range(d.parts):
            first = s * d.rows + d.mem + p * d.share
            pay_ref[p, 0, s] = payload(keys[mine], value[mine], query[first : first + d.share], d)


def lane_sums(product, experts):
    slot = lax.broadcasted_iota(jnp.int32, (experts * lanes, lanes), 0) // lanes
    target = lax.broadcasted_iota(jnp.int32, (experts * lanes, lanes), 1)
    ones = (slot == target).astype(full).astype(low)
    high = product.astype(low)
    rest = (product - high.astype(full)).astype(low)
    return (dot_nn(high, ones) + dot_nn(rest, ones))[:, :experts]


def turn_context(scal_ref, ctx_ref, *refs, bits=None):
    first_ref, second_ref = refs[-2:]
    value = ctx_ref[...].reshape(-1, ctx_ref.shape[-1])
    turn(value, first_ref, scal_ref[3], bits[0])
    turn(value, second_ref, scal_ref[3], bits[1])


def folded_in(d):
    half = d.share // 2
    return 2 * d.rows == 6 * half and 7 * (lanes - d.size) == d.size


def payload_rows(d):
    return 2 * d.rows + (d.share // 2 if folded_in(d) else d.share)


def payload(keys, values, queries, d):
    size, half = d.size, d.share // 2
    if not folded_in(d):
        return jnp.concatenate([keys, values, queries], axis=0)
    rows = jnp.concatenate([keys, values, queries[:half]], axis=0)
    step = lanes - size
    spare = [queries[half:, at : at + step] for at in range(0, size, step)]
    return jnp.concatenate([rows[:, :size], jnp.concatenate(spare, axis=0)], axis=1)


def payload_queries(block, d):
    size, half = d.size, d.share // 2
    blank = jnp.zeros((d.share, lanes - size), block.dtype)
    if not folded_in(d):
        return jnp.concatenate([block[2 * d.rows :, :size], blank], axis=1)
    rest = jnp.concatenate([block[at * half : (at + 1) * half, size:] for at in range(7)], axis=1)
    return jnp.concatenate([jnp.concatenate([block[2 * d.rows :, :size], rest], axis=0), blank], axis=1)


def key_value(pay_ref, k_ref, v_ref, d):
    for j in range(d.cycle):
        k_ref[j * d.mem : (j + 1) * d.mem] = pay_ref[j, 0 : d.mem]
        v_ref[j * d.mem : (j + 1) * d.mem] = pay_ref[j, d.rows : d.rows + d.mem]
        base = d.cycle * d.mem + j * d.seg
        k_ref[base : base + d.seg] = pay_ref[j, d.mem : d.rows]
        v_ref[base : base + d.seg] = pay_ref[j, d.rows + d.mem : 2 * d.rows]


def query_block(pay_ref, first, d):
    found = [payload_queries(pay_ref[j], d) for j in range(first, first + d.group)]
    return jnp.concatenate(found, axis=0)


def attend(scal_ref, pay_ref, *refs, d=None):
    att_ref, keep_ref, lse_ref, k_ref, v_ref = refs[-5:]
    share, group = d.share, d.group
    mem_len = d.cycle * d.mem
    ctx_len = d.cycle * d.rows
    length, head, part = scal_ref[0], scal_ref[1], scal_ref[2]
    key_value(pay_ref, k_ref, v_ref, d)
    slope = slope_base * (head + 1).astype(full) / ctx_len * log2_e
    place = lax.broadcasted_iota(jnp.int32, (1, ctx_len), 1) - mem_len
    bias = jnp.where(place < length, place.astype(full) * slope, neg_large)
    q_rows = group * share
    for first in range(0, d.cycle, group):
        width = mem_len + (first + group) * d.seg
        cut = width - group * d.seg
        query = query_block(pay_ref, first, d)
        scores = dot_nt(query, k_ref[0:width]) * (d.size**-0.5 * log2_e) + bias[:, :width]
        row = lax.broadcasted_iota(jnp.int32, (q_rows, group * d.seg), 0)
        col = lax.broadcasted_iota(jnp.int32, (q_rows, group * d.seg), 1)
        row_place = (row // share) * d.seg + part * share + row % share
        tail = jnp.where(col <= row_place, scores[:, cut:], neg_large)
        scores = jnp.concatenate([scores[:, :cut], tail], axis=1)
        top = jnp.max(scores, axis=1, keepdims=True)
        weights = jnp.exp2(scores - top)
        total = jnp.sum(weights, axis=1, keepdims=True)
        attended = dot_nn(weights.astype(low), v_ref[0:width]) / total
        keep_ref[first * share : first * share + q_rows] = attended
        lse_ref[first * share : first * share + q_rows] = top + jnp.log2(total)
        for j in range(group):
            att_ref[first + j] = attended[j * share : (j + 1) * share].astype(low)


def attend_back(
    scal_ref, pay_ref, keep_ref, lse_ref, grad_ref, *refs, d=None
):
    out_ref, k_ref, v_ref, dk_ref, dv_ref = refs[-5:]
    share, group, size = d.share, d.group, d.size
    mem_len = d.cycle * d.mem
    ctx_len = d.cycle * d.rows
    length, head, part = scal_ref[0], scal_ref[1], scal_ref[2]
    key_value(pay_ref, k_ref, v_ref, d)
    scale = size**-0.5
    slope = slope_base * (head + 1).astype(full) / ctx_len * log2_e
    place = lax.broadcasted_iota(jnp.int32, (ctx_len, lanes), 0) - mem_len
    bias = jnp.where(place < length, place.astype(full) * slope, neg_large)[:, 0:1]
    dk_ref[...] = jnp.zeros_like(dk_ref)
    dv_ref[...] = jnp.zeros_like(dv_ref)
    q_rows = group * share
    lane_at = lax.broadcasted_iota(jnp.int32, (q_rows, lanes), 1)
    query_grads = []
    for first in range(0, d.cycle, group):
        width = mem_len + (first + group) * d.seg
        cut = width - group * d.seg
        begin = first * share
        query = query_block(pay_ref, first, d)
        raw = jnp.concatenate([grad_ref[j] for j in range(first, first + group)], axis=0)
        grad = jnp.where(lane_at < size, raw, jnp.zeros_like(raw))
        kept = keep_ref[begin : begin + q_rows]
        delta = jnp.sum(jnp.where(lane_at < size, grad.astype(full) * kept, 0.0), axis=1, keepdims=True)
        both = jnp.concatenate(
            [
                jnp.broadcast_to(delta, (q_rows, lanes)),
                jnp.broadcast_to(lse_ref[begin : begin + q_rows], (q_rows, lanes)),
            ],
            axis=1,
        ).T
        delta_row = both[0:1]
        lse_row = both[lanes : lanes + 1]
        scores = dot_nt(k_ref[0:width], query) * (scale * log2_e) + bias[:width]
        weights = jnp.exp2(scores - lse_row)
        row = lax.broadcasted_iota(jnp.int32, (group * d.seg, q_rows), 0)
        col = lax.broadcasted_iota(jnp.int32, (group * d.seg, q_rows), 1)
        col_place = (col // share) * d.seg + part * share + col % share
        weights = jnp.concatenate([weights[:cut], jnp.where(row <= col_place, weights[cut:], 0.0)], axis=0)
        grad_weights = dot_nt(v_ref[0:width], grad)
        grad_scores = (weights * (grad_weights - delta_row)).astype(low)
        dk_ref[0:width] += dot_nn(grad_scores, query)
        dv_ref[0:width] += dot_nn(weights.astype(low), grad)
        dq = (dot_tn(grad_scores, k_ref[0:width]) * scale).astype(low)
        query_grads.append(dq)
    for j in range(d.cycle):
        base = mem_len + j * d.seg
        dk = jnp.concatenate([dk_ref[j * d.mem : (j + 1) * d.mem], dk_ref[base : base + d.seg]], axis=0)
        dv = jnp.concatenate([dv_ref[j * d.mem : (j + 1) * d.mem], dv_ref[base : base + d.seg]], axis=0)
        dq = query_grads[j // group][j % group * share : (j % group + 1) * share]
        out_ref[j] = payload((dk * scale).astype(low), dv.astype(low), dq, d)


def place_of(mask, bits):
    place = jnp.int32(0)
    for at, bit in enumerate(bits):
        place = place + ((mask >> bit) & 1) * (1 << (len(bits) - 1 - at))
    return place


def turn(value, out_ref, me, bits):
    turned = value.T
    count = 1 << len(bits)
    own = turned.shape[0] // count
    for block in range(count):
        place = place_of(block ^ me, bits)
        side = lax.div(place, count // 2)
        inside = lax.rem(place, count // 2)
        out_ref[side, pl.ds(pl.multiple_of(inside * own, own), own), :] = turned[block * own : (block + 1) * own]


def beside(turn_ref, pack_ref):
    half, tokens = turn_ref.shape[1] // 2, turn_ref.shape[2]
    first = pack_ref.shape[1] - 2 * tokens
    pack_ref[:, first : first + tokens] = turn_ref[1, 0:half]
    pack_ref[:, first + tokens :] = turn_ref[1, half:]


def feed(
    scal_ref, att_ref, ogate_ref, x_ref, gain_ref, live_ref, gf_ref, wo_ref, up_ref, down_ref,
    mix_hbm, act_hbm, pack_hbm, out_ref, resid_ref, branch_ref, normed_ref, turned_ref, gatt_ref,
    sum_ref, ffn_ref, back_ref, held_ref, turn_ref, out_mix_ref, act_ref, pack_ref, copied, d=None, bits=None
):
    step = pl.program_id(0)
    together = wo_ref.shape[0]
    steps_h = d.heads // together
    last = pl.num_programs(0) - 1 - steps_h
    experts = d.experts
    me = scal_ref[3]

    @pl.when(step == 0)
    def _():
        for s in range(d.seqs):
            sum_ref[s * d.seg : (s + 1) * d.seg] = x_ref[s].astype(full)
        ffn_ref[...] = jnp.zeros_like(ffn_ref)
        back_ref[...] = jnp.zeros_like(back_ref)

    @pl.when(step < steps_h)
    def _():
        total = sum_ref[...]
        for k in range(together):
            found = [att_ref[p, k, s] for s in range(d.seqs) for p in range(d.parts)]
            att = jnp.concatenate(found, axis=0).astype(full)
            gate = ogate_ref[k]
            mixed = jnp.concatenate([(gate[:, e : e + 1] * att).astype(low) for e in range(experts)], axis=1)
            wide = mixed.shape[1]
            out_mix_ref[:, pl.ds(pl.multiple_of((step * together + k) * wide, lanes), wide)] = mixed
            total = total + dot_nn(mixed, wo_ref[k])
        sum_ref[...] = total

    @pl.when(step == steps_h - 1)
    def _():
        hat, _ = norm_parts(sum_ref[...])
        normed = (hat * gain_ref[...]).astype(low)
        held_ref[...] = normed
        if bits is None:
            normed_ref[...] = normed
        else:
            turn(normed, turn_ref, me, bits[1])
            normed_ref[...] = turn_ref[0]
            beside(turn_ref, pack_ref)

    @pl.when((step >= steps_h) & (step <= last))
    def _():
        coeff = 0.7978845608028654
        held = held_ref[...]
        outer_grad = gf_ref[...]
        acts = []
        grads = []
        part = up_ref.shape[1] // 4
        for c in range(4):
            mine = slice(c * part, (c + 1) * part)
            value = dot_nn(held, up_ref[:, mine])
            grad_act = dot_nt(outer_grad, down_ref[mine, :])
            square = value * value
            wave = jnp.tanh(value * (coeff + (0.044715 * coeff) * square))
            rise = 0.5 + 0.5 * wave
            acts.append((value * rise).astype(low))
            slope = rise + (0.5 * value) * (1.0 - wave * wave) * (coeff + (3 * 0.044715 * coeff) * square)
            grads.append((grad_act * slope).astype(low))
        act = jnp.concatenate(acts, axis=1)
        gu = jnp.concatenate(grads, axis=1)
        ffn_ref[...] += dot_nn(act, down_ref[...])
        back_ref[...] += dot_nt(gu, up_ref[...])
        block = step - steps_h
        span = act.shape[1]
        if bits is None:
            pack_ref[:, pl.ds(pl.multiple_of(block * span, span), span)] = gu
            act_ref[:, pl.ds(pl.multiple_of(block * span, span), span)] = act
        else:
            half = 1 << (len(bits[0]) - 1)
            own = act_ref.shape[1] // half
            pack_ref[:, pl.ds(pl.multiple_of(half * own + block * span, lanes), span)] = gu
            for b in range(span // own):
                piece = act[:, b * own : (b + 1) * own]
                place = place_of((block * (span // own) + b) ^ me, bits[0])
                inside = pl.ds(pl.multiple_of(lax.rem(place, half) * own, own), own)

                @pl.when(place < half)
                def _():
                    act_ref[:, inside] = piece

                @pl.when(place >= half)
                def _():
                    pack_ref[:, inside] = piece

    @pl.when(step == last)
    def _():
        residual = sum_ref[...]
        out_ref[...] = ((residual + ffn_ref[...]) * live_ref[...]).astype(low)
        hat, inverse = norm_parts(residual)
        grad = gf_ref[...].astype(full) + norm_back(back_ref[...], hat, inverse, gain_ref[...])
        resid_ref[...] = grad
        branch = grad.astype(low)
        branch_ref[...] = branch
        if bits is None:
            turned_ref[...] = branch
        else:
            turn(branch, turn_ref, me, bits[2])
            turned_ref[...] = turn_ref[0]
            beside(turn_ref, out_mix_ref)

    moves = [
        pltpu.make_async_copy(held, result, copied.at[at])
        for at, (held, result) in enumerate(((out_mix_ref, mix_hbm), (act_ref, act_hbm), (pack_ref, pack_hbm)))
    ]

    @pl.when(step == last)
    def _():
        for move in moves:
            move.start()

    @pl.when(step > last)
    def _():
        for k in range(together):
            unmix(branch_ref, att_ref, ogate_ref, wo_ref, gatt_ref, k, d)

    @pl.when(step == pl.num_programs(0) - 1)
    def _():
        for move in moves:
            move.wait()


def unmix(branch_ref, att_ref, ogate_ref, wo_ref, out_ref, k, d):
    size, experts = d.size, d.experts
    tokens = d.seqs * d.seg
    grad_mixed = dot_nt(branch_ref[...], wo_ref[k])
    found = [att_ref[p, k, s] for s in range(d.seqs) for p in range(d.parts)]
    att = jnp.concatenate(found, axis=0).astype(full)
    gate = ogate_ref[k]
    grad = jnp.zeros((tokens, lanes), full)
    product = []
    for e in range(experts):
        piece = grad_mixed[:, e * lanes : (e + 1) * lanes]
        grad = grad + gate[:, e : e + 1] * piece
        product.append(piece * att)
    logit = lane_sums(jnp.concatenate(product, axis=1), experts) * gate * (1.0 - gate)
    joined = jnp.concatenate(
        [grad[:, :size].astype(low), logit.astype(low), jnp.zeros((tokens, lanes - size - experts), low)], axis=1
    )
    for s in range(d.seqs):
        for p in range(d.parts):
            first = s * d.seg + p * d.share
            out_ref[p, k, s] = joined[first : first + d.share]


def make_deltas(back_ref, grad_ref, vgate_ref, exp_ref, *refs, d=None):
    size, experts = d.size, d.experts
    q_found, k_found, v_found, lo_found = [], [], [], []
    for s in range(d.seqs):
        kv = back_ref[0, 0, s, 0 : 2 * d.rows]
        if d.parts > 1:
            kv = kv.astype(full)
            for p in range(1, d.parts):
                kv = kv + back_ref[p, 0, s, 0 : 2 * d.rows].astype(full)
            kv = kv.astype(low)
        k_found.append(kv[: d.rows])
        v_found.append(kv[d.rows :])
        q_found.append(jnp.zeros((d.mem, lanes), low))
        lo_found.append(jnp.zeros((d.mem, lanes), low))
        for p in range(d.parts):
            q_found.append(payload_queries(back_ref[p, 0, s], d))
            lo_found.append(grad_ref[p, 0, s])
    query = jnp.concatenate(q_found, axis=0)
    keys = jnp.concatenate(k_found, axis=0)
    values = jnp.concatenate(v_found, axis=0)
    out_logit = jnp.concatenate(lo_found, axis=0)[:, size : size + experts]
    gate = vgate_ref[0]
    lane_at = lax.broadcasted_iota(jnp.int32, (d.seqs * d.rows, lanes), 1)
    value = jnp.where(lane_at < size, values.astype(full), 0.0)
    keys = jnp.where(lane_at < size, keys, jnp.zeros_like(keys))
    product = jnp.concatenate(
        [value * exp_ref[0, :, e * lanes : (e + 1) * lanes].astype(full) for e in range(experts)], axis=1
    )
    logit = (lane_sums(product, experts) * gate * (1.0 - gate)).astype(low)
    first = jnp.concatenate(
        [query[:, :size], logit, out_logit, jnp.zeros((d.seqs * d.rows, lanes - size - 2 * experts), low)], axis=1
    )
    step = pl.program_id(0)
    for at, delta_ref in enumerate(refs[-2:]):

        @pl.when(step // (d.heads // 2) == at)
        def _():
            delta_ref[:, 0:lanes] = first
            delta_ref[:, lanes : 2 * lanes] = keys
            for e in range(experts):
                delta_ref[:, (2 + e) * lanes : (3 + e) * lanes] = (gate[:, e : e + 1] * value).astype(low)


def finish(first_ref, second_ref, x_ref, gain_ref, resid_ref, wall_ref, *refs, d=None):
    out_ref, sum_ref = refs[-2:]
    step = pl.program_id(0)

    @pl.when(step == 0)
    def _():
        sum_ref[...] = jnp.zeros_like(sum_ref)

    for at, delta_ref in enumerate((first_ref, second_ref)):

        @pl.when(step // (d.heads // 2) == at)
        def _():
            rows = [delta_ref[s * d.rows + d.mem : (s + 1) * d.rows] for s in range(d.seqs)]
            sum_ref[...] += dot_nn(jnp.concatenate(rows, axis=0), wall_ref[0])

    @pl.when(step == pl.num_programs(0) - 1)
    def _():
        for s in range(d.seqs):
            hat, inverse = norm_parts(x_ref[s].astype(full))
            mine = slice(s * d.seg, (s + 1) * d.seg)
            out_ref[s] = resid_ref[mine] + norm_back(sum_ref[mine], hat, inverse, gain_ref[...])


def both(first, second, axis):
    return jnp.concatenate([first, second], axis=axis)


def send_down(gf_ref, act_ref, act_got_ref, *refs):
    refs[-1][...] = dot_nn(gf_ref[...], both(act_ref[...], act_got_ref[...], 0)).astype(low)


def send_up(left_ref, left_got_ref, gu_ref, gu_got_ref, *refs):
    left = both(left_ref[...], left_got_ref[...], 1)
    refs[-1][...] = dot_nn(left, both(gu_ref[...], gu_got_ref[...], 0)).astype(low)


def cross_down(gf_ref, act_ref, act_got_ref, new_ref, *refs):
    send_ref, keep_ref = refs[-2:]
    total = dot_nn(gf_ref[...], both(act_ref[...], act_got_ref[...], 0)) + new_ref[...].astype(full)
    half = total.shape[1] // 2
    keep_ref[...] = total[:, :half]
    send_ref[...] = total[:, half:].astype(low)


def cross_up(left_ref, left_got_ref, gu_ref, gu_got_ref, new_ref, *refs):
    send_ref, keep_ref = refs[-2:]
    left = both(left_ref[...], left_got_ref[...], 1)
    total = dot_nn(left, both(gu_ref[...], gu_got_ref[...], 0)) + new_ref[...].astype(full)
    half = total.shape[0] // 2
    keep_ref[...] = total[:half]
    send_ref[...] = total[half:].astype(low)


def fold_lanes(keep_ref, got_ref, *refs):
    send_ref, left_ref = refs[-2:]
    total = keep_ref[...] + got_ref[...].astype(full)
    half = total.shape[1] // 2
    left_ref[...] = total[:, :half]
    send_ref[...] = total[:, half:].astype(low)


def end_feed(keep_d_ref, got_d_ref, keep_u_ref, got_u_ref, weight_ref, gain_ref, *refs):
    down_ref, up_ref, norm_ref = refs[-3:]
    down_ref[...] = (keep_d_ref[...] + got_d_ref[...].astype(full)).T
    total = keep_u_ref[...] + got_u_ref[...].astype(full)
    up_ref[...] = total
    along = jnp.sum(total * weight_ref[...].astype(full), axis=1, keepdims=True)
    norm_ref[...] = row_of(along / gain_ref[...])


def outer_send(left_ref, left_got_ref, right_ref, right_got_ref, *refs):
    left = both(left_ref[...], left_got_ref[...], 1)
    refs[-1][...] = dot_nn(left, both(right_ref[...], right_got_ref[...], 0)).astype(low)


def outer_split(left_ref, left_got_ref, right_ref, right_got_ref, new_ref, *refs):
    send_ref, keep_ref = refs[-2:]
    left = both(left_ref[...], left_got_ref[...], 1)
    total = dot_nn(left, both(right_ref[...], right_got_ref[...], 0)) + new_ref[...].astype(full)
    half = total.shape[0] // 2
    keep_ref[...] = total[:half]
    send_ref[...] = total[half:].astype(low)


def heads_send(a_ref, a_got_ref, b_ref, b_got_ref, da_ref, da_got_ref, db_ref, db_got_ref, *refs):
    a_out, b_out = refs[-2:]
    a_out[...] = dot_nn(both(a_ref[0], a_got_ref[...], 1), both(da_ref[...], da_got_ref[...], 0)).astype(low)
    b_out[...] = dot_nn(both(b_ref[0], b_got_ref[...], 1), both(db_ref[...], db_got_ref[...], 0)).astype(low)


def heads_split(
    a_ref, a_got_ref, b_ref, b_got_ref, da_ref, da_got_ref, db_ref, db_got_ref, new_a_ref, new_b_ref, *refs
):
    outs = refs[-4:]
    left = both(a_ref[0], a_got_ref[...], 1), both(b_ref[0], b_got_ref[...], 1)
    right = both(da_ref[...], da_got_ref[...], 0), both(db_ref[...], db_got_ref[...], 0)
    for at, new_ref in enumerate((new_a_ref, new_b_ref)):
        total = dot_nn(left[at], right[at]) + new_ref[...].astype(full)
        half = total.shape[0] // 2
        outs[2 + at][...] = total[:half]
        outs[at][...] = total[half:].astype(low)


def heads_third(keep_a_ref, keep_b_ref, got_a_ref, got_b_ref, *refs):
    outs = refs[-4:]
    for at, (keep_ref, got_ref) in enumerate(((keep_a_ref, got_a_ref), (keep_b_ref, got_b_ref))):
        half = keep_ref.shape[0] // 2
        outs[2 + at][...] = keep_ref[:half] + got_ref[:half].astype(full)
        outs[at][...] = (keep_ref[half:] + got_ref[half:].astype(full)).astype(low)


def heads_last(*refs):
    heads_third(*refs)


def fold(keep_ref, got_ref, *refs):
    send_ref, left_ref = refs[-2:]
    half = keep_ref.shape[0] // 2
    left_ref[...] = keep_ref[:half] + got_ref[:half].astype(full)
    send_ref[...] = (keep_ref[half:] + got_ref[half:].astype(full)).astype(low)


def row_of(column):
    n = column.shape[0]
    same = lax.broadcasted_iota(jnp.int32, (n, n), 0) == lax.broadcasted_iota(jnp.int32, (n, n), 1)
    return jnp.sum(jnp.where(same, column, 0.0), axis=0, keepdims=True)


def assemble_out(kept_ref, got_ref, *refs, d=None):
    total = kept_ref[...] + got_ref[...].astype(full)
    refs[-1][...] = jnp.concatenate(
        [total[:, at * lanes : at * lanes + d.size] for at in range(d.heads * d.experts)], axis=1
    )


def assemble(a_ref, got_a_ref, b_ref, got_b_ref, wall_ref, gain_ref, *refs, d=None):
    q_ref, k_ref, v_ref, r_ref, norm_ref = refs[-5:]
    size, experts = d.size, d.experts
    slots = 2 + experts

    def total(kept, got, first):
        here = slice(first * lanes, (first + 1) * lanes)
        return kept[:, here] + got[:, here].astype(full)

    half = d.heads // 2
    every = [[total(a_ref, got_a_ref, h * slots + at) for at in range(slots)] for h in range(half)]
    every += [[total(b_ref, got_b_ref, h * slots + at) for at in range(slots)] for h in range(half)]
    along = jnp.zeros(every[0][0].shape, full)
    for h in range(d.heads):
        for at in range(slots):
            along = along + every[h][at] * wall_ref[h, :, at * lanes : (at + 1) * lanes].astype(full)
    norm_ref[...] = row_of(jnp.sum(along, axis=1, keepdims=True) / gain_ref[...])
    q_ref[...] = jnp.concatenate([one[0][:, :size] for one in every], axis=1)
    k_ref[...] = jnp.concatenate([one[1][:, :size] for one in every], axis=1)
    v_ref[...] = jnp.concatenate([one[2 + e][:, :size] for one in every for e in range(experts)], axis=1)
    values = [one[0][:, size : size + experts] for one in every]
    outs = [one[0][:, size + experts : size + 2 * experts] for one in every]
    r_ref[...] = jnp.concatenate(values + outs, axis=1)


class Halver:
    def __init__(self):
        self.cycle = lax.axis_size("seq")
        self.width = lax.axis_size("batch")
        self.low_bits = self.width.bit_length() - 1
        self.high_bits = self.cycle.bit_length() - 1
        self.me = lax.axis_index("seq") * self.width + lax.axis_index("batch")

    def swap(self, value, bit):
        if bit < self.low_bits:
            axis, size, mask = "batch", self.width, 1 << bit
        else:
            axis, size, mask = "seq", self.cycle, 1 << (bit - self.low_bits)
        return lax.ppermute(value, axis, [(i, i ^ mask) for i in range(size)])

    def order(self, bits):
        count = len(bits)
        found = np.zeros(1 << count, np.int32)
        for place in range(1 << count):
            for at, bit in enumerate(bits):
                if place >> (count - 1 - at) & 1:
                    found[place] |= 1 << bit
        return found


def halve(value, axis):
    size = value.shape[axis] // 2
    return (
        lax.slice_in_dim(value, 0, size, axis=axis),
        lax.slice_in_dim(value, size, 2 * size, axis=axis),
    )


def reduced(halver, product, bits, axis):
    got = halver.swap(product(2, 4).astype(low), bits[0])
    got_keep, got_send = halve(got, axis)
    got = halver.swap((product(1, 2) + got_send.astype(full)).astype(low), bits[1])
    keep = product(0, 1) + got_keep.astype(full) + got.astype(full)
    for bit in bits[2:]:
        keep, send = halve(keep, axis)
        keep = keep + halver.swap(send.astype(low), bit).astype(full)
    return keep


def local(
    inputs, memory, cotangent, valid_len, value_routes, memory_routes, output_routes, norm1_gain, norm2_gain,
    query_weight, key_weight, value_weight, router_weight, output_weight, up_weight, down_weight
):
    seqs, seg, width = inputs.shape
    mem = memory.shape[1]
    rows = seg + mem
    heads = value_routes.shape[2]
    slots_count = value_routes.shape[3]
    qk_width = query_weight.shape[1]
    size = qk_width // heads
    experts = value_weight.shape[1] // qk_width
    span = experts * size
    ff = up_weight.shape[1]
    tokens = seqs * seg
    halver = Halver()
    cycle = halver.cycle
    parts = cycle // (seqs * heads)
    share = seg // parts
    d = Dims(seqs, seg, mem, rows, heads, size, experts, parts, share, cycle, width, 2)
    pay_rows = payload_rows(d)
    at = lax.axis_index("seq")
    my_seq = at % seqs
    my_head = at // seqs % heads
    my_part = at // (seqs * heads)
    my_length = lax.dynamic_index_in_dim(valid_len, my_seq, 0, keepdims=False)
    scal = jnp.stack([my_length, my_head, my_part, halver.me]).astype(jnp.int32)
    gain_one = norm1_gain.reshape(1, width)
    gain_two = norm2_gain.reshape(1, width)
    place = at * seg + jnp.arange(seg, dtype=jnp.int32)
    live = (place[None, :] < valid_len[:, None]).astype(full).reshape(tokens, 1)
    grad_ffn = (cotangent.reshape(tokens, width).astype(full) * live).astype(low)
    wq, wk, wv, wr = query_weight.T, key_weight.T, value_weight.T, router_weight.T
    v_routes = jnp.transpose(value_routes, (0, 2, 3, 1))
    m_routes = jnp.transpose(memory_routes, (0, 2, 3, 1))
    o_routes = jnp.transpose(output_routes, (0, 2, 3, 1))
    blocks = cycle * halver.width
    own = width // blocks
    wide = experts * lanes
    wall_rows = 2 * lanes + wide
    wall_shape = (heads, wall_rows, width)

    def routes_spec(count):
        return by_step((seqs, 1, slots_count, count), 1)

    def head_spec(*tail):
        return by_step((parts, 1, seqs) + tail, 1)

    def given(array):
        return (array, at_all(array.shape))

    def made(shape, kind):
        return (shape, kind, at_all(shape))

    pay, ctx, vgate, ogate = call(
        functools.partial(project, d=d),
        heads,
        [
            given(inputs),
            given(memory),
            (v_routes, routes_spec(seg)),
            (m_routes, routes_spec(mem)),
            (o_routes, routes_spec(seg)),
            given(gain_one),
            (wq, by_step((size, width), 0)),
            (wk, by_step((size, width), 0)),
            (wv, by_step((span, width), 0)),
            given(wr),
        ],
        [
            ((parts, heads, seqs, pay_rows, lanes), low, head_spec(pay_rows, lanes)),
            made((seqs, rows, width), low),
            ((heads, seqs * rows, experts), full, by_step((1, seqs * rows, experts), 0)),
            ((heads, tokens, experts), full, by_step((1, tokens, experts), 0)),
        ],
        scratch=[pltpu.VMEM(wall_shape[1:], low), pltpu.VMEM((seqs * rows, width), low)],
    )
    wall, expanded, wo, wall_own = call(
        functools.partial(prepare, d=d),
        heads,
        [
            (scal, smem),
            given(ctx),
            (wq, by_step((size, width), 0)),
            (wk, by_step((size, width), 0)),
            (wv, by_step((span, width), 0)),
            given(wr),
            (output_weight, by_step((span, width), 0)),
        ],
        [
            (wall_shape, low, by_step((1,) + wall_shape[1:], 0)),
            ((heads, seqs * rows, wide), low, by_step((1, seqs * rows, wide), 0)),
            ((heads, wide, width), low, by_step((1, wide, width), 0)),
            ((heads, own, wall_rows), low, by_step((1, own, wall_rows), 0)),
        ],
    )
    up_own = lax.dynamic_slice_in_dim(up_weight, halver.me * own, own, axis=0)
    bit_count = halver.low_bits + halver.high_bits
    low_b = list(range(halver.low_bits))
    high_b = list(range(halver.low_bits, bit_count))
    core, chip_y, chip_x, chip_z = low_b[:1], low_b[1:], high_b[:1], high_b[1:]
    down_bits = core + chip_x + chip_y + chip_z
    up_bits = core + chip_y + chip_z + chip_x
    out_bits = core + chip_z[:1] + chip_x + chip_y + chip_z[1:]
    fast = own == 32 and ff == blocks * lanes and len(chip_z) == 2 and len(chip_y) == 1

    qkv_bits = down_bits, core + chip_y + chip_z[:1] + chip_x + chip_z[1:]
    grad_ffn_t = grad_ffn.T
    after = [wo]
    if fast:
        turned_ctx = (2, width // 2, seqs * rows)
        ctx_a, ctx_b = call(
            functools.partial(turn_context, bits=qkv_bits),
            1,
            [(scal, smem), given(ctx), (wo, unread)],
            [made(turned_ctx, low), made(turned_ctx, low)],
        )
        grad_ffn_both = jnp.concatenate([grad_ffn_t, halver.swap(grad_ffn_t, core[0])], axis=1)
        ctx_a_got, ctx_b_got = halver.swap(ctx_a[1], core[0]), halver.swap(ctx_b[1], core[0])
        after += [grad_ffn_both, ctx_a_got, ctx_b_got]
    pay = lax.all_to_all(pay.reshape(cycle, pay_rows, lanes), "seq", 0, 0)
    att, kept, lse = call(
        functools.partial(attend, d=d),
        1,
        [(scal, smem), given(pay)] + [(a, unread) for a in after],
        [
            made((cycle, share, lanes), low),
            made((cycle * share, lanes), full),
            made((cycle * share, 1), full),
        ],
        scratch=[pltpu.VMEM((cycle * rows, lanes), low)] * 2,
        vmem=vmem_attend,
    )
    att = lax.all_to_all(att, "seq", 0, 0)
    steps, together = 4, 2
    steps_h = heads // together
    att_heads = att.reshape(parts, heads, seqs, share, lanes)

    def ff_block(i):
        return jnp.clip(i - steps_h, 0, steps - 1)

    def head_of(i):
        return jnp.where(i < steps_h + steps, jnp.minimum(i, steps_h - 1), i - steps_h - steps)

    def back_of(i):
        return jnp.maximum(i - steps_h - steps, 0)

    turned_shape = (width // 2, tokens) if fast else (tokens, width)
    act_shape = (tokens, ff // 2) if fast else (tokens, ff)
    pack_shape = (tokens, ff // 2 + ff + 2 * tokens) if fast else (tokens, ff)
    mix_shape = (tokens, heads * wide + 2 * tokens) if fast else (tokens, heads * wide)
    mixed, act, pack, output, grad_residual, grad_branch, normed, turned, grad_out = call(
        functools.partial(feed, d=d, bits=(tuple(down_bits), tuple(up_bits), tuple(out_bits)) if fast else None),
        2 * steps_h + steps,
        [
            (scal, smem),
            (att_heads, pl.BlockSpec((parts, together, seqs, share, lanes), lambda i: (0, head_of(i), 0, 0, 0))),
            (ogate, pl.BlockSpec((together, tokens, experts), lambda i: (head_of(i), 0, 0))),
            given(inputs),
            given(gain_two),
            given(live),
            given(grad_ffn),
            (wo, pl.BlockSpec((together, wide, width), lambda i: (head_of(i), 0, 0))),
            (up_weight, pl.BlockSpec((width, ff // steps), lambda i: (0, ff_block(i)))),
            (down_weight, pl.BlockSpec((ff // steps, width), lambda i: (ff_block(i), 0))),
        ],
        [
            (mix_shape, low, unread),
            (act_shape, low, unread),
            (pack_shape, low, unread),
            made((tokens, width), low),
            made((tokens, width), full),
            made((tokens, width), low),
            made(turned_shape, low),
            made(turned_shape, low),
            (
                (parts, heads, seqs, share, lanes),
                low,
                pl.BlockSpec((parts, together, seqs, share, lanes), lambda i: (0, back_of(i), 0, 0, 0)),
            ),
        ],
        scratch=[pltpu.VMEM((tokens, width), full)] * 3
        + [pltpu.VMEM((tokens, width), low), pltpu.VMEM((2, width // 2, tokens), low)]
        + [pltpu.VMEM(shape, low) for shape in (mix_shape, act_shape, pack_shape)]
        + [pltpu.SemaphoreType.DMA((3,))],
    )
    output = output.reshape(seqs, seg, width)

    pay_shape = (cycle, pay_rows, lanes)

    def attended_back(grad_att, *after):
        (back,) = call(
            functools.partial(attend_back, d=d),
            1,
            [(scal, smem), given(pay), given(kept), given(lse), given(grad_att)]
            + [(a, unread) for a in after],
            [made(pay_shape, low)],
            scratch=[pltpu.VMEM((cycle * rows, lanes), low)] * 2 + [pltpu.VMEM((cycle * rows, lanes), full)] * 2,
            vmem=vmem_back,
        )
        return back

    delta_shape = (seqs * rows, heads // 2 * wall_rows)
    first_half = pl.BlockSpec((seqs * rows, wall_rows), lambda i: (0, jnp.minimum(i, heads // 2 - 1)))
    second_half = pl.BlockSpec((seqs * rows, wall_rows), lambda i: (0, jnp.maximum(i - heads // 2, 0)))

    def head_deltas(returned, grad_out, *after):
        return call(
            functools.partial(make_deltas, d=d),
            heads,
            [
                (returned.reshape(parts, heads, seqs, pay_rows, lanes), head_spec(pay_rows, lanes)),
                (grad_out, head_spec(share, lanes)),
                (vgate, by_step((1, seqs * rows, experts), 0)),
                (expanded, by_step((1, seqs * rows, wide), 0)),
            ]
            + [(a, unread) for a in after],
            [(delta_shape, low, first_half), (delta_shape, low, second_half)],
            vmem=vmem_delta,
            flops=cost.get("deltas", 1),
        )

    def finished(deltas, *after):
        (input_grad,) = call(
            functools.partial(finish, d=d),
            heads,
            [
                (deltas[0], first_half),
                (deltas[1], second_half),
                given(inputs),
                given(gain_one),
                given(grad_residual),
                (wall, by_step((1, wall_rows, width), 0)),
            ]
            + [(a, unread) for a in after],
            [made((seqs, seg, width), full)],
            scratch=[pltpu.VMEM((tokens, width), full)],
            vmem=vmem_finish,
        )
        return input_grad

    def rows_by(array, order):
        cols = array.T.reshape(blocks, -1, array.shape[0])
        return jnp.take(cols, order ^ halver.me, axis=0).reshape(-1, array.shape[0])

    def row_product(left, right):
        quarter = left.shape[0] // 4
        return lambda lo, hi: dot_nn(left[lo * quarter : hi * quarter], right)

    gain_rows = lax.dynamic_slice_in_dim(jnp.stack([norm1_gain, norm2_gain], axis=1), halver.me * own, own, axis=0)
    if fast:
        split = 2
        pack_got = halver.swap(pack, core[0])
        mixed_got = halver.swap(mixed, core[0])
        assert width // 4 == tokens

        def down_products(piece):
            return [
                (grad_ffn_both, by_step((width // split, 2 * tokens), 0)),
                (act, pl.BlockSpec((tokens, ff // 4), lambda i: (0, piece))),
                (pack_got, pl.BlockSpec((tokens, ff // 4), lambda i: (0, piece))),
            ]

        def up_products(piece):
            step_u = ff // split
            first_u, first_n = ff // 2 // step_u, (ff // 2 + ff) // tokens
            right = pl.BlockSpec((tokens, step_u), lambda i: (0, first_u + i))
            return [
                (normed, pl.BlockSpec((tokens, tokens), lambda i: (piece, 0))),
                (pack_got, pl.BlockSpec((tokens, tokens), lambda i: (0, first_n + piece))),
                (pack, right),
                (pack_got, right),
            ]

        def d_made(cols, kind):
            return ((width, cols), kind, by_step((width // split, cols), 0))

        def u_made(rows_u, kind):
            return ((rows_u, ff), kind, by_step((rows_u, ff // split), 1))

        def out_products(piece):
            first_t = heads * wide // tokens
            right = by_step((tokens, heads * wide // split), 1)
            return [
                (turned, pl.BlockSpec((tokens, tokens), lambda i: (piece, 0))),
                (mixed_got, pl.BlockSpec((tokens, tokens), lambda i: (0, first_t + piece))),
                (mixed, right),
                (mixed_got, right),
            ]

        def out_made(rows_o, kind):
            return ((rows_o, heads * wide), kind, by_step((rows_o, heads * wide // split), 1))

        span_d = heads // 2 * wall_rows

        def head_products(piece):
            half = width // 4
            turned_spec = pl.BlockSpec((1, half, seqs * rows), lambda i: (0, piece, 0))
            got_spec = pl.BlockSpec((half, seqs * rows), lambda i: (piece, 0))
            right = by_step((seqs * rows, wall_rows), 1)
            return [
                (ctx_a, turned_spec), (ctx_a_got, got_spec), (ctx_b, turned_spec), (ctx_b_got, got_spec),
                (deltas[0], right), (deltas_a, right), (deltas[1], right), (deltas_b, right),
            ]

        def head_made(count, kind):
            return ((count, span_d), kind, by_step((count, wall_rows), 1))

        def then(*after):
            return [(a, unread) for a in after]

        def stage(kernel, steps, operands, after, outs, vmem=vmem_less):
            name = kernel.__name__
            return call(kernel, steps, operands + then(*after), outs, vmem=vmem, flops=cost.get(name, 1))

        def step_fold(kernel, keep, got, axis, *after):
            shape = tuple(n // 2 if a == axis else n for a, n in enumerate(keep.shape))
            return stage(kernel, 1, [given(keep), given(got)], after, [made(shape, low), made(shape, full)])

        grad_att = lax.all_to_all(grad_out.reshape(cycle, share, lanes), "seq", 0, 0)
        (send_u,) = stage(send_up, split, up_products(1), [grad_out], [u_made(width // 4, low)], vmem_plane)
        got_u = halver.swap(send_u, up_bits[1])
        back = attended_back(grad_att, send_u)
        returned = lax.all_to_all(back, "seq", 0, 0)
        (send_d,) = stage(send_down, split, down_products(1), [back], [d_made(ff // 4, low)], vmem_plane)
        got_d = halver.swap(send_d, down_bits[1])
        (send_o,) = stage(outer_send, split, out_products(1), [send_d], [out_made(width // 4, low)], vmem_plane)
        got_o = halver.swap(send_o, out_bits[1])
        deltas = head_deltas(returned, grad_out, send_o)
        deltas_a, deltas_b = halver.swap(deltas[0], core[0]), halver.swap(deltas[1], core[0])
        send_a, send_b = stage(
            heads_send, heads // 2, head_products(1), [deltas[0]], [head_made(width // 4, low)] * 2,
            vmem_big,
        )
        got_a, got_b = halver.swap(send_a, qkv_bits[0][1]), halver.swap(send_b, qkv_bits[1][1])
        send_u, keep_u = stage(
            cross_up,
            split,
            up_products(0) + [(got_u, by_step((width // 4, ff // split), 1))],
            [send_a],
            [u_made(width // 8, low), u_made(width // 8, full)],
            vmem_big,
        )
        got_u = halver.swap(send_u, up_bits[2])
        send_d, keep_d = stage(
            cross_down,
            split,
            down_products(0) + [(got_d, by_step((width // split, ff // 4), 0))],
            [send_u],
            [d_made(ff // 8, low), d_made(ff // 8, full)],
            vmem_big,
        )
        got_d = halver.swap(send_d, down_bits[2])
        send_o, keep_o = stage(
            outer_split,
            split,
            out_products(0) + [(got_o, by_step((width // 4, heads * wide // split), 1))],
            [send_d],
            [out_made(width // 8, low), out_made(width // 8, full)],
            vmem_big,
        )
        got_o = halver.swap(send_o, out_bits[2])
        input_grad = finished(deltas, send_o)
        send_a, send_b, keep_a, keep_b = stage(
            heads_split,
            heads // 2,
            head_products(0)
            + [(got_a, by_step((width // 4, wall_rows), 1)), (got_b, by_step((width // 4, wall_rows), 1))],
            [input_grad],
            [head_made(width // 8, low)] * 2 + [head_made(width // 8, full)] * 2,
            vmem_big,
        )
        got_a, got_b = halver.swap(send_a, qkv_bits[0][2]), halver.swap(send_b, qkv_bits[1][2])
        send_u, keep_u = step_fold(fold, keep_u, got_u, 0, send_a)
        got_u = halver.swap(send_u, up_bits[3])
        send_d, keep_d = step_fold(fold_lanes, keep_d, got_d, 1, send_u)
        got_d = halver.swap(send_d, down_bits[3])
        send_o, keep_o = step_fold(fold, keep_o, got_o, 0, send_d)
        got_o = halver.swap(send_o, out_bits[3])
        a_shape = (width // 16, span_d)
        send_a, send_b, keep_a, keep_b = stage(
            heads_third,
            1,
            [given(a) for a in (keep_a, keep_b, got_a, got_b)],
            [send_o],
            [made(a_shape, low)] * 2 + [made(a_shape, full)] * 2,
        )
        got_a, got_b = halver.swap(send_a, qkv_bits[0][3]), halver.swap(send_b, qkv_bits[1][3])
        send_d, keep_d = step_fold(fold_lanes, keep_d, got_d, 1, send_a)
        got_d = halver.swap(send_d, down_bits[4])
        send_u, keep_u = step_fold(fold, keep_u, got_u, 0, send_d)
        got_u = halver.swap(send_u, up_bits[4])
        send_o, keep_o = step_fold(fold, keep_o, got_o, 0, send_u)
        got_o = halver.swap(send_o, out_bits[4])
        a_shape = (own, span_d)
        send_a, send_b, keep_a, keep_b = stage(
            heads_last,
            1,
            [given(a) for a in (keep_a, keep_b, got_a, got_b)],
            [send_o],
            [made(a_shape, low)] * 2 + [made(a_shape, full)] * 2,
        )
        got_a, got_b = halver.swap(send_a, qkv_bits[0][4]), halver.swap(send_b, qkv_bits[1][4])
        down_grad, up_grad, norm2_grad = stage(
            end_feed,
            1,
            [given(a) for a in (keep_d, got_d, keep_u, got_u, up_own, gain_rows[:, 1:2])],
            [send_a],
            [made((lanes, width), full), made((own, ff), full), made((1, own), full)],
        )
        norm2_grad = norm2_grad.reshape(own)
        flat = [heads * size, heads * size, heads * span, 2 * heads * experts]
        query_grad, key_grad, value_grad, router_grad, norm1_grad = call(
            functools.partial(assemble, d=d),
            1,
            [given(a) for a in (keep_a, got_a, keep_b, got_b, wall_own, gain_rows[:, 0:1])] + then(up_grad),
            [made((own, cols), full) for cols in flat] + [made((1, own), full)],
            vmem=vmem_less,
            flops=cost.get("assemble", 1),
        )
        norm1_grad = norm1_grad.reshape(own)
        (outproj_grad,) = call(
            functools.partial(assemble_out, d=d),
            1,
            [given(keep_o), given(got_o)] + then(router_grad),
            [made((own, heads * span), full)],
            vmem=vmem_less,
        )
        outproj_grad = outproj_grad.T
    else:
        act = act.reshape(tokens, blocks, -1)
        act = jnp.take(act, halver.order(down_bits) ^ halver.me, axis=1).reshape(tokens, -1)

        def down_product(lo, hi):
            quarter = ff // 4
            return dot_nn(grad_ffn_t, act[:, lo * quarter : hi * quarter])

        up_product = row_product(rows_by(normed, halver.order(up_bits)), pack)
        out_product = row_product(rows_by(grad_branch, halver.order(out_bits)), mixed)
        grad_att = lax.all_to_all(grad_out.reshape(cycle, share, lanes), "seq", 0, 0)
        back = attended_back(grad_att)
        returned = lax.all_to_all(back, "seq", 0, 0)
        deltas = head_deltas(returned, grad_out)
        input_grad = finished(deltas)
        down_grad = reduced(halver, down_product, down_bits, 1).T
        up_grad = reduced(halver, up_product, up_bits, 0)
        outproj_grad = reduced(halver, out_product, out_bits, 0)
        outproj_grad = outproj_grad.reshape(own, heads * experts, lanes)[:, :, :size].reshape(own, -1).T
        qkv_left = rows_by(ctx.reshape(seqs * rows, width), halver.order(qkv_bits[0]))
        qkv_product = row_product(qkv_left, jnp.concatenate(deltas, axis=1))
        by_head = reduced(halver, qkv_product, qkv_bits[0], 0).reshape(own, heads, 2 + experts, lanes)
        query_grad = by_head[:, :, 0, :size].reshape(own, -1)
        key_grad = by_head[:, :, 1, :size].reshape(own, -1)
        value_grad = by_head[:, :, 2:, :size].reshape(own, -1)
        router_grad = jnp.concatenate(
            [by_head[:, :, 0, size + i * experts : size + (i + 1) * experts].reshape(own, -1) for i in range(2)], axis=1
        )

        def own_rows(array):
            return lax.dynamic_slice_in_dim(array, halver.me * own, own, axis=0).astype(full)

        norm1_grad = (
            jnp.sum(own_rows(query_weight) * query_grad, axis=1)
            + jnp.sum(own_rows(key_weight) * key_grad, axis=1)
            + jnp.sum(own_rows(value_weight) * value_grad, axis=1)
            + jnp.sum(own_rows(router_weight) * router_grad, axis=1)
        ) / gain_rows[:, 0]
        norm2_grad = jnp.sum(own_rows(up_weight) * up_grad, axis=1) / gain_rows[:, 1]
    return (
        output, input_grad, norm1_grad, norm2_grad, query_grad, key_grad, value_grad, router_grad,
        outproj_grad, up_grad, down_grad,
    )


def solution(mesh):
    token = P("batch", "seq", None)
    routes = P("batch", "seq", None, None)
    spread = ("seq", "batch")
    return jax.shard_map(
        local,
        mesh=mesh,
        in_specs=(token, token, token, P("batch"), routes, routes, routes) + (P(),) * 9,
        out_specs=(
            token, token, P(spread), P(spread), P(spread, None), P(spread, None), P(spread, None), P(spread, None),
            P(None, spread), P(spread, None), P(spread, None),
        ),
        check_vma=False,
    )
```

```python
import collections
import functools

import jax
import jax.numpy as jnp
import numpy as np
from jax import lax
from jax.experimental import pallas as pl
from jax.experimental.pallas import tpu as pltpu
from jax.sharding import PartitionSpec as P

epsilon = 1e-05
neg_large = -1e30
slope_base = 0.5
log2_e = 1.4426950408889634
lanes = 128
low = jnp.bfloat16
full = jnp.float32
vmem_bytes = 56 << 20
vmem_less = 24 << 20
cost = {'heads_split': 4000000000, 'heads_third': 4000000000, 'heads_last': 4000000000, 'cross_down': 2000000000, 'end_down': 6000000000, 'end_up': 3000000000, 'assemble': 3000000000}
vmem_back = 56 << 20
vmem_finish = 56 << 20
vmem_big = 56 << 20
vmem_attend = 56 << 20
vmem_end = 56 << 20
vmem_delta = 56 << 20
vmem_plane = 56 << 20

names = ["seqs", "seg", "mem", "rows", "heads", "size"]
names += ["experts", "parts", "share", "cycle", "width", "group"]
Dims = collections.namedtuple("Dims", names)


def dot_nn(left, right):
    return lax.dot_general(left, right, (((1,), (0,)), ((), ())), preferred_element_type=full)


def dot_nt(left, right):
    return lax.dot_general(left, right, (((1,), (1,)), ((), ())), preferred_element_type=full)


def dot_tn(left, right):
    return lax.dot_general(left, right, (((0,), (0,)), ((), ())), preferred_element_type=full)


def norm_parts(values):
    centred = values - jnp.mean(values, axis=-1, keepdims=True)
    spread = jnp.mean(centred * centred, axis=-1, keepdims=True)
    inverse = lax.rsqrt(spread + epsilon)
    return centred * inverse, inverse


def norm_back(grad, hat, inverse, gain_row):
    scaled = grad * gain_row
    along = jnp.mean(scaled * hat, axis=-1, keepdims=True)
    return inverse * (scaled - jnp.mean(scaled, axis=-1, keepdims=True) - hat * along)


smem = pl.BlockSpec(memory_space=pltpu.SMEM)
whole = pl.BlockSpec(memory_space=pltpu.VMEM)
unread = pl.BlockSpec(memory_space=pl.ANY)


def by_step(shape, axis):
    return pl.BlockSpec(shape, lambda i: tuple(i if a == axis else 0 for a in range(len(shape))))


def at_all(shape):
    return pl.BlockSpec(shape, lambda *i: (0,) * len(shape))


def call(kernel, steps, operands, outs, scratch=(), vmem=vmem_bytes, flops=1):
    return pl.pallas_call(
        kernel,
        grid=(steps,),
        out_shape=[jax.ShapeDtypeStruct(shape, kind) for shape, kind, _ in outs],
        in_specs=[spec for _, spec in operands],
        out_specs=[spec for _, _, spec in outs],
        scratch_shapes=list(scratch),
        compiler_params=pltpu.CompilerParams(
            vmem_limit_bytes=vmem, dimension_semantics=("arbitrary",)
        ),
        cost_estimate=pl.CostEstimate(flops=flops, bytes_accessed=1, transcendentals=0),
    )(*[a for a, _ in operands])


def picks(routes, experts):
    slots, tokens = routes.shape
    wide = jnp.concatenate([routes.astype(full), jnp.zeros((8 - slots, tokens), full)], axis=0)
    columns = wide.T
    expert = lax.broadcasted_iota(jnp.int32, (tokens, experts), 1).astype(full)
    total = jnp.zeros((tokens, experts), full)
    for slot in range(slots):
        total = total + (columns[:, slot : slot + 1] == expert).astype(full)
    return total


def fill_wall(wall_ref, wq_ref, wk_ref, wv_ref, wr_ref, d):
    size, experts = d.size, d.experts
    blank = jnp.zeros((lanes - size, d.width), low)
    wall_ref[0:size] = wq_ref[...]
    router = wr_ref[...]
    count = router.shape[0] // 2
    for h in range(d.heads):

        @pl.when(pl.program_id(0) == h)
        def _():
            mine = [router[at + h * experts : at + (h + 1) * experts] for at in (0, count)]
            wall_ref[size:lanes] = jnp.concatenate(mine + [blank[2 * experts :]], axis=0)

    wall_ref[lanes : lanes + size] = wk_ref[...]
    wall_ref[lanes + size : 2 * lanes] = blank
    for e in range(experts):
        first = (2 + e) * lanes
        wall_ref[first : first + size] = wv_ref[e * size : (e + 1) * size]
        wall_ref[first + size : first + lanes] = blank


def prepare(scal_ref, ctx_ref, wq_ref, wk_ref, wv_ref, wr_ref, wo_ref, wall_ref, exp_ref, out_ref, own_ref, d=None):
    fill_wall(wall_ref.at[0], wq_ref, wk_ref, wv_ref, wr_ref, d)
    ctx = ctx_ref[...].reshape(-1, d.width)
    exp_ref[0] = dot_nt(ctx, wall_ref[0, 2 * lanes :]).astype(low)
    for e in range(d.experts):
        out_ref[0, e * lanes : e * lanes + d.size] = wo_ref[e * d.size : (e + 1) * d.size]
        out_ref[0, e * lanes + d.size : (e + 1) * lanes] = jnp.zeros((lanes - d.size, d.width), low)
    rows = own_ref.shape[1]
    if lanes % rows == 0:
        first = scal_ref[3] * rows
        column = pl.ds(pl.multiple_of(lax.div(first, lanes) * lanes, lanes), lanes)
        turned = wall_ref[0, :, column].T
        for at in range(0, lanes, rows):

            @pl.when(lax.rem(first, lanes) == at)
            def _():
                own_ref[0] = turned[at : at + rows]


def project(
    x_ref, m_ref, vr_ref, mr_ref, or_ref, gain_ref, wq_ref, wk_ref, wv_ref, wr_ref,
    pay_ref, ctx_ref, vgate_ref, ogate_ref, wall_ref, held_ref, d=None
):
    size, experts = d.size, d.experts
    spare = lanes - size

    @pl.when(pl.program_id(0) == 0)
    def _():
        for s in range(d.seqs):
            block = jnp.concatenate([m_ref[s], x_ref[s]], axis=0).astype(full)
            hat, _ = norm_parts(block)
            block_low = (hat * gain_ref[...]).astype(low)
            held_ref[s * d.rows : (s + 1) * d.rows] = block_low
            ctx_ref[s] = block_low

    fill_wall(wall_ref, wq_ref, wk_ref, wv_ref, wr_ref, d)
    ctx = held_ref[...]
    every = dot_nt(ctx, wall_ref[...])
    query = every[:, 0:lanes]
    sig = jax.nn.sigmoid(query[:, size : size + 2 * experts])
    pick = []
    out_pick = []
    out_sig = []
    for s in range(d.seqs):
        pick.append(picks(mr_ref[s, 0], experts))
        pick.append(picks(vr_ref[s, 0], experts))
        out_pick.append(picks(or_ref[s, 0], experts))
        out_sig.append(sig[s * d.rows + d.mem : (s + 1) * d.rows, experts:])
    gate = sig[:, :experts] * jnp.concatenate(pick, axis=0)
    vgate_ref[0] = gate
    ogate_ref[0] = jnp.concatenate(out_sig, axis=0) * jnp.concatenate(out_pick, axis=0)
    count = d.seqs * d.rows
    value = jnp.zeros((count, lanes), full)
    for e in range(experts):
        value = value + gate[:, e : e + 1] * every[:, (2 + e) * lanes : (3 + e) * lanes]
    lane_at = lax.broadcasted_iota(jnp.int32, (count, lanes), 1)
    query = jnp.where(lane_at < size, query, 0.0).astype(low)
    keys = every[:, lanes : 2 * lanes].astype(low)
    value = value.astype(low)
    for s in range(d.seqs):
        mine = slice(s * d.rows, (s + 1) * d.rows)
        for p in range(d.parts):
            first = s * d.rows + d.mem + p * d.share
            pay_ref[p, 0, s] = payload(keys[mine], value[mine], query[first : first + d.share], d)


def lane_sums(product, experts):
    slot = lax.broadcasted_iota(jnp.int32, (experts * lanes, lanes), 0) // lanes
    target = lax.broadcasted_iota(jnp.int32, (experts * lanes, lanes), 1)
    ones = (slot == target).astype(full).astype(low)
    high = product.astype(low)
    rest = (product - high.astype(full)).astype(low)
    return (dot_nn(high, ones) + dot_nn(rest, ones))[:, :experts]


def turn_context(scal_ref, ctx_ref, *refs, bits=None):
    first_ref, second_ref = refs[-2:]
    value = ctx_ref[...].reshape(-1, ctx_ref.shape[-1])
    turn(value, first_ref, scal_ref[3], bits[0])
    turn(value, second_ref, scal_ref[3], bits[1])


def folded_in(d):
    half = d.share // 2
    return 2 * d.rows == 6 * half and 7 * (lanes - d.size) == d.size


def payload_rows(d):
    return 2 * d.rows + (d.share // 2 if folded_in(d) else d.share)


def payload(keys, values, queries, d):
    size, half = d.size, d.share // 2
    if not folded_in(d):
        return jnp.concatenate([keys, values, queries], axis=0)
    rows = jnp.concatenate([keys, values, queries[:half]], axis=0)
    step = lanes - size
    spare = [queries[half:, at : at + step] for at in range(0, size, step)]
    return jnp.concatenate([rows[:, :size], jnp.concatenate(spare, axis=0)], axis=1)


def payload_queries(block, d):
    size, half = d.size, d.share // 2
    blank = jnp.zeros((d.share, lanes - size), block.dtype)
    if not folded_in(d):
        return jnp.concatenate([block[2 * d.rows :, :size], blank], axis=1)
    rest = jnp.concatenate([block[at * half : (at + 1) * half, size:] for at in range(7)], axis=1)
    return jnp.concatenate([jnp.concatenate([block[2 * d.rows :, :size], rest], axis=0), blank], axis=1)


def key_value(pay_ref, k_ref, v_ref, d):
    for j in range(d.cycle):
        k_ref[j * d.mem : (j + 1) * d.mem] = pay_ref[j, 0 : d.mem]
        v_ref[j * d.mem : (j + 1) * d.mem] = pay_ref[j, d.rows : d.rows + d.mem]
        base = d.cycle * d.mem + j * d.seg
        k_ref[base : base + d.seg] = pay_ref[j, d.mem : d.rows]
        v_ref[base : base + d.seg] = pay_ref[j, d.rows + d.mem : 2 * d.rows]


def query_block(pay_ref, first, d):
    found = [payload_queries(pay_ref[j], d) for j in range(first, first + d.group)]
    return jnp.concatenate(found, axis=0)


def attend(scal_ref, pay_ref, *refs, d=None):
    att_ref, keep_ref, lse_ref, k_ref, v_ref = refs[-5:]
    share, group = d.share, d.group
    mem_len = d.cycle * d.mem
    ctx_len = d.cycle * d.rows
    length, head, part = scal_ref[0], scal_ref[1], scal_ref[2]
    key_value(pay_ref, k_ref, v_ref, d)
    slope = slope_base * (head + 1).astype(full) / ctx_len * log2_e
    place = lax.broadcasted_iota(jnp.int32, (1, ctx_len), 1) - mem_len
    bias = jnp.where(place < length, place.astype(full) * slope, neg_large)
    q_rows = group * share
    for first in range(0, d.cycle, group):
        width = mem_len + (first + group) * d.seg
        cut = width - group * d.seg
        query = query_block(pay_ref, first, d)
        scores = dot_nt(query, k_ref[0:width]) * (d.size**-0.5 * log2_e) + bias[:, :width]
        row = lax.broadcasted_iota(jnp.int32, (q_rows, group * d.seg), 0)
        col = lax.broadcasted_iota(jnp.int32, (q_rows, group * d.seg), 1)
        row_place = (row // share) * d.seg + part * share + row % share
        tail = jnp.where(col <= row_place, scores[:, cut:], neg_large)
        scores = jnp.concatenate([scores[:, :cut], tail], axis=1)
        top = jnp.max(scores, axis=1, keepdims=True)
        weights = jnp.exp2(scores - top)
        total = jnp.sum(weights, axis=1, keepdims=True)
        attended = dot_nn(weights.astype(low), v_ref[0:width]) / total
        keep_ref[first * share : first * share + q_rows] = attended
        lse_ref[first * share : first * share + q_rows] = top + jnp.log2(total)
        for j in range(group):
            att_ref[first + j] = attended[j * share : (j + 1) * share].astype(low)


def attend_back(
    scal_ref, pay_ref, keep_ref, lse_ref, grad_ref, *refs, d=None
):
    out_ref, k_ref, v_ref, dk_ref, dv_ref = refs[-5:]
    share, group, size = d.share, d.group, d.size
    mem_len = d.cycle * d.mem
    ctx_len = d.cycle * d.rows
    length, head, part = scal_ref[0], scal_ref[1], scal_ref[2]
    key_value(pay_ref, k_ref, v_ref, d)
    scale = size**-0.5
    slope = slope_base * (head + 1).astype(full) / ctx_len * log2_e
    place = lax.broadcasted_iota(jnp.int32, (ctx_len, lanes), 0) - mem_len
    bias = jnp.where(place < length, place.astype(full) * slope, neg_large)[:, 0:1]
    dk_ref[...] = jnp.zeros_like(dk_ref)
    dv_ref[...] = jnp.zeros_like(dv_ref)
    q_rows = group * share
    lane_at = lax.broadcasted_iota(jnp.int32, (q_rows, lanes), 1)
    query_grads = []
    for first in range(0, d.cycle, group):
        width = mem_len + (first + group) * d.seg
        cut = width - group * d.seg
        begin = first * share
        query = query_block(pay_ref, first, d)
        raw = jnp.concatenate([grad_ref[j] for j in range(first, first + group)], axis=0)
        grad = jnp.where(lane_at < size, raw, jnp.zeros_like(raw))
        kept = keep_ref[begin : begin + q_rows]
        delta = jnp.sum(jnp.where(lane_at < size, grad.astype(full) * kept, 0.0), axis=1, keepdims=True)
        both = jnp.concatenate(
            [
                jnp.broadcast_to(delta, (q_rows, lanes)),
                jnp.broadcast_to(lse_ref[begin : begin + q_rows], (q_rows, lanes)),
            ],
            axis=1,
        ).T
        delta_row = both[0:1]
        lse_row = both[lanes : lanes + 1]
        scores = dot_nt(k_ref[0:width], query) * (scale * log2_e) + bias[:width]
        weights = jnp.exp2(scores - lse_row)
        row = lax.broadcasted_iota(jnp.int32, (group * d.seg, q_rows), 0)
        col = lax.broadcasted_iota(jnp.int32, (group * d.seg, q_rows), 1)
        col_place = (col // share) * d.seg + part * share + col % share
        weights = jnp.concatenate([weights[:cut], jnp.where(row <= col_place, weights[cut:], 0.0)], axis=0)
        grad_weights = dot_nt(v_ref[0:width], grad)
        grad_scores = (weights * (grad_weights - delta_row)).astype(low)
        dk_ref[0:width] += dot_nn(grad_scores, query)
        dv_ref[0:width] += dot_nn(weights.astype(low), grad)
        dq = (dot_tn(grad_scores, k_ref[0:width]) * scale).astype(low)
        query_grads.append(dq)
    for j in range(d.cycle):
        base = mem_len + j * d.seg
        dk = jnp.concatenate([dk_ref[j * d.mem : (j + 1) * d.mem], dk_ref[base : base + d.seg]], axis=0)
        dv = jnp.concatenate([dv_ref[j * d.mem : (j + 1) * d.mem], dv_ref[base : base + d.seg]], axis=0)
        dq = query_grads[j // group][j % group * share : (j % group + 1) * share]
        out_ref[j] = payload((dk * scale).astype(low), dv.astype(low), dq, d)


def place_of(mask, bits):
    place = jnp.int32(0)
    for at, bit in enumerate(bits):
        place = place + ((mask >> bit) & 1) * (1 << (len(bits) - 1 - at))
    return place


def turn(value, out_ref, me, bits):
    turned = value.T
    count = 1 << len(bits)
    own = turned.shape[0] // count
    for block in range(count):
        place = place_of(block ^ me, bits)
        side = lax.div(place, count // 2)
        inside = lax.rem(place, count // 2)
        out_ref[side, pl.ds(pl.multiple_of(inside * own, own), own), :] = turned[block * own : (block + 1) * own]


def beside(turn_ref, pack_ref):
    half, tokens = turn_ref.shape[1] // 2, turn_ref.shape[2]
    first = pack_ref.shape[1] - 2 * tokens
    pack_ref[:, first : first + tokens] = turn_ref[1, 0:half]
    pack_ref[:, first + tokens :] = turn_ref[1, half:]


def feed(
    scal_ref, att_ref, ogate_ref, x_ref, gain_ref, live_ref, gf_ref, wo_ref, up_ref, down_ref,
    mix_hbm, act_hbm, pack_hbm, out_ref, resid_ref, branch_ref, normed_ref, turned_ref, gatt_ref,
    sum_ref, ffn_ref, back_ref, held_ref, turn_ref, out_mix_ref, act_ref, pack_ref, copied, d=None, bits=None
):
    step = pl.program_id(0)
    together = wo_ref.shape[0]
    steps_h = d.heads // together
    last = pl.num_programs(0) - 1 - steps_h
    experts = d.experts
    me = scal_ref[3]

    @pl.when(step == 0)
    def _():
        for s in range(d.seqs):
            sum_ref[s * d.seg : (s + 1) * d.seg] = x_ref[s].astype(full)
        ffn_ref[...] = jnp.zeros_like(ffn_ref)
        back_ref[...] = jnp.zeros_like(back_ref)

    @pl.when(step < steps_h)
    def _():
        total = sum_ref[...]
        for k in range(together):
            found = [att_ref[p, k, s] for s in range(d.seqs) for p in range(d.parts)]
            att = jnp.concatenate(found, axis=0).astype(full)
            gate = ogate_ref[k]
            mixed = jnp.concatenate([(gate[:, e : e + 1] * att).astype(low) for e in range(experts)], axis=1)
            wide = mixed.shape[1]
            out_mix_ref[:, pl.ds(pl.multiple_of((step * together + k) * wide, lanes), wide)] = mixed
            total = total + dot_nn(mixed, wo_ref[k])
        sum_ref[...] = total

    @pl.when(step == steps_h - 1)
    def _():
        hat, _ = norm_parts(sum_ref[...])
        normed = (hat * gain_ref[...]).astype(low)
        held_ref[...] = normed
        if bits is None:
            normed_ref[...] = normed
        else:
            turn(normed, turn_ref, me, bits[1])
            normed_ref[...] = turn_ref[0]
            beside(turn_ref, pack_ref)

    @pl.when((step >= steps_h) & (step <= last))
    def _():
        coeff = 0.7978845608028654
        held = held_ref[...]
        outer_grad = gf_ref[...]
        acts = []
        grads = []
        part = up_ref.shape[1] // 4
        for c in range(4):
            mine = slice(c * part, (c + 1) * part)
            value = dot_nn(held, up_ref[:, mine])
            grad_act = dot_nt(outer_grad, down_ref[mine, :])
            square = value * value
            wave = jnp.tanh(value * (coeff + (0.044715 * coeff) * square))
            rise = 0.5 + 0.5 * wave
            acts.append((value * rise).astype(low))
            slope = rise + (0.5 * value) * (1.0 - wave * wave) * (coeff + (3 * 0.044715 * coeff) * square)
            grads.append((grad_act * slope).astype(low))
        act = jnp.concatenate(acts, axis=1)
        gu = jnp.concatenate(grads, axis=1)
        ffn_ref[...] += dot_nn(act, down_ref[...])
        back_ref[...] += dot_nt(gu, up_ref[...])
        block = step - steps_h
        span = act.shape[1]
        if bits is None:
            pack_ref[:, pl.ds(pl.multiple_of(block * span, span), span)] = gu
            act_ref[:, pl.ds(pl.multiple_of(block * span, span), span)] = act
        else:
            half = 1 << (len(bits[0]) - 1)
            own = act_ref.shape[1] // half
            pack_ref[:, pl.ds(pl.multiple_of(half * own + block * span, lanes), span)] = gu
            for b in range(span // own):
                piece = act[:, b * own : (b + 1) * own]
                place = place_of((block * (span // own) + b) ^ me, bits[0])
                inside = pl.ds(pl.multiple_of(lax.rem(place, half) * own, own), own)

                @pl.when(place < half)
                def _():
                    act_ref[:, inside] = piece

                @pl.when(place >= half)
                def _():
                    pack_ref[:, inside] = piece

    @pl.when(step == last)
    def _():
        residual = sum_ref[...]
        out_ref[...] = ((residual + ffn_ref[...]) * live_ref[...]).astype(low)
        hat, inverse = norm_parts(residual)
        grad = gf_ref[...].astype(full) + norm_back(back_ref[...], hat, inverse, gain_ref[...])
        resid_ref[...] = grad
        branch = grad.astype(low)
        branch_ref[...] = branch
        if bits is None:
            turned_ref[...] = branch
        else:
            turn(branch, turn_ref, me, bits[2])
            turned_ref[...] = turn_ref[0]
            beside(turn_ref, out_mix_ref)

    moves = [
        pltpu.make_async_copy(held, result, copied.at[at])
        for at, (held, result) in enumerate(((out_mix_ref, mix_hbm), (act_ref, act_hbm), (pack_ref, pack_hbm)))
    ]

    @pl.when(step == last)
    def _():
        for move in moves:
            move.start()

    @pl.when(step > last)
    def _():
        for k in range(together):
            unmix(branch_ref, att_ref, ogate_ref, wo_ref, gatt_ref, k, d)

    @pl.when(step == pl.num_programs(0) - 1)
    def _():
        for move in moves:
            move.wait()


def unmix(branch_ref, att_ref, ogate_ref, wo_ref, out_ref, k, d):
    size, experts = d.size, d.experts
    tokens = d.seqs * d.seg
    grad_mixed = dot_nt(branch_ref[...], wo_ref[k])
    found = [att_ref[p, k, s] for s in range(d.seqs) for p in range(d.parts)]
    att = jnp.concatenate(found, axis=0).astype(full)
    gate = ogate_ref[k]
    grad = jnp.zeros((tokens, lanes), full)
    product = []
    for e in range(experts):
        piece = grad_mixed[:, e * lanes : (e + 1) * lanes]
        grad = grad + gate[:, e : e + 1] * piece
        product.append(piece * att)
    logit = lane_sums(jnp.concatenate(product, axis=1), experts) * gate * (1.0 - gate)
    joined = jnp.concatenate(
        [grad[:, :size].astype(low), logit.astype(low), jnp.zeros((tokens, lanes - size - experts), low)], axis=1
    )
    for s in range(d.seqs):
        for p in range(d.parts):
            first = s * d.seg + p * d.share
            out_ref[p, k, s] = joined[first : first + d.share]


def make_deltas(back_ref, grad_ref, vgate_ref, exp_ref, *refs, d=None):
    size, experts = d.size, d.experts
    q_found, k_found, v_found, lo_found = [], [], [], []
    for s in range(d.seqs):
        kv = back_ref[0, 0, s, 0 : 2 * d.rows]
        if d.parts > 1:
            kv = kv.astype(full)
            for p in range(1, d.parts):
                kv = kv + back_ref[p, 0, s, 0 : 2 * d.rows].astype(full)
            kv = kv.astype(low)
        k_found.append(kv[: d.rows])
        v_found.append(kv[d.rows :])
        q_found.append(jnp.zeros((d.mem, lanes), low))
        lo_found.append(jnp.zeros((d.mem, lanes), low))
        for p in range(d.parts):
            q_found.append(payload_queries(back_ref[p, 0, s], d))
            lo_found.append(grad_ref[p, 0, s])
    query = jnp.concatenate(q_found, axis=0)
    keys = jnp.concatenate(k_found, axis=0)
    values = jnp.concatenate(v_found, axis=0)
    out_logit = jnp.concatenate(lo_found, axis=0)[:, size : size + experts]
    gate = vgate_ref[0]
    lane_at = lax.broadcasted_iota(jnp.int32, (d.seqs * d.rows, lanes), 1)
    value = jnp.where(lane_at < size, values.astype(full), 0.0)
    keys = jnp.where(lane_at < size, keys, jnp.zeros_like(keys))
    product = jnp.concatenate(
        [value * exp_ref[0, :, e * lanes : (e + 1) * lanes].astype(full) for e in range(experts)], axis=1
    )
    logit = (lane_sums(product, experts) * gate * (1.0 - gate)).astype(low)
    first = jnp.concatenate(
        [query[:, :size], logit, out_logit, jnp.zeros((d.seqs * d.rows, lanes - size - 2 * experts), low)], axis=1
    )
    step = pl.program_id(0)
    for at, delta_ref in enumerate(refs[-2:]):

        @pl.when(step // (d.heads // 2) == at)
        def _():
            delta_ref[:, 0:lanes] = first
            delta_ref[:, lanes : 2 * lanes] = keys
            for e in range(experts):
                delta_ref[:, (2 + e) * lanes : (3 + e) * lanes] = (gate[:, e : e + 1] * value).astype(low)


def finish(first_ref, second_ref, x_ref, gain_ref, resid_ref, wall_ref, *refs, d=None):
    out_ref, sum_ref = refs[-2:]
    step = pl.program_id(0)

    @pl.when(step == 0)
    def _():
        sum_ref[...] = jnp.zeros_like(sum_ref)

    for at, delta_ref in enumerate((first_ref, second_ref)):

        @pl.when(step // (d.heads // 2) == at)
        def _():
            rows = [delta_ref[s * d.rows + d.mem : (s + 1) * d.rows] for s in range(d.seqs)]
            sum_ref[...] += dot_nn(jnp.concatenate(rows, axis=0), wall_ref[0])

    @pl.when(step == pl.num_programs(0) - 1)
    def _():
        for s in range(d.seqs):
            hat, inverse = norm_parts(x_ref[s].astype(full))
            mine = slice(s * d.seg, (s + 1) * d.seg)
            out_ref[s] = resid_ref[mine] + norm_back(sum_ref[mine], hat, inverse, gain_ref[...])


def both(first, second, axis):
    return jnp.concatenate([first, second], axis=axis)


def send_down(gf_ref, act_ref, act_got_ref, *refs):
    refs[-1][...] = dot_nn(gf_ref[...], both(act_ref[...], act_got_ref[...], 0)).astype(low)


def send_up(left_ref, left_got_ref, gu_ref, gu_got_ref, *refs):
    left = both(left_ref[...], left_got_ref[...], 1)
    refs[-1][...] = dot_nn(left, both(gu_ref[...], gu_got_ref[...], 0)).astype(low)


def cross_down(gf_ref, act_ref, act_got_ref, new_ref, *refs):
    send_ref, keep_ref = refs[-2:]
    total = dot_nn(gf_ref[...], both(act_ref[...], act_got_ref[...], 0)) + new_ref[...].astype(full)
    half = total.shape[1] // 2
    keep_ref[...] = total[:, :half]
    send_ref[...] = total[:, half:].astype(low)


def cross_up(left_ref, left_got_ref, gu_ref, gu_got_ref, new_ref, *refs):
    send_ref, keep_ref = refs[-2:]
    left = both(left_ref[...], left_got_ref[...], 1)
    total = dot_nn(left, both(gu_ref[...], gu_got_ref[...], 0)) + new_ref[...].astype(full)
    half = total.shape[0] // 2
    keep_ref[...] = total[:half]
    send_ref[...] = total[half:].astype(low)


def fold_lanes(keep_ref, got_ref, *refs):
    send_ref, left_ref = refs[-2:]
    total = keep_ref[...] + got_ref[...].astype(full)
    half = total.shape[1] // 2
    left_ref[...] = total[:, :half]
    send_ref[...] = total[:, half:].astype(low)


def end_down(keep_ref, got_ref, *refs):
    refs[-1][...] = (keep_ref[...] + got_ref[...].astype(full)).T


def end_up(keep_u_ref, got_u_ref, weight_ref, gain_ref, *refs):
    up_ref, norm_ref = refs[-2:]
    total = keep_u_ref[...] + got_u_ref[...].astype(full)
    up_ref[...] = total
    along = jnp.sum(total * weight_ref[...].astype(full), axis=1, keepdims=True)
    norm_ref[...] = row_of(along / gain_ref[...])


def outer_send(left_ref, left_got_ref, right_ref, right_got_ref, *refs):
    left = both(left_ref[...], left_got_ref[...], 1)
    refs[-1][...] = dot_nn(left, both(right_ref[...], right_got_ref[...], 0)).astype(low)


def outer_split(left_ref, left_got_ref, right_ref, right_got_ref, new_ref, *refs):
    send_ref, keep_ref = refs[-2:]
    left = both(left_ref[...], left_got_ref[...], 1)
    total = dot_nn(left, both(right_ref[...], right_got_ref[...], 0)) + new_ref[...].astype(full)
    half = total.shape[0] // 2
    keep_ref[...] = total[:half]
    send_ref[...] = total[half:].astype(low)


def heads_send(a_ref, a_got_ref, b_ref, b_got_ref, da_ref, da_got_ref, db_ref, db_got_ref, *refs):
    a_out, b_out = refs[-2:]
    a_out[...] = dot_nn(both(a_ref[0], a_got_ref[...], 1), both(da_ref[...], da_got_ref[...], 0)).astype(low)
    b_out[...] = dot_nn(both(b_ref[0], b_got_ref[...], 1), both(db_ref[...], db_got_ref[...], 0)).astype(low)


def heads_split(
    a_ref, a_got_ref, b_ref, b_got_ref, da_ref, da_got_ref, db_ref, db_got_ref, new_a_ref, new_b_ref, *refs
):
    outs = refs[-4:]
    left = both(a_ref[0], a_got_ref[...], 1), both(b_ref[0], b_got_ref[...], 1)
    right = both(da_ref[...], da_got_ref[...], 0), both(db_ref[...], db_got_ref[...], 0)
    for at, new_ref in enumerate((new_a_ref, new_b_ref)):
        total = dot_nn(left[at], right[at]) + new_ref[...].astype(full)
        half = total.shape[0] // 2
        outs[2 + at][...] = total[:half]
        outs[at][...] = total[half:].astype(low)


def heads_third(keep_a_ref, keep_b_ref, got_a_ref, got_b_ref, *refs):
    outs = refs[-4:]
    for at, (keep_ref, got_ref) in enumerate(((keep_a_ref, got_a_ref), (keep_b_ref, got_b_ref))):
        half = keep_ref.shape[0] // 2
        outs[2 + at][...] = keep_ref[:half] + got_ref[:half].astype(full)
        outs[at][...] = (keep_ref[half:] + got_ref[half:].astype(full)).astype(low)


def heads_last(*refs):
    heads_third(*refs)


def fold(keep_ref, got_ref, *refs):
    send_ref, left_ref = refs[-2:]
    half = keep_ref.shape[0] // 2
    left_ref[...] = keep_ref[:half] + got_ref[:half].astype(full)
    send_ref[...] = (keep_ref[half:] + got_ref[half:].astype(full)).astype(low)


def row_of(column):
    n = column.shape[0]
    same = lax.broadcasted_iota(jnp.int32, (n, n), 0) == lax.broadcasted_iota(jnp.int32, (n, n), 1)
    return jnp.sum(jnp.where(same, column, 0.0), axis=0, keepdims=True)


def assemble(a_ref, got_a_ref, b_ref, got_b_ref, o_ref, got_o_ref, wall_ref, gain_ref, *refs, d=None):
    q_ref, k_ref, v_ref, r_ref, out_ref, norm_ref = refs[-6:]
    size, experts = d.size, d.experts
    slots = 2 + experts

    def total(kept, got, first):
        here = slice(first * lanes, (first + 1) * lanes)
        return kept[:, here] + got[:, here].astype(full)

    half = d.heads // 2
    every = [[total(a_ref, got_a_ref, h * slots + at) for at in range(slots)] for h in range(half)]
    every += [[total(b_ref, got_b_ref, h * slots + at) for at in range(slots)] for h in range(half)]
    along = jnp.zeros(every[0][0].shape, full)
    for h in range(d.heads):
        for at in range(slots):
            along = along + every[h][at] * wall_ref[h, :, at * lanes : (at + 1) * lanes].astype(full)
    norm_ref[...] = row_of(jnp.sum(along, axis=1, keepdims=True) / gain_ref[...])
    q_ref[...] = jnp.concatenate([one[0][:, :size] for one in every], axis=1)
    k_ref[...] = jnp.concatenate([one[1][:, :size] for one in every], axis=1)
    v_ref[...] = jnp.concatenate([one[2 + e][:, :size] for one in every for e in range(experts)], axis=1)
    values = [one[0][:, size : size + experts] for one in every]
    outs = [one[0][:, size + experts : size + 2 * experts] for one in every]
    r_ref[...] = jnp.concatenate(values + outs, axis=1)
    out_ref[...] = jnp.concatenate(
        [total(o_ref, got_o_ref, at)[:, :size] for at in range(d.heads * experts)], axis=1
    )


class Halver:
    def __init__(self):
        self.cycle = lax.axis_size("seq")
        self.width = lax.axis_size("batch")
        self.low_bits = self.width.bit_length() - 1
        self.high_bits = self.cycle.bit_length() - 1
        self.me = lax.axis_index("seq") * self.width + lax.axis_index("batch")

    def swap(self, value, bit):
        if bit < self.low_bits:
            axis, size, mask = "batch", self.width, 1 << bit
        else:
            axis, size, mask = "seq", self.cycle, 1 << (bit - self.low_bits)
        return lax.ppermute(value, axis, [(i, i ^ mask) for i in range(size)])

    def order(self, bits):
        count = len(bits)
        found = np.zeros(1 << count, np.int32)
        for place in range(1 << count):
            for at, bit in enumerate(bits):
                if place >> (count - 1 - at) & 1:
                    found[place] |= 1 << bit
        return found


def halve(value, axis):
    size = value.shape[axis] // 2
    return (
        lax.slice_in_dim(value, 0, size, axis=axis),
        lax.slice_in_dim(value, size, 2 * size, axis=axis),
    )


def reduced(halver, product, bits, axis):
    got = halver.swap(product(2, 4).astype(low), bits[0])
    got_keep, got_send = halve(got, axis)
    got = halver.swap((product(1, 2) + got_send.astype(full)).astype(low), bits[1])
    keep = product(0, 1) + got_keep.astype(full) + got.astype(full)
    for bit in bits[2:]:
        keep, send = halve(keep, axis)
        keep = keep + halver.swap(send.astype(low), bit).astype(full)
    return keep


def local(
    inputs, memory, cotangent, valid_len, value_routes, memory_routes, output_routes, norm1_gain, norm2_gain,
    query_weight, key_weight, value_weight, router_weight, output_weight, up_weight, down_weight
):
    seqs, seg, width = inputs.shape
    mem = memory.shape[1]
    rows = seg + mem
    heads = value_routes.shape[2]
    slots_count = value_routes.shape[3]
    qk_width = query_weight.shape[1]
    size = qk_width // heads
    experts = value_weight.shape[1] // qk_width
    span = experts * size
    ff = up_weight.shape[1]
    tokens = seqs * seg
    halver = Halver()
    cycle = halver.cycle
    parts = cycle // (seqs * heads)
    share = seg // parts
    d = Dims(seqs, seg, mem, rows, heads, size, experts, parts, share, cycle, width, 2)
    pay_rows = payload_rows(d)
    at = lax.axis_index("seq")
    my_seq = at % seqs
    my_head = at // seqs % heads
    my_part = at // (seqs * heads)
    my_length = lax.dynamic_index_in_dim(valid_len, my_seq, 0, keepdims=False)
    scal = jnp.stack([my_length, my_head, my_part, halver.me]).astype(jnp.int32)
    gain_one = norm1_gain.reshape(1, width)
    gain_two = norm2_gain.reshape(1, width)
    place = at * seg + jnp.arange(seg, dtype=jnp.int32)
    live = (place[None, :] < valid_len[:, None]).astype(full).reshape(tokens, 1)
    grad_ffn = (cotangent.reshape(tokens, width).astype(full) * live).astype(low)
    wq, wk, wv, wr = query_weight.T, key_weight.T, value_weight.T, router_weight.T
    v_routes = jnp.transpose(value_routes, (0, 2, 3, 1))
    m_routes = jnp.transpose(memory_routes, (0, 2, 3, 1))
    o_routes = jnp.transpose(output_routes, (0, 2, 3, 1))
    blocks = cycle * halver.width
    own = width // blocks
    wide = experts * lanes
    wall_rows = 2 * lanes + wide
    wall_shape = (heads, wall_rows, width)

    def routes_spec(count):
        return by_step((seqs, 1, slots_count, count), 1)

    def head_spec(*tail):
        return by_step((parts, 1, seqs) + tail, 1)

    def given(array):
        return (array, at_all(array.shape))

    def made(shape, kind):
        return (shape, kind, at_all(shape))

    pay, ctx, vgate, ogate = call(
        functools.partial(project, d=d),
        heads,
        [
            given(inputs),
            given(memory),
            (v_routes, routes_spec(seg)),
            (m_routes, routes_spec(mem)),
            (o_routes, routes_spec(seg)),
            given(gain_one),
            (wq, by_step((size, width), 0)),
            (wk, by_step((size, width), 0)),
            (wv, by_step((span, width), 0)),
            given(wr),
        ],
        [
            ((parts, heads, seqs, pay_rows, lanes), low, head_spec(pay_rows, lanes)),
            made((seqs, rows, width), low),
            ((heads, seqs * rows, experts), full, by_step((1, seqs * rows, experts), 0)),
            ((heads, tokens, experts), full, by_step((1, tokens, experts), 0)),
        ],
        scratch=[pltpu.VMEM(wall_shape[1:], low), pltpu.VMEM((seqs * rows, width), low)],
    )
    wall, expanded, wo, wall_own = call(
        functools.partial(prepare, d=d),
        heads,
        [
            (scal, smem),
            given(ctx),
            (wq, by_step((size, width), 0)),
            (wk, by_step((size, width), 0)),
            (wv, by_step((span, width), 0)),
            given(wr),
            (output_weight, by_step((span, width), 0)),
        ],
        [
            (wall_shape, low, by_step((1,) + wall_shape[1:], 0)),
            ((heads, seqs * rows, wide), low, by_step((1, seqs * rows, wide), 0)),
            ((heads, wide, width), low, by_step((1, wide, width), 0)),
            ((heads, own, wall_rows), low, by_step((1, own, wall_rows), 0)),
        ],
    )
    up_own = lax.dynamic_slice_in_dim(up_weight, halver.me * own, own, axis=0)
    bit_count = halver.low_bits + halver.high_bits
    low_b = list(range(halver.low_bits))
    high_b = list(range(halver.low_bits, bit_count))
    core, chip_y, chip_x, chip_z = low_b[:1], low_b[1:], high_b[:1], high_b[1:]
    down_bits = core + chip_x + chip_y + chip_z
    up_bits = core + chip_y + chip_z[:1] + chip_x + chip_z[1:]
    out_bits = core + chip_z[:1] + chip_x + chip_y + chip_z[1:]
    fast = own == 32 and ff == blocks * lanes and len(chip_z) == 2 and len(chip_y) == 1

    qkv_bits = down_bits, core + chip_y + chip_z[:1] + chip_x + chip_z[1:]
    grad_ffn_t = grad_ffn.T
    after = [wo]
    if fast:
        turned_ctx = (2, width // 2, seqs * rows)
        ctx_a, ctx_b = call(
            functools.partial(turn_context, bits=qkv_bits),
            1,
            [(scal, smem), given(ctx), (wo, unread)],
            [made(turned_ctx, low), made(turned_ctx, low)],
        )
        grad_ffn_both = jnp.concatenate([grad_ffn_t, halver.swap(grad_ffn_t, core[0])], axis=1)
        ctx_a_got, ctx_b_got = halver.swap(ctx_a[1], core[0]), halver.swap(ctx_b[1], core[0])
        after += [grad_ffn_both, ctx_a_got, ctx_b_got]
    pay = lax.all_to_all(pay.reshape(cycle, pay_rows, lanes), "seq", 0, 0)
    att, kept, lse = call(
        functools.partial(attend, d=d),
        1,
        [(scal, smem), given(pay)] + [(a, unread) for a in after],
        [
            made((cycle, share, lanes), low),
            made((cycle * share, lanes), full),
            made((cycle * share, 1), full),
        ],
        scratch=[pltpu.VMEM((cycle * rows, lanes), low)] * 2,
        vmem=vmem_attend,
    )
    att = lax.all_to_all(att, "seq", 0, 0)
    steps, together = 4, 2
    steps_h = heads // together
    att_heads = att.reshape(parts, heads, seqs, share, lanes)

    def ff_block(i):
        return jnp.clip(i - steps_h, 0, steps - 1)

    def head_of(i):
        return jnp.where(i < steps_h + steps, jnp.minimum(i, steps_h - 1), i - steps_h - steps)

    def back_of(i):
        return jnp.maximum(i - steps_h - steps, 0)

    turned_shape = (width // 2, tokens) if fast else (tokens, width)
    act_shape = (tokens, ff // 2) if fast else (tokens, ff)
    pack_shape = (tokens, ff // 2 + ff + 2 * tokens) if fast else (tokens, ff)
    mix_shape = (tokens, heads * wide + 2 * tokens) if fast else (tokens, heads * wide)
    mixed, act, pack, output, grad_residual, grad_branch, normed, turned, grad_out = call(
        functools.partial(feed, d=d, bits=(tuple(down_bits), tuple(up_bits), tuple(out_bits)) if fast else None),
        2 * steps_h + steps,
        [
            (scal, smem),
            (att_heads, pl.BlockSpec((parts, together, seqs, share, lanes), lambda i: (0, head_of(i), 0, 0, 0))),
            (ogate, pl.BlockSpec((together, tokens, experts), lambda i: (head_of(i), 0, 0))),
            given(inputs),
            given(gain_two),
            given(live),
            given(grad_ffn),
            (wo, pl.BlockSpec((together, wide, width), lambda i: (head_of(i), 0, 0))),
            (up_weight, pl.BlockSpec((width, ff // steps), lambda i: (0, ff_block(i)))),
            (down_weight, pl.BlockSpec((ff // steps, width), lambda i: (ff_block(i), 0))),
        ],
        [
            (mix_shape, low, unread),
            (act_shape, low, unread),
            (pack_shape, low, unread),
            made((tokens, width), low),
            made((tokens, width), full),
            made((tokens, width), low),
            made(turned_shape, low),
            made(turned_shape, low),
            (
                (parts, heads, seqs, share, lanes),
                low,
                pl.BlockSpec((parts, together, seqs, share, lanes), lambda i: (0, back_of(i), 0, 0, 0)),
            ),
        ],
        scratch=[pltpu.VMEM((tokens, width), full)] * 3
        + [pltpu.VMEM((tokens, width), low), pltpu.VMEM((2, width // 2, tokens), low)]
        + [pltpu.VMEM(shape, low) for shape in (mix_shape, act_shape, pack_shape)]
        + [pltpu.SemaphoreType.DMA((3,))],
    )
    output = output.reshape(seqs, seg, width)

    pay_shape = (cycle, pay_rows, lanes)

    def attended_back(grad_att, *after):
        (back,) = call(
            functools.partial(attend_back, d=d),
            1,
            [(scal, smem), given(pay), given(kept), given(lse), given(grad_att)]
            + [(a, unread) for a in after],
            [made(pay_shape, low)],
            scratch=[pltpu.VMEM((cycle * rows, lanes), low)] * 2 + [pltpu.VMEM((cycle * rows, lanes), full)] * 2,
            vmem=vmem_back,
        )
        return back

    delta_shape = (seqs * rows, heads // 2 * wall_rows)
    first_half = pl.BlockSpec((seqs * rows, wall_rows), lambda i: (0, jnp.minimum(i, heads // 2 - 1)))
    second_half = pl.BlockSpec((seqs * rows, wall_rows), lambda i: (0, jnp.maximum(i - heads // 2, 0)))

    def head_deltas(returned, grad_out, *after):
        return call(
            functools.partial(make_deltas, d=d),
            heads,
            [
                (returned.reshape(parts, heads, seqs, pay_rows, lanes), head_spec(pay_rows, lanes)),
                (grad_out, head_spec(share, lanes)),
                (vgate, by_step((1, seqs * rows, experts), 0)),
                (expanded, by_step((1, seqs * rows, wide), 0)),
            ]
            + [(a, unread) for a in after],
            [(delta_shape, low, first_half), (delta_shape, low, second_half)],
            vmem=vmem_delta,
            flops=cost.get("deltas", 1),
        )

    def finished(deltas, *after):
        (input_grad,) = call(
            functools.partial(finish, d=d),
            heads,
            [
                (deltas[0], first_half),
                (deltas[1], second_half),
                given(inputs),
                given(gain_one),
                given(grad_residual),
                (wall, by_step((1, wall_rows, width), 0)),
            ]
            + [(a, unread) for a in after],
            [made((seqs, seg, width), full)],
            scratch=[pltpu.VMEM((tokens, width), full)],
            vmem=vmem_finish,
        )
        return input_grad

    def rows_by(array, order):
        cols = array.T.reshape(blocks, -1, array.shape[0])
        return jnp.take(cols, order ^ halver.me, axis=0).reshape(-1, array.shape[0])

    def row_product(left, right):
        quarter = left.shape[0] // 4
        return lambda lo, hi: dot_nn(left[lo * quarter : hi * quarter], right)

    gain_rows = lax.dynamic_slice_in_dim(jnp.stack([norm1_gain, norm2_gain], axis=1), halver.me * own, own, axis=0)
    if fast:
        split = 2
        pack_got = halver.swap(pack, core[0])
        mixed_got = halver.swap(mixed, core[0])
        assert width // 4 == tokens

        def down_products(piece):
            return [
                (grad_ffn_both, by_step((width // split, 2 * tokens), 0)),
                (act, pl.BlockSpec((tokens, ff // 4), lambda i: (0, piece))),
                (pack_got, pl.BlockSpec((tokens, ff // 4), lambda i: (0, piece))),
            ]

        def up_products(piece):
            step_u = ff // split
            first_u, first_n = ff // 2 // step_u, (ff // 2 + ff) // tokens
            right = pl.BlockSpec((tokens, step_u), lambda i: (0, first_u + i))
            return [
                (normed, pl.BlockSpec((tokens, tokens), lambda i: (piece, 0))),
                (pack_got, pl.BlockSpec((tokens, tokens), lambda i: (0, first_n + piece))),
                (pack, right),
                (pack_got, right),
            ]

        def d_made(cols, kind):
            return ((width, cols), kind, by_step((width // split, cols), 0))

        def u_made(rows_u, kind):
            return ((rows_u, ff), kind, by_step((rows_u, ff // split), 1))

        def out_products(piece):
            first_t = heads * wide // tokens
            right = by_step((tokens, heads * wide // split), 1)
            return [
                (turned, pl.BlockSpec((tokens, tokens), lambda i: (piece, 0))),
                (mixed_got, pl.BlockSpec((tokens, tokens), lambda i: (0, first_t + piece))),
                (mixed, right),
                (mixed_got, right),
            ]

        def out_made(rows_o, kind):
            return ((rows_o, heads * wide), kind, by_step((rows_o, heads * wide // split), 1))

        span_d = heads // 2 * wall_rows

        def head_products(piece):
            half = width // 4
            turned_spec = pl.BlockSpec((1, half, seqs * rows), lambda i: (0, piece, 0))
            got_spec = pl.BlockSpec((half, seqs * rows), lambda i: (piece, 0))
            right = by_step((seqs * rows, wall_rows), 1)
            return [
                (ctx_a, turned_spec), (ctx_a_got, got_spec), (ctx_b, turned_spec), (ctx_b_got, got_spec),
                (deltas[0], right), (deltas_a, right), (deltas[1], right), (deltas_b, right),
            ]

        def head_made(count, kind):
            return ((count, span_d), kind, by_step((count, wall_rows), 1))

        def then(*after):
            return [(a, unread) for a in after]

        def stage(kernel, steps, operands, after, outs, vmem=vmem_less):
            name = kernel.__name__
            return call(kernel, steps, operands + then(*after), outs, vmem=vmem, flops=cost.get(name, 1))

        def step_fold(kernel, keep, got, axis, *after):
            shape = tuple(n // 2 if a == axis else n for a, n in enumerate(keep.shape))
            return stage(kernel, 1, [given(keep), given(got)], after, [made(shape, low), made(shape, full)])

        grad_att = lax.all_to_all(grad_out.reshape(cycle, share, lanes), "seq", 0, 0)
        (send_u,) = stage(send_up, split, up_products(1), [grad_out], [u_made(width // 4, low)], vmem_plane)
        got_u = halver.swap(send_u, up_bits[1])
        back = attended_back(grad_att, send_u)
        returned = lax.all_to_all(back, "seq", 0, 0)
        (send_d,) = stage(send_down, split, down_products(1), [back], [d_made(ff // 4, low)], vmem_plane)
        got_d = halver.swap(send_d, down_bits[1])
        (send_o,) = stage(outer_send, split, out_products(1), [send_d], [out_made(width // 4, low)], vmem_plane)
        got_o = halver.swap(send_o, out_bits[1])
        deltas = head_deltas(returned, grad_out, send_o)
        deltas_a, deltas_b = halver.swap(deltas[0], core[0]), halver.swap(deltas[1], core[0])
        send_a, send_b = stage(
            heads_send, heads // 2, head_products(1), [deltas[0]], [head_made(width // 4, low)] * 2,
            vmem_big,
        )
        got_a, got_b = halver.swap(send_a, qkv_bits[0][1]), halver.swap(send_b, qkv_bits[1][1])
        send_u, keep_u = stage(
            cross_up,
            split,
            up_products(0) + [(got_u, by_step((width // 4, ff // split), 1))],
            [send_a],
            [u_made(width // 8, low), u_made(width // 8, full)],
            vmem_big,
        )
        got_u = halver.swap(send_u, up_bits[2])
        send_d, keep_d = stage(
            cross_down,
            split,
            down_products(0) + [(got_d, by_step((width // split, ff // 4), 0))],
            [send_u],
            [d_made(ff // 8, low), d_made(ff // 8, full)],
            vmem_big,
        )
        got_d = halver.swap(send_d, down_bits[2])
        send_o, keep_o = stage(
            outer_split,
            split,
            out_products(0) + [(got_o, by_step((width // 4, heads * wide // split), 1))],
            [send_d],
            [out_made(width // 8, low), out_made(width // 8, full)],
            vmem_big,
        )
        got_o = halver.swap(send_o, out_bits[2])
        input_grad = finished(deltas, send_o)
        send_a, send_b, keep_a, keep_b = stage(
            heads_split,
            heads // 2,
            head_products(0)
            + [(got_a, by_step((width // 4, wall_rows), 1)), (got_b, by_step((width // 4, wall_rows), 1))],
            [input_grad],
            [head_made(width // 8, low)] * 2 + [head_made(width // 8, full)] * 2,
            vmem_big,
        )
        got_a, got_b = halver.swap(send_a, qkv_bits[0][2]), halver.swap(send_b, qkv_bits[1][2])
        send_u, keep_u = step_fold(fold, keep_u, got_u, 0, send_a)
        got_u = halver.swap(send_u, up_bits[3])
        send_d, keep_d = step_fold(fold_lanes, keep_d, got_d, 1, send_u)
        got_d = halver.swap(send_d, down_bits[3])
        send_o, keep_o = step_fold(fold, keep_o, got_o, 0, send_d)
        got_o = halver.swap(send_o, out_bits[3])
        send_u, keep_u = step_fold(fold, keep_u, got_u, 0, send_o)
        got_u = halver.swap(send_u, up_bits[4])
        a_shape = (width // 16, span_d)
        send_a, send_b, keep_a, keep_b = stage(
            heads_third,
            1,
            [given(a) for a in (keep_a, keep_b, got_a, got_b)],
            [send_u],
            [made(a_shape, low)] * 2 + [made(a_shape, full)] * 2,
        )
        got_a, got_b = halver.swap(send_a, qkv_bits[0][3]), halver.swap(send_b, qkv_bits[1][3])
        send_d, keep_d = step_fold(fold_lanes, keep_d, got_d, 1, send_a)
        got_d = halver.swap(send_d, down_bits[4])
        send_o, keep_o = step_fold(fold, keep_o, got_o, 0, send_d)
        got_o = halver.swap(send_o, out_bits[4])
        up_grad, norm2_grad = stage(
            end_up,
            1,
            [given(a) for a in (keep_u, got_u, up_own, gain_rows[:, 1:2])],
            [send_o],
            [made((own, ff), full), made((1, own), full)],
        )
        a_shape = (own, span_d)
        send_a, send_b, keep_a, keep_b = stage(
            heads_last,
            1,
            [given(a) for a in (keep_a, keep_b, got_a, got_b)],
            [up_grad],
            [made(a_shape, low)] * 2 + [made(a_shape, full)] * 2,
        )
        got_a, got_b = halver.swap(send_a, qkv_bits[0][4]), halver.swap(send_b, qkv_bits[1][4])
        (down_grad,) = stage(end_down, 1, [given(keep_d), given(got_d)], [send_a], [made((lanes, width), full)])
        norm2_grad = norm2_grad.reshape(own)
        flat = [heads * size, heads * size, heads * span, 2 * heads * experts, heads * span]
        query_grad, key_grad, value_grad, router_grad, outproj_grad, norm1_grad = call(
            functools.partial(assemble, d=d),
            1,
            [given(a) for a in (keep_a, got_a, keep_b, got_b, keep_o, got_o, wall_own, gain_rows[:, 0:1])] + then(down_grad),
            [made((own, cols), full) for cols in flat] + [made((1, own), full)],
            vmem=vmem_less,
            flops=cost.get("assemble", 1),
        )
        norm1_grad = norm1_grad.reshape(own)
        outproj_grad = outproj_grad.T
    else:
        act = act.reshape(tokens, blocks, -1)
        act = jnp.take(act, halver.order(down_bits) ^ halver.me, axis=1).reshape(tokens, -1)

        def down_product(lo, hi):
            quarter = ff // 4
            return dot_nn(grad_ffn_t, act[:, lo * quarter : hi * quarter])

        up_product = row_product(rows_by(normed, halver.order(up_bits)), pack)
        out_product = row_product(rows_by(grad_branch, halver.order(out_bits)), mixed)
        grad_att = lax.all_to_all(grad_out.reshape(cycle, share, lanes), "seq", 0, 0)
        back = attended_back(grad_att)
        returned = lax.all_to_all(back, "seq", 0, 0)
        deltas = head_deltas(returned, grad_out)
        input_grad = finished(deltas)
        down_grad = reduced(halver, down_product, down_bits, 1).T
        up_grad = reduced(halver, up_product, up_bits, 0)
        outproj_grad = reduced(halver, out_product, out_bits, 0)
        outproj_grad = outproj_grad.reshape(own, heads * experts, lanes)[:, :, :size].reshape(own, -1).T
        qkv_left = rows_by(ctx.reshape(seqs * rows, width), halver.order(qkv_bits[0]))
        qkv_product = row_product(qkv_left, jnp.concatenate(deltas, axis=1))
        by_head = reduced(halver, qkv_product, qkv_bits[0], 0).reshape(own, heads, 2 + experts, lanes)
        query_grad = by_head[:, :, 0, :size].reshape(own, -1)
        key_grad = by_head[:, :, 1, :size].reshape(own, -1)
        value_grad = by_head[:, :, 2:, :size].reshape(own, -1)
        router_grad = jnp.concatenate(
            [by_head[:, :, 0, size + i * experts : size + (i + 1) * experts].reshape(own, -1) for i in range(2)], axis=1
        )

        def own_rows(array):
            return lax.dynamic_slice_in_dim(array, halver.me * own, own, axis=0).astype(full)

        norm1_grad = (
            jnp.sum(own_rows(query_weight) * query_grad, axis=1)
            + jnp.sum(own_rows(key_weight) * key_grad, axis=1)
            + jnp.sum(own_rows(value_weight) * value_grad, axis=1)
            + jnp.sum(own_rows(router_weight) * router_grad, axis=1)
        ) / gain_rows[:, 0]
        norm2_grad = jnp.sum(own_rows(up_weight) * up_grad, axis=1) / gain_rows[:, 1]
    return (
        output, input_grad, norm1_grad, norm2_grad, query_grad, key_grad, value_grad, router_grad,
        outproj_grad, up_grad, down_grad,
    )


def solution(mesh):
    token = P("batch", "seq", None)
    routes = P("batch", "seq", None, None)
    spread = ("seq", "batch")
    return jax.shard_map(
        local,
        mesh=mesh,
        in_specs=(token, token, token, P("batch"), routes, routes, routes) + (P(),) * 9,
        out_specs=(
            token, token, P(spread), P(spread), P(spread, None), P(spread, None), P(spread, None), P(spread, None),
            P(None, spread), P(spread, None), P(spread, None),
        ),
        check_vma=False,
    )
```

```python
import collections
import functools

import jax
import jax.numpy as jnp
import numpy as np
from jax import lax
from jax.experimental import pallas as pl
from jax.experimental.pallas import tpu as pltpu
from jax.sharding import PartitionSpec as P

epsilon = 1e-05
neg_large = -1e30
slope_base = 0.5
log2_e = 1.4426950408889634
lanes = 128
low = jnp.bfloat16
full = jnp.float32
vmem_bytes = 56 << 20
vmem_less = 24 << 20
cost = {'heads_split': 4000000000, 'heads_third': 4000000000, 'heads_last': 4000000000, 'cross_down': 2000000000, 'end_down': 6000000000, 'end_up': 3000000000, 'assemble': 3000000000}
vmem_back = 56 << 20
vmem_finish = 56 << 20
vmem_big = 56 << 20
vmem_attend = 56 << 20
vmem_end = 56 << 20
vmem_delta = 56 << 20
vmem_plane = 56 << 20

names = ["seqs", "seg", "mem", "rows", "heads", "size"]
names += ["experts", "parts", "share", "cycle", "width", "group"]
Dims = collections.namedtuple("Dims", names)


def dot_nn(left, right):
    return lax.dot_general(left, right, (((1,), (0,)), ((), ())), preferred_element_type=full)


def dot_nt(left, right):
    return lax.dot_general(left, right, (((1,), (1,)), ((), ())), preferred_element_type=full)


def dot_tn(left, right):
    return lax.dot_general(left, right, (((0,), (0,)), ((), ())), preferred_element_type=full)


def norm_parts(values):
    centred = values - jnp.mean(values, axis=-1, keepdims=True)
    spread = jnp.mean(centred * centred, axis=-1, keepdims=True)
    inverse = lax.rsqrt(spread + epsilon)
    return centred * inverse, inverse


def norm_back(grad, hat, inverse, gain_row):
    scaled = grad * gain_row
    along = jnp.mean(scaled * hat, axis=-1, keepdims=True)
    return inverse * (scaled - jnp.mean(scaled, axis=-1, keepdims=True) - hat * along)


smem = pl.BlockSpec(memory_space=pltpu.SMEM)
whole = pl.BlockSpec(memory_space=pltpu.VMEM)
unread = pl.BlockSpec(memory_space=pl.ANY)


def by_step(shape, axis):
    return pl.BlockSpec(shape, lambda i: tuple(i if a == axis else 0 for a in range(len(shape))))


def at_all(shape):
    return pl.BlockSpec(shape, lambda *i: (0,) * len(shape))


def call(kernel, steps, operands, outs, scratch=(), vmem=vmem_bytes, flops=1):
    return pl.pallas_call(
        kernel,
        grid=(steps,),
        out_shape=[jax.ShapeDtypeStruct(shape, kind) for shape, kind, _ in outs],
        in_specs=[spec for _, spec in operands],
        out_specs=[spec for _, _, spec in outs],
        scratch_shapes=list(scratch),
        compiler_params=pltpu.CompilerParams(
            vmem_limit_bytes=vmem, dimension_semantics=("arbitrary",)
        ),
        cost_estimate=pl.CostEstimate(flops=flops, bytes_accessed=1, transcendentals=0),
    )(*[a for a, _ in operands])


def picks(routes, experts):
    slots, tokens = routes.shape
    wide = jnp.concatenate([routes.astype(full), jnp.zeros((8 - slots, tokens), full)], axis=0)
    columns = wide.T
    expert = lax.broadcasted_iota(jnp.int32, (tokens, experts), 1).astype(full)
    total = jnp.zeros((tokens, experts), full)
    for slot in range(slots):
        total = total + (columns[:, slot : slot + 1] == expert).astype(full)
    return total


def fill_wall(wall_ref, wq_ref, wk_ref, wv_ref, wr_ref, d):
    size, experts = d.size, d.experts
    blank = jnp.zeros((lanes - size, d.width), low)
    wall_ref[0:size] = wq_ref[...]
    router = wr_ref[...]
    count = router.shape[0] // 2
    for h in range(d.heads):

        @pl.when(pl.program_id(0) == h)
        def _():
            mine = [router[at + h * experts : at + (h + 1) * experts] for at in (0, count)]
            wall_ref[size:lanes] = jnp.concatenate(mine + [blank[2 * experts :]], axis=0)

    wall_ref[lanes : lanes + size] = wk_ref[...]
    wall_ref[lanes + size : 2 * lanes] = blank
    for e in range(experts):
        first = (2 + e) * lanes
        wall_ref[first : first + size] = wv_ref[e * size : (e + 1) * size]
        wall_ref[first + size : first + lanes] = blank


def prepare(scal_ref, ctx_ref, wq_ref, wk_ref, wv_ref, wr_ref, wo_ref, wall_ref, exp_ref, out_ref, own_ref, d=None):
    fill_wall(wall_ref.at[0], wq_ref, wk_ref, wv_ref, wr_ref, d)
    ctx = ctx_ref[...].reshape(-1, d.width)
    exp_ref[0] = dot_nt(ctx, wall_ref[0, 2 * lanes :]).astype(low)
    for e in range(d.experts):
        out_ref[0, e * lanes : e * lanes + d.size] = wo_ref[e * d.size : (e + 1) * d.size]
        out_ref[0, e * lanes + d.size : (e + 1) * lanes] = jnp.zeros((lanes - d.size, d.width), low)
    rows = own_ref.shape[1]
    if lanes % rows == 0:
        first = scal_ref[3] * rows
        column = pl.ds(pl.multiple_of(lax.div(first, lanes) * lanes, lanes), lanes)
        turned = wall_ref[0, :, column].T
        for at in range(0, lanes, rows):

            @pl.when(lax.rem(first, lanes) == at)
            def _():
                own_ref[0] = turned[at : at + rows]


def project(
    x_ref, m_ref, vr_ref, mr_ref, or_ref, gain_ref, wq_ref, wk_ref, wv_ref, wr_ref,
    pay_ref, ctx_ref, vgate_ref, ogate_ref, wall_ref, held_ref, d=None
):
    size, experts = d.size, d.experts
    spare = lanes - size

    @pl.when(pl.program_id(0) == 0)
    def _():
        for s in range(d.seqs):
            block = jnp.concatenate([m_ref[s], x_ref[s]], axis=0).astype(full)
            hat, _ = norm_parts(block)
            block_low = (hat * gain_ref[...]).astype(low)
            held_ref[s * d.rows : (s + 1) * d.rows] = block_low
            ctx_ref[s] = block_low

    fill_wall(wall_ref, wq_ref, wk_ref, wv_ref, wr_ref, d)
    ctx = held_ref[...]
    every = dot_nt(ctx, wall_ref[...])
    query = every[:, 0:lanes]
    sig = jax.nn.sigmoid(query[:, size : size + 2 * experts])
    pick = []
    out_pick = []
    out_sig = []
    for s in range(d.seqs):
        pick.append(picks(mr_ref[s, 0], experts))
        pick.append(picks(vr_ref[s, 0], experts))
        out_pick.append(picks(or_ref[s, 0], experts))
        out_sig.append(sig[s * d.rows + d.mem : (s + 1) * d.rows, experts:])
    gate = sig[:, :experts] * jnp.concatenate(pick, axis=0)
    vgate_ref[0] = gate
    ogate_ref[0] = jnp.concatenate(out_sig, axis=0) * jnp.concatenate(out_pick, axis=0)
    count = d.seqs * d.rows
    value = jnp.zeros((count, lanes), full)
    for e in range(experts):
        value = value + gate[:, e : e + 1] * every[:, (2 + e) * lanes : (3 + e) * lanes]
    lane_at = lax.broadcasted_iota(jnp.int32, (count, lanes), 1)
    query = jnp.where(lane_at < size, query, 0.0).astype(low)
    keys = every[:, lanes : 2 * lanes].astype(low)
    value = value.astype(low)
    for s in range(d.seqs):
        mine = slice(s * d.rows, (s + 1) * d.rows)
        for p in range(d.parts):
            first = s * d.rows + d.mem + p * d.share
            pay_ref[p, 0, s] = payload(keys[mine], value[mine], query[first : first + d.share], d)


def lane_sums(product, experts):
    slot = lax.broadcasted_iota(jnp.int32, (experts * lanes, lanes), 0) // lanes
    target = lax.broadcasted_iota(jnp.int32, (experts * lanes, lanes), 1)
    ones = (slot == target).astype(full).astype(low)
    high = product.astype(low)
    rest = (product - high.astype(full)).astype(low)
    return (dot_nn(high, ones) + dot_nn(rest, ones))[:, :experts]


def turn_context(scal_ref, ctx_ref, *refs, bits=None):
    first_ref, second_ref = refs[-2:]
    value = ctx_ref[...].reshape(-1, ctx_ref.shape[-1])
    turn(value, first_ref, scal_ref[3], bits[0])
    turn(value, second_ref, scal_ref[3], bits[1])


def folded_in(d):
    half = d.share // 2
    return 2 * d.rows == 6 * half and 7 * (lanes - d.size) == d.size


def payload_rows(d):
    return 2 * d.rows + (d.share // 2 if folded_in(d) else d.share)


def payload(keys, values, queries, d):
    size, half = d.size, d.share // 2
    if not folded_in(d):
        return jnp.concatenate([keys, values, queries], axis=0)
    rows = jnp.concatenate([keys, values, queries[:half]], axis=0)
    step = lanes - size
    spare = [queries[half:, at : at + step] for at in range(0, size, step)]
    return jnp.concatenate([rows[:, :size], jnp.concatenate(spare, axis=0)], axis=1)


def payload_queries(block, d):
    size, half = d.size, d.share // 2
    blank = jnp.zeros((d.share, lanes - size), block.dtype)
    if not folded_in(d):
        return jnp.concatenate([block[2 * d.rows :, :size], blank], axis=1)
    rest = jnp.concatenate([block[at * half : (at + 1) * half, size:] for at in range(7)], axis=1)
    return jnp.concatenate([jnp.concatenate([block[2 * d.rows :, :size], rest], axis=0), blank], axis=1)


def key_value(pay_ref, k_ref, v_ref, d):
    for j in range(d.cycle):
        k_ref[j * d.mem : (j + 1) * d.mem] = pay_ref[j, 0 : d.mem]
        v_ref[j * d.mem : (j + 1) * d.mem] = pay_ref[j, d.rows : d.rows + d.mem]
        base = d.cycle * d.mem + j * d.seg
        k_ref[base : base + d.seg] = pay_ref[j, d.mem : d.rows]
        v_ref[base : base + d.seg] = pay_ref[j, d.rows + d.mem : 2 * d.rows]


def query_block(pay_ref, first, d):
    found = [payload_queries(pay_ref[j], d) for j in range(first, first + d.group)]
    return jnp.concatenate(found, axis=0)


def attend(scal_ref, pay_ref, *refs, d=None):
    att_ref, keep_ref, lse_ref, k_ref, v_ref = refs[-5:]
    share, group = d.share, d.group
    mem_len = d.cycle * d.mem
    ctx_len = d.cycle * d.rows
    length, head, part = scal_ref[0], scal_ref[1], scal_ref[2]
    key_value(pay_ref, k_ref, v_ref, d)
    slope = slope_base * (head + 1).astype(full) / ctx_len * log2_e
    place = lax.broadcasted_iota(jnp.int32, (1, ctx_len), 1) - mem_len
    bias = jnp.where(place < length, place.astype(full) * slope, neg_large)
    q_rows = group * share
    for first in range(0, d.cycle, group):
        width = mem_len + (first + group) * d.seg
        cut = width - group * d.seg
        query = query_block(pay_ref, first, d)
        scores = dot_nt(query, k_ref[0:width]) * (d.size**-0.5 * log2_e) + bias[:, :width]
        row = lax.broadcasted_iota(jnp.int32, (q_rows, group * d.seg), 0)
        col = lax.broadcasted_iota(jnp.int32, (q_rows, group * d.seg), 1)
        row_place = (row // share) * d.seg + part * share + row % share
        tail = jnp.where(col <= row_place, scores[:, cut:], neg_large)
        scores = jnp.concatenate([scores[:, :cut], tail], axis=1)
        top = jnp.max(scores, axis=1, keepdims=True)
        weights = jnp.exp2(scores - top)
        total = jnp.sum(weights, axis=1, keepdims=True)
        attended = dot_nn(weights.astype(low), v_ref[0:width]) / total
        keep_ref[first * share : first * share + q_rows] = attended
        lse_ref[first * share : first * share + q_rows] = top + jnp.log2(total)
        for j in range(group):
            att_ref[first + j] = attended[j * share : (j + 1) * share].astype(low)


def attend_back(
    scal_ref, pay_ref, keep_ref, lse_ref, grad_ref, *refs, d=None
):
    out_ref, k_ref, v_ref, dk_ref, dv_ref = refs[-5:]
    share, group, size = d.share, d.group, d.size
    mem_len = d.cycle * d.mem
    ctx_len = d.cycle * d.rows
    length, head, part = scal_ref[0], scal_ref[1], scal_ref[2]
    key_value(pay_ref, k_ref, v_ref, d)
    scale = size**-0.5
    slope = slope_base * (head + 1).astype(full) / ctx_len * log2_e
    place = lax.broadcasted_iota(jnp.int32, (ctx_len, lanes), 0) - mem_len
    bias = jnp.where(place < length, place.astype(full) * slope, neg_large)[:, 0:1]
    dk_ref[...] = jnp.zeros_like(dk_ref)
    dv_ref[...] = jnp.zeros_like(dv_ref)
    q_rows = group * share
    lane_at = lax.broadcasted_iota(jnp.int32, (q_rows, lanes), 1)
    query_grads = []
    for first in range(0, d.cycle, group):
        width = mem_len + (first + group) * d.seg
        cut = width - group * d.seg
        begin = first * share
        query = query_block(pay_ref, first, d)
        raw = jnp.concatenate([grad_ref[j] for j in range(first, first + group)], axis=0)
        grad = jnp.where(lane_at < size, raw, jnp.zeros_like(raw))
        kept = keep_ref[begin : begin + q_rows]
        delta = jnp.sum(jnp.where(lane_at < size, grad.astype(full) * kept, 0.0), axis=1, keepdims=True)
        both = jnp.concatenate(
            [
                jnp.broadcast_to(delta, (q_rows, lanes)),
                jnp.broadcast_to(lse_ref[begin : begin + q_rows], (q_rows, lanes)),
            ],
            axis=1,
        ).T
        delta_row = both[0:1]
        lse_row = both[lanes : lanes + 1]
        scores = dot_nt(k_ref[0:width], query) * (scale * log2_e) + bias[:width]
        weights = jnp.exp2(scores - lse_row)
        row = lax.broadcasted_iota(jnp.int32, (group * d.seg, q_rows), 0)
        col = lax.broadcasted_iota(jnp.int32, (group * d.seg, q_rows), 1)
        col_place = (col // share) * d.seg + part * share + col % share
        weights = jnp.concatenate([weights[:cut], jnp.where(row <= col_place, weights[cut:], 0.0)], axis=0)
        grad_weights = dot_nt(v_ref[0:width], grad)
        grad_scores = (weights * (grad_weights - delta_row)).astype(low)
        dk_ref[0:width] += dot_nn(grad_scores, query)
        dv_ref[0:width] += dot_nn(weights.astype(low), grad)
        dq = (dot_tn(grad_scores, k_ref[0:width]) * scale).astype(low)
        query_grads.append(dq)
    for j in range(d.cycle):
        base = mem_len + j * d.seg
        dk = jnp.concatenate([dk_ref[j * d.mem : (j + 1) * d.mem], dk_ref[base : base + d.seg]], axis=0)
        dv = jnp.concatenate([dv_ref[j * d.mem : (j + 1) * d.mem], dv_ref[base : base + d.seg]], axis=0)
        dq = query_grads[j // group][j % group * share : (j % group + 1) * share]
        out_ref[j] = payload((dk * scale).astype(low), dv.astype(low), dq, d)


def place_of(mask, bits):
    place = jnp.int32(0)
    for at, bit in enumerate(bits):
        place = place + ((mask >> bit) & 1) * (1 << (len(bits) - 1 - at))
    return place


def turn(value, out_ref, me, bits):
    turned = value.T
    count = 1 << len(bits)
    own = turned.shape[0] // count
    for block in range(count):
        place = place_of(block ^ me, bits)
        side = lax.div(place, count // 2)
        inside = lax.rem(place, count // 2)
        out_ref[side, pl.ds(pl.multiple_of(inside * own, own), own), :] = turned[block * own : (block + 1) * own]


def beside(turn_ref, pack_ref):
    half, tokens = turn_ref.shape[1] // 2, turn_ref.shape[2]
    first = pack_ref.shape[1] - 2 * tokens
    pack_ref[:, first : first + tokens] = turn_ref[1, 0:half]
    pack_ref[:, first + tokens :] = turn_ref[1, half:]


def feed(
    scal_ref, att_ref, ogate_ref, x_ref, gain_ref, live_ref, gf_ref, wo_ref, up_ref, down_ref,
    mix_hbm, act_hbm, pack_hbm, out_ref, resid_ref, branch_ref, normed_ref, turned_ref, gatt_ref,
    sum_ref, ffn_ref, back_ref, held_ref, turn_ref, out_mix_ref, act_ref, pack_ref, copied, d=None, bits=None
):
    step = pl.program_id(0)
    together = wo_ref.shape[0]
    steps_h = d.heads // together
    last = pl.num_programs(0) - 1 - steps_h
    experts = d.experts
    me = scal_ref[3]

    @pl.when(step == 0)
    def _():
        for s in range(d.seqs):
            sum_ref[s * d.seg : (s + 1) * d.seg] = x_ref[s].astype(full)
        ffn_ref[...] = jnp.zeros_like(ffn_ref)
        back_ref[...] = jnp.zeros_like(back_ref)

    @pl.when(step < steps_h)
    def _():
        total = sum_ref[...]
        for k in range(together):
            found = [att_ref[p, k, s] for s in range(d.seqs) for p in range(d.parts)]
            att = jnp.concatenate(found, axis=0).astype(full)
            gate = ogate_ref[k]
            mixed = jnp.concatenate([(gate[:, e : e + 1] * att).astype(low) for e in range(experts)], axis=1)
            wide = mixed.shape[1]
            out_mix_ref[:, pl.ds(pl.multiple_of((step * together + k) * wide, lanes), wide)] = mixed
            total = total + dot_nn(mixed, wo_ref[k])
        sum_ref[...] = total

    @pl.when(step == steps_h - 1)
    def _():
        hat, _ = norm_parts(sum_ref[...])
        normed = (hat * gain_ref[...]).astype(low)
        held_ref[...] = normed
        if bits is None:
            normed_ref[...] = normed
        else:
            turn(normed, turn_ref, me, bits[1])
            normed_ref[...] = turn_ref[0]
            beside(turn_ref, pack_ref)

    @pl.when((step >= steps_h) & (step <= last))
    def _():
        coeff = 0.7978845608028654
        held = held_ref[...]
        outer_grad = gf_ref[...]
        acts = []
        grads = []
        part = up_ref.shape[1] // 4
        for c in range(4):
            mine = slice(c * part, (c + 1) * part)
            value = dot_nn(held, up_ref[:, mine])
            grad_act = dot_nt(outer_grad, down_ref[mine, :])
            square = value * value
            wave = jnp.tanh(value * (coeff + (0.044715 * coeff) * square))
            rise = 0.5 + 0.5 * wave
            acts.append((value * rise).astype(low))
            slope = rise + (0.5 * value) * (1.0 - wave * wave) * (coeff + (3 * 0.044715 * coeff) * square)
            grads.append((grad_act * slope).astype(low))
        act = jnp.concatenate(acts, axis=1)
        gu = jnp.concatenate(grads, axis=1)
        ffn_ref[...] += dot_nn(act, down_ref[...])
        back_ref[...] += dot_nt(gu, up_ref[...])
        block = step - steps_h
        span = act.shape[1]
        if bits is None:
            pack_ref[:, pl.ds(pl.multiple_of(block * span, span), span)] = gu
            act_ref[:, pl.ds(pl.multiple_of(block * span, span), span)] = act
        else:
            half = 1 << (len(bits[0]) - 1)
            own = act_ref.shape[1] // half
            pack_ref[:, pl.ds(pl.multiple_of(half * own + block * span, lanes), span)] = gu
            for b in range(span // own):
                piece = act[:, b * own : (b + 1) * own]
                place = place_of((block * (span // own) + b) ^ me, bits[0])
                inside = pl.ds(pl.multiple_of(lax.rem(place, half) * own, own), own)

                @pl.when(place < half)
                def _():
                    act_ref[:, inside] = piece

                @pl.when(place >= half)
                def _():
                    pack_ref[:, inside] = piece

    @pl.when(step == last)
    def _():
        residual = sum_ref[...]
        out_ref[...] = ((residual + ffn_ref[...]) * live_ref[...]).astype(low)
        hat, inverse = norm_parts(residual)
        grad = gf_ref[...].astype(full) + norm_back(back_ref[...], hat, inverse, gain_ref[...])
        resid_ref[...] = grad
        branch = grad.astype(low)
        branch_ref[...] = branch
        if bits is None:
            turned_ref[...] = branch
        else:
            turn(branch, turn_ref, me, bits[2])
            turned_ref[...] = turn_ref[0]
            beside(turn_ref, out_mix_ref)

    moves = [
        pltpu.make_async_copy(held, result, copied.at[at])
        for at, (held, result) in enumerate(((out_mix_ref, mix_hbm), (act_ref, act_hbm), (pack_ref, pack_hbm)))
    ]

    @pl.when(step == last)
    def _():
        for move in moves:
            move.start()

    @pl.when(step > last)
    def _():
        for k in range(together):
            unmix(branch_ref, att_ref, ogate_ref, wo_ref, gatt_ref, k, d)

    @pl.when(step == pl.num_programs(0) - 1)
    def _():
        for move in moves:
            move.wait()


def unmix(branch_ref, att_ref, ogate_ref, wo_ref, out_ref, k, d):
    size, experts = d.size, d.experts
    tokens = d.seqs * d.seg
    grad_mixed = dot_nt(branch_ref[...], wo_ref[k])
    found = [att_ref[p, k, s] for s in range(d.seqs) for p in range(d.parts)]
    att = jnp.concatenate(found, axis=0).astype(full)
    gate = ogate_ref[k]
    grad = jnp.zeros((tokens, lanes), full)
    product = []
    for e in range(experts):
        piece = grad_mixed[:, e * lanes : (e + 1) * lanes]
        grad = grad + gate[:, e : e + 1] * piece
        product.append(piece * att)
    logit = lane_sums(jnp.concatenate(product, axis=1), experts) * gate * (1.0 - gate)
    joined = jnp.concatenate(
        [grad[:, :size].astype(low), logit.astype(low), jnp.zeros((tokens, lanes - size - experts), low)], axis=1
    )
    for s in range(d.seqs):
        for p in range(d.parts):
            first = s * d.seg + p * d.share
            out_ref[p, k, s] = joined[first : first + d.share]


def make_deltas(back_ref, grad_ref, vgate_ref, exp_ref, *refs, d=None):
    size, experts = d.size, d.experts
    q_found, k_found, v_found, lo_found = [], [], [], []
    for s in range(d.seqs):
        kv = back_ref[0, 0, s, 0 : 2 * d.rows]
        if d.parts > 1:
            kv = kv.astype(full)
            for p in range(1, d.parts):
                kv = kv + back_ref[p, 0, s, 0 : 2 * d.rows].astype(full)
            kv = kv.astype(low)
        k_found.append(kv[: d.rows])
        v_found.append(kv[d.rows :])
        q_found.append(jnp.zeros((d.mem, lanes), low))
        lo_found.append(jnp.zeros((d.mem, lanes), low))
        for p in range(d.parts):
            q_found.append(payload_queries(back_ref[p, 0, s], d))
            lo_found.append(grad_ref[p, 0, s])
    query = jnp.concatenate(q_found, axis=0)
    keys = jnp.concatenate(k_found, axis=0)
    values = jnp.concatenate(v_found, axis=0)
    out_logit = jnp.concatenate(lo_found, axis=0)[:, size : size + experts]
    gate = vgate_ref[0]
    lane_at = lax.broadcasted_iota(jnp.int32, (d.seqs * d.rows, lanes), 1)
    value = jnp.where(lane_at < size, values.astype(full), 0.0)
    keys = jnp.where(lane_at < size, keys, jnp.zeros_like(keys))
    product = jnp.concatenate(
        [value * exp_ref[0, :, e * lanes : (e + 1) * lanes].astype(full) for e in range(experts)], axis=1
    )
    logit = (lane_sums(product, experts) * gate * (1.0 - gate)).astype(low)
    first = jnp.concatenate(
        [query[:, :size], logit, out_logit, jnp.zeros((d.seqs * d.rows, lanes - size - 2 * experts), low)], axis=1
    )
    step = pl.program_id(0)
    for at, delta_ref in enumerate(refs[-2:]):

        @pl.when(step // (d.heads // 2) == at)
        def _():
            delta_ref[:, 0:lanes] = first
            delta_ref[:, lanes : 2 * lanes] = keys
            for e in range(experts):
                delta_ref[:, (2 + e) * lanes : (3 + e) * lanes] = (gate[:, e : e + 1] * value).astype(low)


def finish(first_ref, second_ref, x_ref, gain_ref, resid_ref, wall_ref, *refs, d=None):
    out_ref, sum_ref = refs[-2:]
    step = pl.program_id(0)

    @pl.when(step == 0)
    def _():
        sum_ref[...] = jnp.zeros_like(sum_ref)

    for at, delta_ref in enumerate((first_ref, second_ref)):

        @pl.when(step // (d.heads // 2) == at)
        def _():
            rows = [delta_ref[s * d.rows + d.mem : (s + 1) * d.rows] for s in range(d.seqs)]
            sum_ref[...] += dot_nn(jnp.concatenate(rows, axis=0), wall_ref[0])

    @pl.when(step == pl.num_programs(0) - 1)
    def _():
        for s in range(d.seqs):
            hat, inverse = norm_parts(x_ref[s].astype(full))
            mine = slice(s * d.seg, (s + 1) * d.seg)
            out_ref[s] = resid_ref[mine] + norm_back(sum_ref[mine], hat, inverse, gain_ref[...])


def both(first, second, axis):
    return jnp.concatenate([first, second], axis=axis)


def send_down(gf_ref, act_ref, act_got_ref, *refs):
    refs[-1][...] = dot_nn(gf_ref[...], both(act_ref[...], act_got_ref[...], 0)).astype(low)


def send_up(left_ref, left_got_ref, gu_ref, gu_got_ref, *refs):
    left = both(left_ref[...], left_got_ref[...], 1)
    refs[-1][...] = dot_nn(left, both(gu_ref[...], gu_got_ref[...], 0)).astype(low)


def cross_down(gf_ref, act_ref, act_got_ref, new_ref, *refs):
    send_ref, keep_ref = refs[-2:]
    total = dot_nn(gf_ref[...], both(act_ref[...], act_got_ref[...], 0)) + new_ref[...].astype(full)
    half = total.shape[1] // 2
    keep_ref[...] = total[:, :half]
    send_ref[...] = total[:, half:].astype(low)


def cross_up(left_ref, left_got_ref, gu_ref, gu_got_ref, new_ref, *refs):
    send_ref, keep_ref = refs[-2:]
    left = both(left_ref[...], left_got_ref[...], 1)
    total = dot_nn(left, both(gu_ref[...], gu_got_ref[...], 0)) + new_ref[...].astype(full)
    half = total.shape[0] // 2
    keep_ref[...] = total[:half]
    send_ref[...] = total[half:].astype(low)


def fold_lanes(keep_ref, got_ref, *refs):
    send_ref, left_ref = refs[-2:]
    total = keep_ref[...] + got_ref[...].astype(full)
    half = total.shape[1] // 2
    left_ref[...] = total[:, :half]
    send_ref[...] = total[:, half:].astype(low)


def end_down(keep_ref, got_ref, *refs):
    refs[-1][...] = (keep_ref[...] + got_ref[...].astype(full)).T


def end_up(keep_u_ref, got_u_ref, weight_ref, gain_ref, *refs):
    up_ref, norm_ref = refs[-2:]
    total = keep_u_ref[...] + got_u_ref[...].astype(full)
    up_ref[...] = total
    along = jnp.sum(total * weight_ref[...].astype(full), axis=1, keepdims=True)
    norm_ref[...] = row_of(along / gain_ref[...])


def outer_send(left_ref, left_got_ref, right_ref, right_got_ref, *refs):
    left = both(left_ref[...], left_got_ref[...], 1)
    refs[-1][...] = dot_nn(left, both(right_ref[...], right_got_ref[...], 0)).astype(low)


def outer_split(left_ref, left_got_ref, right_ref, right_got_ref, new_ref, *refs):
    send_ref, keep_ref = refs[-2:]
    left = both(left_ref[...], left_got_ref[...], 1)
    total = dot_nn(left, both(right_ref[...], right_got_ref[...], 0)) + new_ref[...].astype(full)
    half = total.shape[0] // 2
    keep_ref[...] = total[:half]
    send_ref[...] = total[half:].astype(low)


def heads_send(a_ref, a_got_ref, b_ref, b_got_ref, da_ref, da_got_ref, db_ref, db_got_ref, *refs):
    a_out, b_out = refs[-2:]
    a_out[...] = dot_nn(both(a_ref[0], a_got_ref[...], 1), both(da_ref[...], da_got_ref[...], 0)).astype(low)
    b_out[...] = dot_nn(both(b_ref[0], b_got_ref[...], 1), both(db_ref[...], db_got_ref[...], 0)).astype(low)


def heads_split(
    a_ref, a_got_ref, b_ref, b_got_ref, da_ref, da_got_ref, db_ref, db_got_ref, new_a_ref, new_b_ref, *refs
):
    outs = refs[-4:]
    left = both(a_ref[0], a_got_ref[...], 1), both(b_ref[0], b_got_ref[...], 1)
    right = both(da_ref[...], da_got_ref[...], 0), both(db_ref[...], db_got_ref[...], 0)
    for at, new_ref in enumerate((new_a_ref, new_b_ref)):
        total = dot_nn(left[at], right[at]) + new_ref[...].astype(full)
        half = total.shape[0] // 2
        outs[2 + at][...] = total[:half]
        outs[at][...] = total[half:].astype(low)


def heads_third(keep_a_ref, keep_b_ref, got_a_ref, got_b_ref, *refs):
    outs = refs[-4:]
    for at, (keep_ref, got_ref) in enumerate(((keep_a_ref, got_a_ref), (keep_b_ref, got_b_ref))):
        half = keep_ref.shape[0] // 2
        outs[2 + at][...] = keep_ref[:half] + got_ref[:half].astype(full)
        outs[at][...] = (keep_ref[half:] + got_ref[half:].astype(full)).astype(low)


def heads_last(*refs):
    send_ref, left_ref = refs[-2:]
    half = send_ref.shape[0]
    first = 0
    for keep_ref, got_ref in (refs[0:2], refs[2:4], refs[4:6]):
        here = slice(first, first + keep_ref.shape[1])
        left_ref[:, here] = keep_ref[:half] + got_ref[:half].astype(full)
        send_ref[:, here] = (keep_ref[half:] + got_ref[half:].astype(full)).astype(low)
        first += keep_ref.shape[1]


def fold(keep_ref, got_ref, *refs):
    send_ref, left_ref = refs[-2:]
    half = keep_ref.shape[0] // 2
    left_ref[...] = keep_ref[:half] + got_ref[:half].astype(full)
    send_ref[...] = (keep_ref[half:] + got_ref[half:].astype(full)).astype(low)


def row_of(column):
    n = column.shape[0]
    same = lax.broadcasted_iota(jnp.int32, (n, n), 0) == lax.broadcasted_iota(jnp.int32, (n, n), 1)
    return jnp.sum(jnp.where(same, column, 0.0), axis=0, keepdims=True)


def assemble(keep_ref, got_ref, wall_ref, gain_ref, *refs, d=None):
    q_ref, k_ref, v_ref, r_ref, out_ref, norm_ref = refs[-6:]
    size, experts = d.size, d.experts
    slots = 2 + experts

    def total(kept, got, first):
        here = slice(first * lanes, (first + 1) * lanes)
        return kept[:, here] + got[:, here].astype(full)

    every = [[total(keep_ref, got_ref, h * slots + at) for at in range(slots)] for h in range(d.heads)]
    along = jnp.zeros(every[0][0].shape, full)
    for h in range(d.heads):
        for at in range(slots):
            along = along + every[h][at] * wall_ref[h, :, at * lanes : (at + 1) * lanes].astype(full)
    norm_ref[...] = row_of(jnp.sum(along, axis=1, keepdims=True) / gain_ref[...])
    q_ref[...] = jnp.concatenate([one[0][:, :size] for one in every], axis=1)
    k_ref[...] = jnp.concatenate([one[1][:, :size] for one in every], axis=1)
    v_ref[...] = jnp.concatenate([one[2 + e][:, :size] for one in every for e in range(experts)], axis=1)
    values = [one[0][:, size : size + experts] for one in every]
    outs = [one[0][:, size + experts : size + 2 * experts] for one in every]
    r_ref[...] = jnp.concatenate(values + outs, axis=1)
    out_ref[...] = jnp.concatenate(
        [total(keep_ref, got_ref, d.heads * slots + at)[:, :size] for at in range(d.heads * experts)], axis=1
    )


class Halver:
    def __init__(self):
        self.cycle = lax.axis_size("seq")
        self.width = lax.axis_size("batch")
        self.low_bits = self.width.bit_length() - 1
        self.high_bits = self.cycle.bit_length() - 1
        self.me = lax.axis_index("seq") * self.width + lax.axis_index("batch")

    def swap(self, value, bit):
        if bit < self.low_bits:
            axis, size, mask = "batch", self.width, 1 << bit
        else:
            axis, size, mask = "seq", self.cycle, 1 << (bit - self.low_bits)
        return lax.ppermute(value, axis, [(i, i ^ mask) for i in range(size)])

    def order(self, bits):
        count = len(bits)
        found = np.zeros(1 << count, np.int32)
        for place in range(1 << count):
            for at, bit in enumerate(bits):
                if place >> (count - 1 - at) & 1:
                    found[place] |= 1 << bit
        return found


def halve(value, axis):
    size = value.shape[axis] // 2
    return (
        lax.slice_in_dim(value, 0, size, axis=axis),
        lax.slice_in_dim(value, size, 2 * size, axis=axis),
    )


def reduced(halver, product, bits, axis):
    got = halver.swap(product(2, 4).astype(low), bits[0])
    got_keep, got_send = halve(got, axis)
    got = halver.swap((product(1, 2) + got_send.astype(full)).astype(low), bits[1])
    keep = product(0, 1) + got_keep.astype(full) + got.astype(full)
    for bit in bits[2:]:
        keep, send = halve(keep, axis)
        keep = keep + halver.swap(send.astype(low), bit).astype(full)
    return keep


def local(
    inputs, memory, cotangent, valid_len, value_routes, memory_routes, output_routes, norm1_gain, norm2_gain,
    query_weight, key_weight, value_weight, router_weight, output_weight, up_weight, down_weight
):
    seqs, seg, width = inputs.shape
    mem = memory.shape[1]
    rows = seg + mem
    heads = value_routes.shape[2]
    slots_count = value_routes.shape[3]
    qk_width = query_weight.shape[1]
    size = qk_width // heads
    experts = value_weight.shape[1] // qk_width
    span = experts * size
    ff = up_weight.shape[1]
    tokens = seqs * seg
    halver = Halver()
    cycle = halver.cycle
    parts = cycle // (seqs * heads)
    share = seg // parts
    d = Dims(seqs, seg, mem, rows, heads, size, experts, parts, share, cycle, width, 2)
    pay_rows = payload_rows(d)
    at = lax.axis_index("seq")
    my_seq = at % seqs
    my_head = at // seqs % heads
    my_part = at // (seqs * heads)
    my_length = lax.dynamic_index_in_dim(valid_len, my_seq, 0, keepdims=False)
    scal = jnp.stack([my_length, my_head, my_part, halver.me]).astype(jnp.int32)
    gain_one = norm1_gain.reshape(1, width)
    gain_two = norm2_gain.reshape(1, width)
    place = at * seg + jnp.arange(seg, dtype=jnp.int32)
    live = (place[None, :] < valid_len[:, None]).astype(full).reshape(tokens, 1)
    grad_ffn = (cotangent.reshape(tokens, width).astype(full) * live).astype(low)
    wq, wk, wv, wr = query_weight.T, key_weight.T, value_weight.T, router_weight.T
    v_routes = jnp.transpose(value_routes, (0, 2, 3, 1))
    m_routes = jnp.transpose(memory_routes, (0, 2, 3, 1))
    o_routes = jnp.transpose(output_routes, (0, 2, 3, 1))
    blocks = cycle * halver.width
    own = width // blocks
    wide = experts * lanes
    wall_rows = 2 * lanes + wide
    wall_shape = (heads, wall_rows, width)

    def routes_spec(count):
        return by_step((seqs, 1, slots_count, count), 1)

    def head_spec(*tail):
        return by_step((parts, 1, seqs) + tail, 1)

    def given(array):
        return (array, at_all(array.shape))

    def made(shape, kind):
        return (shape, kind, at_all(shape))

    pay, ctx, vgate, ogate = call(
        functools.partial(project, d=d),
        heads,
        [
            given(inputs),
            given(memory),
            (v_routes, routes_spec(seg)),
            (m_routes, routes_spec(mem)),
            (o_routes, routes_spec(seg)),
            given(gain_one),
            (wq, by_step((size, width), 0)),
            (wk, by_step((size, width), 0)),
            (wv, by_step((span, width), 0)),
            given(wr),
        ],
        [
            ((parts, heads, seqs, pay_rows, lanes), low, head_spec(pay_rows, lanes)),
            made((seqs, rows, width), low),
            ((heads, seqs * rows, experts), full, by_step((1, seqs * rows, experts), 0)),
            ((heads, tokens, experts), full, by_step((1, tokens, experts), 0)),
        ],
        scratch=[pltpu.VMEM(wall_shape[1:], low), pltpu.VMEM((seqs * rows, width), low)],
    )
    wall, expanded, wo, wall_own = call(
        functools.partial(prepare, d=d),
        heads,
        [
            (scal, smem),
            given(ctx),
            (wq, by_step((size, width), 0)),
            (wk, by_step((size, width), 0)),
            (wv, by_step((span, width), 0)),
            given(wr),
            (output_weight, by_step((span, width), 0)),
        ],
        [
            (wall_shape, low, by_step((1,) + wall_shape[1:], 0)),
            ((heads, seqs * rows, wide), low, by_step((1, seqs * rows, wide), 0)),
            ((heads, wide, width), low, by_step((1, wide, width), 0)),
            ((heads, own, wall_rows), low, by_step((1, own, wall_rows), 0)),
        ],
    )
    up_own = lax.dynamic_slice_in_dim(up_weight, halver.me * own, own, axis=0)
    bit_count = halver.low_bits + halver.high_bits
    low_b = list(range(halver.low_bits))
    high_b = list(range(halver.low_bits, bit_count))
    core, chip_y, chip_x, chip_z = low_b[:1], low_b[1:], high_b[:1], high_b[1:]
    down_bits = core + chip_x + chip_y + chip_z
    up_bits = core + chip_y + chip_z[:1] + chip_x + chip_z[1:]
    out_bits = core + chip_z[:1] + chip_x + chip_y + chip_z[1:]
    fast = own == 32 and ff == blocks * lanes and len(chip_z) == 2 and len(chip_y) == 1

    qkv_bits = down_bits, core + chip_y + chip_z[:1] + chip_x + chip_z[1:]
    grad_ffn_t = grad_ffn.T
    after = [wo]
    if fast:
        turned_ctx = (2, width // 2, seqs * rows)
        ctx_a, ctx_b = call(
            functools.partial(turn_context, bits=qkv_bits),
            1,
            [(scal, smem), given(ctx), (wo, unread)],
            [made(turned_ctx, low), made(turned_ctx, low)],
        )
        grad_ffn_both = jnp.concatenate([grad_ffn_t, halver.swap(grad_ffn_t, core[0])], axis=1)
        ctx_a_got, ctx_b_got = halver.swap(ctx_a[1], core[0]), halver.swap(ctx_b[1], core[0])
        after += [grad_ffn_both, ctx_a_got, ctx_b_got]
    pay = lax.all_to_all(pay.reshape(cycle, pay_rows, lanes), "seq", 0, 0)
    att, kept, lse = call(
        functools.partial(attend, d=d),
        1,
        [(scal, smem), given(pay)] + [(a, unread) for a in after],
        [
            made((cycle, share, lanes), low),
            made((cycle * share, lanes), full),
            made((cycle * share, 1), full),
        ],
        scratch=[pltpu.VMEM((cycle * rows, lanes), low)] * 2,
        vmem=vmem_attend,
    )
    att = lax.all_to_all(att, "seq", 0, 0)
    steps, together = 4, 2
    steps_h = heads // together
    att_heads = att.reshape(parts, heads, seqs, share, lanes)

    def ff_block(i):
        return jnp.clip(i - steps_h, 0, steps - 1)

    def head_of(i):
        return jnp.where(i < steps_h + steps, jnp.minimum(i, steps_h - 1), i - steps_h - steps)

    def back_of(i):
        return jnp.maximum(i - steps_h - steps, 0)

    turned_shape = (width // 2, tokens) if fast else (tokens, width)
    act_shape = (tokens, ff // 2) if fast else (tokens, ff)
    pack_shape = (tokens, ff // 2 + ff + 2 * tokens) if fast else (tokens, ff)
    mix_shape = (tokens, heads * wide + 2 * tokens) if fast else (tokens, heads * wide)
    mixed, act, pack, output, grad_residual, grad_branch, normed, turned, grad_out = call(
        functools.partial(feed, d=d, bits=(tuple(down_bits), tuple(up_bits), tuple(out_bits)) if fast else None),
        2 * steps_h + steps,
        [
            (scal, smem),
            (att_heads, pl.BlockSpec((parts, together, seqs, share, lanes), lambda i: (0, head_of(i), 0, 0, 0))),
            (ogate, pl.BlockSpec((together, tokens, experts), lambda i: (head_of(i), 0, 0))),
            given(inputs),
            given(gain_two),
            given(live),
            given(grad_ffn),
            (wo, pl.BlockSpec((together, wide, width), lambda i: (head_of(i), 0, 0))),
            (up_weight, pl.BlockSpec((width, ff // steps), lambda i: (0, ff_block(i)))),
            (down_weight, pl.BlockSpec((ff // steps, width), lambda i: (ff_block(i), 0))),
        ],
        [
            (mix_shape, low, unread),
            (act_shape, low, unread),
            (pack_shape, low, unread),
            made((tokens, width), low),
            made((tokens, width), full),
            made((tokens, width), low),
            made(turned_shape, low),
            made(turned_shape, low),
            (
                (parts, heads, seqs, share, lanes),
                low,
                pl.BlockSpec((parts, together, seqs, share, lanes), lambda i: (0, back_of(i), 0, 0, 0)),
            ),
        ],
        scratch=[pltpu.VMEM((tokens, width), full)] * 3
        + [pltpu.VMEM((tokens, width), low), pltpu.VMEM((2, width // 2, tokens), low)]
        + [pltpu.VMEM(shape, low) for shape in (mix_shape, act_shape, pack_shape)]
        + [pltpu.SemaphoreType.DMA((3,))],
    )
    output = output.reshape(seqs, seg, width)

    pay_shape = (cycle, pay_rows, lanes)

    def attended_back(grad_att, *after):
        (back,) = call(
            functools.partial(attend_back, d=d),
            1,
            [(scal, smem), given(pay), given(kept), given(lse), given(grad_att)]
            + [(a, unread) for a in after],
            [made(pay_shape, low)],
            scratch=[pltpu.VMEM((cycle * rows, lanes), low)] * 2 + [pltpu.VMEM((cycle * rows, lanes), full)] * 2,
            vmem=vmem_back,
        )
        return back

    delta_shape = (seqs * rows, heads // 2 * wall_rows)
    first_half = pl.BlockSpec((seqs * rows, wall_rows), lambda i: (0, jnp.minimum(i, heads // 2 - 1)))
    second_half = pl.BlockSpec((seqs * rows, wall_rows), lambda i: (0, jnp.maximum(i - heads // 2, 0)))

    def head_deltas(returned, grad_out, *after):
        return call(
            functools.partial(make_deltas, d=d),
            heads,
            [
                (returned.reshape(parts, heads, seqs, pay_rows, lanes), head_spec(pay_rows, lanes)),
                (grad_out, head_spec(share, lanes)),
                (vgate, by_step((1, seqs * rows, experts), 0)),
                (expanded, by_step((1, seqs * rows, wide), 0)),
            ]
            + [(a, unread) for a in after],
            [(delta_shape, low, first_half), (delta_shape, low, second_half)],
            vmem=vmem_delta,
            flops=cost.get("deltas", 1),
        )

    def finished(deltas, *after):
        (input_grad,) = call(
            functools.partial(finish, d=d),
            heads,
            [
                (deltas[0], first_half),
                (deltas[1], second_half),
                given(inputs),
                given(gain_one),
                given(grad_residual),
                (wall, by_step((1, wall_rows, width), 0)),
            ]
            + [(a, unread) for a in after],
            [made((seqs, seg, width), full)],
            scratch=[pltpu.VMEM((tokens, width), full)],
            vmem=vmem_finish,
        )
        return input_grad

    def rows_by(array, order):
        cols = array.T.reshape(blocks, -1, array.shape[0])
        return jnp.take(cols, order ^ halver.me, axis=0).reshape(-1, array.shape[0])

    def row_product(left, right):
        quarter = left.shape[0] // 4
        return lambda lo, hi: dot_nn(left[lo * quarter : hi * quarter], right)

    gain_rows = lax.dynamic_slice_in_dim(jnp.stack([norm1_gain, norm2_gain], axis=1), halver.me * own, own, axis=0)
    if fast:
        split = 2
        pack_got = halver.swap(pack, core[0])
        mixed_got = halver.swap(mixed, core[0])
        assert width // 4 == tokens

        def down_products(piece):
            return [
                (grad_ffn_both, by_step((width // split, 2 * tokens), 0)),
                (act, pl.BlockSpec((tokens, ff // 4), lambda i: (0, piece))),
                (pack_got, pl.BlockSpec((tokens, ff // 4), lambda i: (0, piece))),
            ]

        def up_products(piece):
            step_u = ff // split
            first_u, first_n = ff // 2 // step_u, (ff // 2 + ff) // tokens
            right = pl.BlockSpec((tokens, step_u), lambda i: (0, first_u + i))
            return [
                (normed, pl.BlockSpec((tokens, tokens), lambda i: (piece, 0))),
                (pack_got, pl.BlockSpec((tokens, tokens), lambda i: (0, first_n + piece))),
                (pack, right),
                (pack_got, right),
            ]

        def d_made(cols, kind):
            return ((width, cols), kind, by_step((width // split, cols), 0))

        def u_made(rows_u, kind):
            return ((rows_u, ff), kind, by_step((rows_u, ff // split), 1))

        def out_products(piece):
            first_t = heads * wide // tokens
            right = by_step((tokens, heads * wide // split), 1)
            return [
                (turned, pl.BlockSpec((tokens, tokens), lambda i: (piece, 0))),
                (mixed_got, pl.BlockSpec((tokens, tokens), lambda i: (0, first_t + piece))),
                (mixed, right),
                (mixed_got, right),
            ]

        def out_made(rows_o, kind):
            return ((rows_o, heads * wide), kind, by_step((rows_o, heads * wide // split), 1))

        span_d = heads // 2 * wall_rows

        def head_products(piece):
            half = width // 4
            turned_spec = pl.BlockSpec((1, half, seqs * rows), lambda i: (0, piece, 0))
            got_spec = pl.BlockSpec((half, seqs * rows), lambda i: (piece, 0))
            right = by_step((seqs * rows, wall_rows), 1)
            return [
                (ctx_a, turned_spec), (ctx_a_got, got_spec), (ctx_b, turned_spec), (ctx_b_got, got_spec),
                (deltas[0], right), (deltas_a, right), (deltas[1], right), (deltas_b, right),
            ]

        def head_made(count, kind):
            return ((count, span_d), kind, by_step((count, wall_rows), 1))

        def then(*after):
            return [(a, unread) for a in after]

        def stage(kernel, steps, operands, after, outs, vmem=vmem_less):
            name = kernel.__name__
            return call(kernel, steps, operands + then(*after), outs, vmem=vmem, flops=cost.get(name, 1))

        def step_fold(kernel, keep, got, axis, *after):
            shape = tuple(n // 2 if a == axis else n for a, n in enumerate(keep.shape))
            return stage(kernel, 1, [given(keep), given(got)], after, [made(shape, low), made(shape, full)])

        grad_att = lax.all_to_all(grad_out.reshape(cycle, share, lanes), "seq", 0, 0)
        (send_u,) = stage(send_up, split, up_products(1), [grad_out], [u_made(width // 4, low)], vmem_plane)
        got_u = halver.swap(send_u, up_bits[1])
        back = attended_back(grad_att, send_u)
        returned = lax.all_to_all(back, "seq", 0, 0)
        (send_d,) = stage(send_down, split, down_products(1), [back], [d_made(ff // 4, low)], vmem_plane)
        got_d = halver.swap(send_d, down_bits[1])
        (send_o,) = stage(outer_send, split, out_products(1), [send_d], [out_made(width // 4, low)], vmem_plane)
        got_o = halver.swap(send_o, out_bits[1])
        deltas = head_deltas(returned, grad_out, send_o)
        deltas_a, deltas_b = halver.swap(deltas[0], core[0]), halver.swap(deltas[1], core[0])
        send_a, send_b = stage(
            heads_send, heads // 2, head_products(1), [deltas[0]], [head_made(width // 4, low)] * 2,
            vmem_big,
        )
        got_a, got_b = halver.swap(send_a, qkv_bits[0][1]), halver.swap(send_b, qkv_bits[1][1])
        send_u, keep_u = stage(
            cross_up,
            split,
            up_products(0) + [(got_u, by_step((width // 4, ff // split), 1))],
            [send_a],
            [u_made(width // 8, low), u_made(width // 8, full)],
            vmem_big,
        )
        got_u = halver.swap(send_u, up_bits[2])
        send_d, keep_d = stage(
            cross_down,
            split,
            down_products(0) + [(got_d, by_step((width // split, ff // 4), 0))],
            [send_u],
            [d_made(ff // 8, low), d_made(ff // 8, full)],
            vmem_big,
        )
        got_d = halver.swap(send_d, down_bits[2])
        send_o, keep_o = stage(
            outer_split,
            split,
            out_products(0) + [(got_o, by_step((width // 4, heads * wide // split), 1))],
            [send_d],
            [out_made(width // 8, low), out_made(width // 8, full)],
            vmem_big,
        )
        got_o = halver.swap(send_o, out_bits[2])
        input_grad = finished(deltas, send_o)
        send_a, send_b, keep_a, keep_b = stage(
            heads_split,
            heads // 2,
            head_products(0)
            + [(got_a, by_step((width // 4, wall_rows), 1)), (got_b, by_step((width // 4, wall_rows), 1))],
            [input_grad],
            [head_made(width // 8, low)] * 2 + [head_made(width // 8, full)] * 2,
            vmem_big,
        )
        got_a, got_b = halver.swap(send_a, qkv_bits[0][2]), halver.swap(send_b, qkv_bits[1][2])
        send_u, keep_u = step_fold(fold, keep_u, got_u, 0, send_a)
        got_u = halver.swap(send_u, up_bits[3])
        send_d, keep_d = step_fold(fold_lanes, keep_d, got_d, 1, send_u)
        got_d = halver.swap(send_d, down_bits[3])
        send_o, keep_o = step_fold(fold, keep_o, got_o, 0, send_d)
        got_o = halver.swap(send_o, out_bits[3])
        send_u, keep_u = step_fold(fold, keep_u, got_u, 0, send_o)
        got_u = halver.swap(send_u, up_bits[4])
        a_shape = (width // 16, span_d)
        send_a, send_b, keep_a, keep_b = stage(
            heads_third,
            1,
            [given(a) for a in (keep_a, keep_b, got_a, got_b)],
            [send_u],
            [made(a_shape, low)] * 2 + [made(a_shape, full)] * 2,
        )
        got_a, got_b = halver.swap(send_a, qkv_bits[0][3]), halver.swap(send_b, qkv_bits[1][3])
        send_d, keep_d = step_fold(fold_lanes, keep_d, got_d, 1, send_a)
        got_d = halver.swap(send_d, down_bits[4])
        up_grad, norm2_grad = stage(
            end_up,
            1,
            [given(a) for a in (keep_u, got_u, up_own, gain_rows[:, 1:2])],
            [send_d],
            [made((own, ff), full), made((1, own), full)],
            vmem_big,
        )
        h_shape = (own, 2 * span_d + heads * wide)
        send_h, keep_h = stage(
            heads_last,
            1,
            [given(a) for a in (keep_a, got_a, keep_b, got_b, keep_o, got_o)],
            [up_grad],
            [made(h_shape, low), made(h_shape, full)],
        )
        got_h = halver.swap(send_h, chip_z[1])
        (down_grad,) = stage(end_down, 1, [given(keep_d), given(got_d)], [send_h], [made((lanes, width), full)], vmem_big)
        norm2_grad = norm2_grad.reshape(own)
        flat = [heads * size, heads * size, heads * span, 2 * heads * experts, heads * span]
        query_grad, key_grad, value_grad, router_grad, outproj_grad, norm1_grad = call(
            functools.partial(assemble, d=d),
            1,
            [given(a) for a in (keep_h, got_h, wall_own, gain_rows[:, 0:1])] + then(down_grad),
            [made((own, cols), full) for cols in flat] + [made((1, own), full)],
            vmem=vmem_less,
            flops=cost.get("assemble", 1),
        )
        norm1_grad = norm1_grad.reshape(own)
        outproj_grad = outproj_grad.T
    else:
        act = act.reshape(tokens, blocks, -1)
        act = jnp.take(act, halver.order(down_bits) ^ halver.me, axis=1).reshape(tokens, -1)

        def down_product(lo, hi):
            quarter = ff // 4
            return dot_nn(grad_ffn_t, act[:, lo * quarter : hi * quarter])

        up_product = row_product(rows_by(normed, halver.order(up_bits)), pack)
        out_product = row_product(rows_by(grad_branch, halver.order(out_bits)), mixed)
        grad_att = lax.all_to_all(grad_out.reshape(cycle, share, lanes), "seq", 0, 0)
        back = attended_back(grad_att)
        returned = lax.all_to_all(back, "seq", 0, 0)
        deltas = head_deltas(returned, grad_out)
        input_grad = finished(deltas)
        down_grad = reduced(halver, down_product, down_bits, 1).T
        up_grad = reduced(halver, up_product, up_bits, 0)
        outproj_grad = reduced(halver, out_product, out_bits, 0)
        outproj_grad = outproj_grad.reshape(own, heads * experts, lanes)[:, :, :size].reshape(own, -1).T
        qkv_left = rows_by(ctx.reshape(seqs * rows, width), halver.order(qkv_bits[0]))
        qkv_product = row_product(qkv_left, jnp.concatenate(deltas, axis=1))
        by_head = reduced(halver, qkv_product, qkv_bits[0], 0).reshape(own, heads, 2 + experts, lanes)
        query_grad = by_head[:, :, 0, :size].reshape(own, -1)
        key_grad = by_head[:, :, 1, :size].reshape(own, -1)
        value_grad = by_head[:, :, 2:, :size].reshape(own, -1)
        router_grad = jnp.concatenate(
            [by_head[:, :, 0, size + i * experts : size + (i + 1) * experts].reshape(own, -1) for i in range(2)], axis=1
        )

        def own_rows(array):
            return lax.dynamic_slice_in_dim(array, halver.me * own, own, axis=0).astype(full)

        norm1_grad = (
            jnp.sum(own_rows(query_weight) * query_grad, axis=1)
            + jnp.sum(own_rows(key_weight) * key_grad, axis=1)
            + jnp.sum(own_rows(value_weight) * value_grad, axis=1)
            + jnp.sum(own_rows(router_weight) * router_grad, axis=1)
        ) / gain_rows[:, 0]
        norm2_grad = jnp.sum(own_rows(up_weight) * up_grad, axis=1) / gain_rows[:, 1]
    return (
        output, input_grad, norm1_grad, norm2_grad, query_grad, key_grad, value_grad, router_grad,
        outproj_grad, up_grad, down_grad,
    )


def solution(mesh):
    token = P("batch", "seq", None)
    routes = P("batch", "seq", None, None)
    spread = ("seq", "batch")
    return jax.shard_map(
        local,
        mesh=mesh,
        in_specs=(token, token, token, P("batch"), routes, routes, routes) + (P(),) * 9,
        out_specs=(
            token, token, P(spread), P(spread), P(spread, None), P(spread, None), P(spread, None), P(spread, None),
            P(None, spread), P(spread, None), P(spread, None),
        ),
        check_vma=False,
    )
```
